256 devices in a mesh: row: 32 (over z_hi, x, y), col: 8 (over z_lo, core).
Axes of the slice: x: 4, y: 4, z: 8 (z_hi: 2, z_lo: 4; z = z_hi * 4 + z_lo), core: 2. Of those that a mesh axis runs over, the one named last changes fastest.
Arguments:
- images: bfloat16 [16384, 1152], P(('row', 'col')), may hold values from -200 to 200
- texts: bfloat16 [16384, 1152], P(('row', 'col')), may hold values from -200 to 200, as said below
- log_temp: float32 [1], replicated, may hold values from 2.5 to 3.4
- bias: float32 [1], replicated, may hold values from -8 to -4
Outputs:
- grad_images: float32 [16384, 1152], P(('row', 'col'))
- grad_texts: float32 [16384, 1152], P(('row', 'col'))
The draws below stay inside these ranges and needn't reach their ends.
Inputs may be any that keep to these rules, and one draw needn't show every extreme that they name: `texts`: raw text embeddings, each row paired with the image row of the same index.
All inputs are finite; a program needn't handle non-finite values.
Results may differ from the reference program's by a relative error of at most 0.025.
Values may be sent and summed in bfloat16 or wider, within the bound.
No kernel may reach another device: no remote copies, remote signals or barrier semaphores. Data moves between devices by JAX's collectives and lax.ppermute only.
A program may use at most 64 MiB of HBM per device.

```python
import math
import jax
import jax.numpy as jnp
from jax import lax

D = 1152
IMG_DEV = 64
B = 16384
N_COL = 8


def shared_parts(key):
    first, second = jax.random.split(key, 2)
    col_scale = jnp.exp(jax.random.uniform(first, (1, D), jnp.float32, 0.0, math.log(30.0)))
    base = jnp.clip(jax.random.normal(second, (B, D), jnp.float32), -4.0, 4.0)
    return (col_scale, base)


def own_rows(key):
    first, second = jax.random.split(key, 2)
    row_scale = jnp.exp(jax.random.uniform(first, (B, 1), jnp.float32, math.log(0.1), 0.0))
    fresh = jnp.clip(jax.random.normal(second, (B, D), jnp.float32), -4.0, 4.0)
    return (row_scale, fresh)


def draw_images(key, part):
    col_scale, common = shared_parts(key)
    key = jax.random.fold_in(key, 11)
    row_scale, fresh = own_rows(key)
    return (common * row_scale * col_scale).astype(jnp.bfloat16)


def draw_texts(key, part):
    col_scale, common = shared_parts(key)
    key = jax.random.fold_in(key, 23)
    row_scale, fresh = own_rows(key)
    mixed = 0.75 * common + 0.66 * fresh
    return (mixed * row_scale * col_scale).astype(jnp.bfloat16)


def setup_inputs(seed: int = 0) -> dict:
    key_list = jax.random.split(jax.random.key(seed), 5)
    return {
        "images": draw_images(jax.random.fold_in(key_list[4], 71), 0),
        "texts": draw_texts(jax.random.fold_in(key_list[4], 71), 0),
        "log_temp": jnp.clip(jax.random.uniform(key_list[2], (1,), jnp.float32, 2.5, 3.4), 2.5, 3.4),
        "bias": jnp.clip(jax.random.uniform(key_list[3], (1,), jnp.float32, -8.0, -4.0), -8.0, -4.0),
    }


def normalize(raw):
    values = raw.astype(jnp.float32)
    inverse = lax.rsqrt(lax.optimization_barrier(jnp.sum(values * values, axis=1, keepdims=True)) + 1e-06)
    return (values * inverse, inverse)

def back_norm(unit, inverse, grad_unit):
    along = lax.optimization_barrier(jnp.sum(unit * grad_unit, axis=1, keepdims=True))
    return (grad_unit - unit * along) * inverse

def reference(images, texts, log_temp, bias):
    img_unit, inv_img = normalize(images)
    txt_unit, inv_txt = normalize(texts)
    img_round = img_unit.astype(jnp.bfloat16)
    txt_round = txt_unit.astype(jnp.bfloat16)
    temp = jnp.exp(log_temp[0])
    shift = bias[0]
    block_rows = IMG_DEV * N_COL
    blocks = B // block_rows

    def one_block(grad_txt, index):
        start = (index * block_rows).astype(jnp.int32)
        rows_here = lax.dynamic_slice_in_dim(img_round, start, block_rows, 0)
        dots = lax.dot_general(rows_here, txt_round, (((1,), (1,)), ((), ())), preferred_element_type=jnp.float32)
        logits = temp * dots + shift
        image_ids = start + lax.broadcasted_iota(jnp.int32, (block_rows, 1), 0)
        text_ids = lax.broadcasted_iota(jnp.int32, (1, B), 1)
        label = jnp.where(image_ids == text_ids, 1.0, -1.0).astype(jnp.float32)
        weights = (-temp * label * jax.nn.sigmoid(-label * logits)).astype(jnp.bfloat16)
        grad_rows = jnp.dot(weights, txt_round, preferred_element_type=jnp.float32)
        grad_txt = grad_txt + lax.dot_general(weights, rows_here, (((0,), (0,)), ((), ())), preferred_element_type=jnp.float32)
        return (grad_txt, grad_rows)
    grad_txt_unit, grad_parts = lax.scan(one_block, jnp.zeros((B, D), jnp.float32), jnp.arange(blocks, dtype=jnp.int32))
    grad_img_unit = grad_parts.reshape(B, D)
    return (back_norm(img_unit, inv_img, grad_img_unit), back_norm(txt_unit, inv_txt, grad_txt_unit))
```

```python
import jax
import jax.numpy as jnp
from jax import lax
from jax.experimental import pallas as pl
from jax.experimental.pallas import tpu as pltpu
from jax.sharding import PartitionSpec as P

AXES = ("row", "col")
F32 = jnp.float32
BF16 = jnp.bfloat16
LOG2E = 1.4426950408889634
SIZE_X, SIZE_Y, SIZE_Z, CORES = 4, 4, 8, 2


def device(x, y, z, c):
    return ((z // 4) * 16 + x * 4 + y) * 8 + (z % 4) * 2 + c


def shift(values, move):
    pairs = []
    for x in range(SIZE_X):
        for y in range(SIZE_Y):
            for z in range(SIZE_Z):
                for c in range(CORES):
                    nx, ny, nz, nc = move(x, y, z, c)
                    pairs.append((device(x, y, z, c), device(nx % SIZE_X, ny % SIZE_Y, nz % SIZE_Z, nc)))
    return lax.ppermute(values, AXES, pairs)


def first(k):
    return lambda x, y, z, c: (x + k, y, z, c) if c == 0 else (x, y + k, z, c)


def second(k):
    return lambda x, y, z, c: (x, y + k, z, c) if c == 0 else (x + k, y, z, c)


def line(k):
    return lambda x, y, z, c: (x, y, z + k, c) if c == 0 else (x, y, z - k, c)


def other(x, y, z, c):
    return (x, y, z, 1 - c)


def cat(parts):
    return jnp.concatenate(parts, axis=0)


def normalize(raw):
    values = raw.astype(F32)
    inverse = lax.rsqrt(jnp.sum(values * values, axis=1, keepdims=True) + 1e-06)
    return (values * inverse, inverse)


def back_norm(unit, inverse, grad_unit):
    along = jnp.sum(unit * grad_unit, axis=1, keepdims=True)
    return (grad_unit - unit * along) * inverse


def load(parts, whole, sems, base):
    copies, at = [], 0
    for n, part in enumerate(parts):
        rows = part.shape[0]
        copies.append(pltpu.make_async_copy(part, whole.at[pl.ds(at, rows)], sems.at[base + n]))
        at += rows
    for copy in copies:
        copy.start()
    return copies


def weights_kernel(n_img, n_txt, own, scal_ref, *refs):
    img_parts, txt_parts = refs[:n_img], refs[n_img:n_img + n_txt]
    w_ref, keep_ref, send_ref, img, txt, sems = refs[n_img + n_txt:]
    img_copies = load(img_parts, img, sems, 0)
    txt_copies = load(txt_parts, txt, sems, n_img)
    temp, shift_ = scal_ref[0], scal_ref[1]
    slope, offset = -temp * LOG2E, -shift_ * LOG2E
    for copy in txt_copies:
        copy.wait()
    at = 0
    for part, copy in zip(img_parts, img_copies):
        copy.wait()
        rows = part.shape[0]
        dots = lax.dot_general(
            img[at:at + rows, :], txt[...], (((1,), (1,)), ((), ())), preferred_element_type=F32
        )
        power = dots * slope + offset
        w_ref[at:at + rows, :] = (temp / (1.0 + jnp.exp2(power))).astype(BF16)
        if at == 0:
            corner = power[:own, :2 * own]
            row = lax.broadcasted_iota(jnp.int32, corner.shape, 0)
            column = lax.broadcasted_iota(jnp.int32, corner.shape, 1)
            positive = row == column
            signed = jnp.where(positive, -corner, corner)
            scale = jnp.where(positive, -temp, temp)
            w_ref[:own, :2 * own] = (scale / (1.0 + jnp.exp2(signed))).astype(BF16)
        at += rows
    half = txt.shape[0] // 2
    step = 256
    for out, start in ((send_ref, half), (keep_ref, 0)):
        for t in range(0, half, step):
            grad = lax.dot_general(
                w_ref[:, start + t:start + t + step], img[...], (((0,), (0,)), ((), ())), preferred_element_type=F32
            )
            out[t:t + step, :] = grad.astype(out.dtype)


def image_kernel(n_txt, w_ref, *refs):
    txt_parts, outs = refs[:n_txt], refs[n_txt:-2]
    txt, sems = refs[-2:]
    copies = load(txt_parts, txt, sems, 0)
    for copy in copies:
        copy.wait()
    at = 0
    for out in outs:
        rows = out.shape[0]
        grad = jnp.dot(w_ref[at:at + rows, :], txt[...], preferred_element_type=F32)
        out[...] = grad.astype(out.dtype)
        at += rows


def block(img_parts, txt_parts, scalars, own):
    n_img, n_txt = len(img_parts), len(txt_parts)
    rows = sum(p.shape[0] for p in img_parts)
    cols = sum(p.shape[0] for p in txt_parts)
    dim = img_parts[0].shape[1]
    anywhere = pl.BlockSpec(memory_space=pl.ANY)
    vmem = pl.BlockSpec(memory_space=pltpu.VMEM)
    flops = 2 * rows * cols * dim
    w, keep, send = pl.pallas_call(
        lambda *refs: weights_kernel(n_img, n_txt, own, *refs),
        out_shape=(
            jax.ShapeDtypeStruct((rows, cols), BF16),
            jax.ShapeDtypeStruct((cols // 2, dim), BF16),
            jax.ShapeDtypeStruct((cols // 2, dim), BF16),
        ),
        in_specs=[pl.BlockSpec(memory_space=pltpu.SMEM)] + [anywhere] * (n_img + n_txt),
        out_specs=(vmem, vmem, vmem),
        scratch_shapes=[
            pltpu.VMEM((rows, dim), BF16),
            pltpu.VMEM((cols, dim), BF16),
            pltpu.SemaphoreType.DMA((n_img + n_txt,)),
        ],
        compiler_params=pltpu.CompilerParams(vmem_limit_bytes=40 * 1024 * 1024),
        cost_estimate=pl.CostEstimate(flops=2 * flops, bytes_accessed=10 * 1024 * 1024, transcendentals=2 * rows * cols),
    )(scalars, *img_parts, *txt_parts)
    grads = pl.pallas_call(
        lambda *refs: image_kernel(n_txt, *refs),
        out_shape=tuple(
            jax.ShapeDtypeStruct(p.shape, F32 if n == 0 else BF16) for n, p in enumerate(img_parts)
        ),
        in_specs=[vmem] + [anywhere] * n_txt,
        out_specs=tuple([vmem] * n_img),
        scratch_shapes=[pltpu.VMEM((cols, dim), BF16), pltpu.SemaphoreType.DMA((n_txt,))],
        compiler_params=pltpu.CompilerParams(vmem_limit_bytes=40 * 1024 * 1024),
        cost_estimate=pl.CostEstimate(flops=flops, bytes_accessed=8 * 1024 * 1024, transcendentals=0),
    )(w, *txt_parts)
    return keep, send, grads


def local(images, texts, log_temp, bias):
    own = images.shape[0]
    img_unit, inv_img = normalize(images)
    txt_unit, inv_txt = normalize(texts)
    img_round = img_unit.astype(BF16)
    txt_round = txt_unit.astype(BF16)
    scalars = jnp.concatenate([jnp.exp(log_temp), bias])

    side = [shift(img_round, first(k)) for k in (1, 2, 3)]
    swapped = shift(txt_round, other)
    pair = cat([txt_round, swapped])
    near2 = shift(pair, line(2))
    near1 = shift(pair, line(1))
    group = cat([img_round] + side)
    far = [shift(group, second(k)) for k in (1, 2, 3)]
    tied = lax.optimization_barrier((near2, *side))[0]
    near3 = shift(tied, line(1))
    near4 = shift(tied[:own], line(2))
    mine = [txt_round, near4, near1, near2, near3]
    theirs = [swapped] + [shift(v, other) for v in mine[1:]]

    keep, send, grads = block([group] + far, mine + theirs, scalars, own)

    total = keep.astype(F32) + shift(send, other).astype(F32)
    packed = total.astype(BF16)
    part4, part1 = packed[own:2 * own], packed[2 * own:4 * own]
    part2, part3 = total[4 * own:6 * own], packed[6 * own:]
    got3 = shift(part3, line(-1))
    got4 = shift(part4, line(-2))
    part2 = part2 + got3.astype(F32)
    part2 = cat([part2[:own] + got4.astype(F32), part2[own:]]).astype(BF16)
    got1 = shift(part1, line(-1))
    got2 = shift(part2, line(-2))
    landed = got1.astype(F32) + got2.astype(F32)
    grad_txt = total[:own] + landed[:own] + shift(landed[own:].astype(BF16), other).astype(F32)

    back = [shift(g, second(-k)) for k, g in zip((1, 2, 3), grads[1:])]
    sums = grads[0] + sum(b.astype(F32) for b in back)
    sums16 = sums.astype(BF16)
    last = [shift(sums16[k * own:(k + 1) * own], first(-k)) for k in (1, 2, 3)]
    grad_img = sums[:own] + sum(b.astype(F32) for b in last)

    return back_norm(img_unit, inv_img, grad_img), back_norm(txt_unit, inv_txt, grad_txt)


def solution(mesh):
    in_specs = (P(("row", "col"), None), P(("row", "col"), None), P(), P())
    out_specs = (P(("row", "col"), None), P(("row", "col"), None))
    return jax.shard_map(local, mesh=mesh, in_specs=in_specs, out_specs=out_specs, check_vma=False)
```

```python
import jax
import jax.numpy as jnp
from jax import lax
from jax.experimental import pallas as pl
from jax.experimental.pallas import tpu as pltpu
from jax.sharding import PartitionSpec as P

AXES = ("row", "col")
F32 = jnp.float32
BF16 = jnp.bfloat16
LOG2E = 1.4426950408889634
SIZE_X, SIZE_Y, SIZE_Z, CORES = 4, 4, 8, 2


def device(x, y, z, c):
    return ((z // 4) * 16 + x * 4 + y) * 8 + (z % 4) * 2 + c


def shift(values, move, name="move"):
    pairs = []
    for x in range(SIZE_X):
        for y in range(SIZE_Y):
            for z in range(SIZE_Z):
                for c in range(CORES):
                    nx, ny, nz, nc = move(x, y, z, c)
                    pairs.append((device(x, y, z, c), device(nx % SIZE_X, ny % SIZE_Y, nz % SIZE_Z, nc)))
    with jax.named_scope(name):
        return lax.ppermute(values, AXES, pairs)


def first(k):
    return lambda x, y, z, c: (x + k, y, z, c) if c == 0 else (x, y + k, z, c)


def second(k):
    return lambda x, y, z, c: (x, y + k, z, c) if c == 0 else (x + k, y, z, c)


def line(k):
    return lambda x, y, z, c: (x, y, z + k, c) if c == 0 else (x, y, z - k, c)


def other(x, y, z, c):
    return (x, y, z, 1 - c)


def cat(parts):
    return jnp.concatenate(parts, axis=0)


def normalize(raw):
    values = raw.astype(F32)
    inverse = lax.rsqrt(jnp.sum(values * values, axis=1, keepdims=True) + 1e-06)
    return (values * inverse, inverse)


def back_norm(unit, inverse, grad_unit):
    along = jnp.sum(unit * grad_unit, axis=1, keepdims=True)
    return (grad_unit - unit * along) * inverse


def load(parts, whole, sems, base):
    copies, at = [], 0
    for n, part in enumerate(parts):
        rows = part.shape[0]
        copies.append(pltpu.make_async_copy(part, whole.at[pl.ds(at, rows)], sems.at[base + n]))
        at += rows
    for copy in copies:
        copy.start()
    return copies


def weights_kernel(n_img, n_txt, own, scal_ref, *refs):
    img_parts, txt_parts = refs[:n_img], refs[n_img:n_img + n_txt]
    w_ref, keep_ref, send_ref, txt, img, sems = refs[n_img + n_txt:]
    img_copies = load(img_parts, img, sems, 0)
    txt_copies = load(txt_parts, txt, sems, n_img)
    temp, shift_ = scal_ref[0], scal_ref[1]
    slope, offset = -temp * LOG2E, -shift_ * LOG2E
    for copy in txt_copies:
        copy.wait()
    at = 0
    for part, copy in zip(img_parts, img_copies):
        copy.wait()
        rows = part.shape[0]
        dots = lax.dot_general(
            img[at:at + rows, :], txt[...], (((1,), (1,)), ((), ())), preferred_element_type=F32
        )
        power = dots * slope + offset
        w_ref[at:at + rows, :] = (temp / (1.0 + jnp.exp2(power))).astype(BF16)
        if at == 0:
            corner = power[:own, :2 * own]
            row = lax.broadcasted_iota(jnp.int32, corner.shape, 0)
            column = lax.broadcasted_iota(jnp.int32, corner.shape, 1)
            positive = row == column
            signed = jnp.where(positive, -corner, corner)
            scale = jnp.where(positive, -temp, temp)
            w_ref[:own, :2 * own] = (scale / (1.0 + jnp.exp2(signed))).astype(BF16)
        at += rows
    half = txt.shape[0] // 2
    step = 256
    for out, start in ((send_ref, half), (keep_ref, 0)):
        for t in range(0, half, step):
            grad = lax.dot_general(
                w_ref[:, start + t:start + t + step], img[...], (((0,), (0,)), ((), ())), preferred_element_type=F32
            )
            out[t:t + step, :] = grad.astype(out.dtype)


def image_kernel(w_ref, txt, *outs):
    at = 0
    for out in outs:
        rows = out.shape[0]
        grad = jnp.dot(w_ref[at:at + rows, :], txt[...], preferred_element_type=F32)
        out[...] = grad.astype(out.dtype)
        at += rows


def block(img_parts, txt_parts, scalars, own):
    n_img, n_txt = len(img_parts), len(txt_parts)
    rows = sum(p.shape[0] for p in img_parts)
    cols = sum(p.shape[0] for p in txt_parts)
    dim = img_parts[0].shape[1]
    anywhere = pl.BlockSpec(memory_space=pl.ANY)
    vmem = pl.BlockSpec(memory_space=pltpu.VMEM)
    flops = 2 * rows * cols * dim
    w, keep, send, txt = pl.pallas_call(
        lambda *refs: weights_kernel(n_img, n_txt, own, *refs),
        out_shape=(
            jax.ShapeDtypeStruct((rows, cols), BF16),
            jax.ShapeDtypeStruct((cols // 2, dim), BF16),
            jax.ShapeDtypeStruct((cols // 2, dim), BF16),
            jax.ShapeDtypeStruct((cols, dim), BF16),
        ),
        in_specs=[pl.BlockSpec(memory_space=pltpu.SMEM)] + [anywhere] * (n_img + n_txt),
        out_specs=(vmem, vmem, vmem, vmem),
        scratch_shapes=[
            pltpu.VMEM((rows, dim), BF16),
            pltpu.SemaphoreType.DMA((n_img + n_txt,)),
        ],
        compiler_params=pltpu.CompilerParams(vmem_limit_bytes=32 * 1024 * 1024),
        cost_estimate=pl.CostEstimate(flops=2 * flops, bytes_accessed=10 * 1024 * 1024, transcendentals=2 * rows * cols),
    )(scalars, *img_parts, *txt_parts)
    grads = pl.pallas_call(
        image_kernel,
        out_shape=tuple(
            jax.ShapeDtypeStruct(p.shape, F32 if n == 0 else BF16) for n, p in enumerate(img_parts)
        ),
        in_specs=[vmem] * 2,
        out_specs=tuple([vmem] * n_img),
        compiler_params=pltpu.CompilerParams(vmem_limit_bytes=32 * 1024 * 1024),
        cost_estimate=pl.CostEstimate(flops=flops, bytes_accessed=8 * 1024 * 1024, transcendentals=0),
    )(w, txt)
    return keep, send, grads


def after(value, *others):
    return lax.optimization_barrier((value, *others))[0]


def local(images, texts, log_temp, bias):
    own = images.shape[0]
    img_unit, inv_img = normalize(images)
    img_round = img_unit.astype(BF16)
    txt_unit, inv_txt = normalize(after(texts, img_round))
    txt_round = txt_unit.astype(BF16)
    scalars = jnp.concatenate([jnp.exp(log_temp), bias])

    side = [shift(img_round, first(k), "gA%d" % k) for k in (1, 2, 3)]
    swapped = shift(txt_round, other, "gC")
    pair = cat([txt_round, swapped])
    near2 = shift(pair, line(2), "gZ2")
    near1 = shift(pair, line(1), "gZ1")
    group = cat([img_round] + side)
    far = [shift(group, second(k), "gB%d" % k) for k in (1, 2, 3)]
    tied = after(near2, group)
    near3 = shift(tied, line(1), "gZ3")
    near4 = shift(tied[:own], line(2), "gZ4")
    mine = [txt_round, near4, near1, near2, near3]
    theirs = [swapped] + [shift(v, other, "gS%d" % n) for v, n in zip(mine[1:], (4, 1, 2, 3))]

    keep, send, grads = block([group] + far, mine + theirs, scalars, own)

    total = keep.astype(F32) + shift(send, other, "rC").astype(F32)
    packed = total.astype(BF16)
    part4, part1 = packed[own:2 * own], packed[2 * own:4 * own]
    part2, part3 = total[4 * own:6 * own], packed[6 * own:]
    got3 = shift(part3, line(-1), "rZ3")
    got4 = shift(part4, line(-2), "rZ4")
    part2 = part2 + got3.astype(F32)
    part2 = cat([part2[:own] + got4.astype(F32), part2[own:]]).astype(BF16)
    got1 = shift(after(part1, part2), line(-1), "rZ1")
    got2 = shift(part2, line(-2), "rZ2")
    landed = got1.astype(F32) + got2.astype(F32)
    grad_txt = total[:own] + landed[:own] + shift(landed[own:].astype(BF16), other, "rS").astype(F32)

    back = [shift(g, second(-k), "rB%d" % k) for k, g in zip((1, 2, 3), grads[1:])]
    sums = after(grads[0], part2) + sum(b.astype(F32) for b in back)
    sums16 = sums.astype(BF16)
    last = [shift(sums16[k * own:(k + 1) * own], first(-k), "rA%d" % k) for k in (1, 2, 3)]
    grad_img = sums[:own] + sum(b.astype(F32) for b in last)

    return back_norm(img_unit, inv_img, grad_img), back_norm(txt_unit, inv_txt, grad_txt)


def solution(mesh):
    in_specs = (P(("row", "col"), None), P(("row", "col"), None), P(), P())
    out_specs = (P(("row", "col"), None), P(("row", "col"), None))
    return jax.shard_map(local, mesh=mesh, in_specs=in_specs, out_specs=out_specs, check_vma=False)
```

```python
import jax
import jax.numpy as jnp
from jax import lax
from jax.experimental import pallas as pl
from jax.experimental.pallas import tpu as pltpu
from jax.sharding import PartitionSpec as P

AXES = ("row", "col")
F32 = jnp.float32
BF16 = jnp.bfloat16
LOG2E = 1.4426950408889634
SIZE_X, SIZE_Y, SIZE_Z, CORES = 4, 4, 8, 2


def device(x, y, z, c):
    return ((z // 4) * 16 + x * 4 + y) * 8 + (z % 4) * 2 + c


def shift(values, move, name="move"):
    pairs = []
    for x in range(SIZE_X):
        for y in range(SIZE_Y):
            for z in range(SIZE_Z):
                for c in range(CORES):
                    nx, ny, nz, nc = move(x, y, z, c)
                    pairs.append((device(x, y, z, c), device(nx % SIZE_X, ny % SIZE_Y, nz % SIZE_Z, nc)))
    with jax.named_scope(name):
        return lax.ppermute(values, AXES, pairs)


def first(k):
    return lambda x, y, z, c: (x + k, y, z, c) if c == 0 else (x, y + k, z, c)


def second(k):
    return lambda x, y, z, c: (x, y + k, z, c) if c == 0 else (x + k, y, z, c)


def line(k):
    return lambda x, y, z, c: (x, y, z + k, c) if c == 0 else (x, y, z - k, c)


def cross(k):
    return lambda x, y, z, c: (x, y, z + k, 0) if c == 1 else (x, y, z - k, 1)


def other(x, y, z, c):
    return (x, y, z, 1 - c)


def cat(parts):
    return jnp.concatenate(parts, axis=0)


def normalize_kernel(raw_ref, round_ref, unit_ref, inv_ref):
    values = raw_ref[...].astype(F32)
    inverse = lax.rsqrt(jnp.sum(values * values, axis=1, keepdims=True) + 1e-06)
    unit = values * inverse
    unit_ref[...] = unit
    round_ref[...] = unit.astype(BF16)
    inv_ref[...] = jnp.broadcast_to(inverse, inv_ref.shape)


def normalize(raw):
    rows = raw.shape[0]
    vmem = pl.BlockSpec(memory_space=pltpu.VMEM)
    rounded, unit, inverse = pl.pallas_call(
        normalize_kernel,
        out_shape=(
            jax.ShapeDtypeStruct(raw.shape, BF16),
            jax.ShapeDtypeStruct(raw.shape, F32),
            jax.ShapeDtypeStruct((rows, 128), F32),
        ),
        in_specs=[vmem],
        out_specs=(vmem, vmem, vmem),
        cost_estimate=pl.CostEstimate(flops=4 * raw.size, bytes_accessed=8 * raw.size, transcendentals=rows),
    )(raw)
    return rounded, unit, inverse[:, :1]


def token_kernel(value_ref, token_ref):
    token_ref[...] = jnp.zeros_like(token_ref)


def token(value):
    return pl.pallas_call(
        token_kernel,
        out_shape=jax.ShapeDtypeStruct((8, 128), F32),
        in_specs=[pl.BlockSpec(memory_space=pl.ANY)],
        out_specs=pl.BlockSpec(memory_space=pltpu.VMEM),
        cost_estimate=pl.CostEstimate(flops=40_000_000_000, bytes_accessed=1024, transcendentals=0),
    )(value)


def back_norm(unit, inverse, grad_unit):
    along = jnp.sum(unit * grad_unit, axis=1, keepdims=True)
    return (grad_unit - unit * along) * inverse


def sigmoid_weights(power, scale):
    return (scale / (1.0 + jnp.exp2(power))).astype(BF16)


def powers(img, txt, scal_ref):
    slope, offset = -scal_ref[0] * LOG2E, -scal_ref[1] * LOG2E
    dots = lax.dot_general(img, txt, (((1,), (1,)), ((), ())), preferred_element_type=F32)
    return dots * slope + offset


def text_grads(w_ref, img_ref, out_ref):
    step = 256
    for t in range(0, out_ref.shape[0], step):
        grad = lax.dot_general(
            w_ref[:, t:t + step], img_ref[...], (((0,), (0,)), ((), ())), preferred_element_type=F32
        )
        out_ref[t:t + step, :] = grad.astype(out_ref.dtype)


def mine_kernel(own, scal_ref, txt_ref, *refs):
    *parts, w_ref, img_ref = refs
    temp = scal_ref[0]
    at = 0
    for part in parts:
        rows = part.shape[0]
        img = part[...]
        img_ref[at:at + rows, :] = img
        power = powers(img, txt_ref[...], scal_ref)
        w_ref[at:at + rows, :] = sigmoid_weights(power, temp)
        if at == 0:
            corner = power[:own, :2 * own]
            row = lax.broadcasted_iota(jnp.int32, corner.shape, 0)
            column = lax.broadcasted_iota(jnp.int32, corner.shape, 1)
            positive = row == column
            signed = jnp.where(positive, -corner, corner)
            w_ref[:own, :2 * own] = sigmoid_weights(signed, jnp.where(positive, -temp, temp))
        at += rows


def theirs_kernel(scal_ref, txt_ref, img_ref, w_ref, send_ref):
    step = 256
    for at in range(0, img_ref.shape[0], step):
        power = powers(img_ref[at:at + step, :], txt_ref[...], scal_ref)
        w_ref[at:at + step, :] = sigmoid_weights(power, scal_ref[0])
    text_grads(w_ref, img_ref, send_ref)


def image_kernel(w1_ref, w2_ref, txt1_ref, txt2_ref, *outs):
    at = 0
    for out in outs:
        rows = out.shape[0]
        grad = jnp.dot(w1_ref[at:at + rows, :], txt1_ref[...], preferred_element_type=F32)
        grad += jnp.dot(w2_ref[at:at + rows, :], txt2_ref[...], preferred_element_type=F32)
        out[...] = grad.astype(out.dtype)
        at += rows


def call(kernel, outs, scalars, *arrays, flops):
    vmem = pl.BlockSpec(memory_space=pltpu.VMEM)
    smem = pl.BlockSpec(memory_space=pltpu.SMEM)
    few = [] if scalars is None else [scalars]
    return pl.pallas_call(
        kernel,
        out_shape=tuple(jax.ShapeDtypeStruct(shape, dtype) for shape, dtype in outs),
        in_specs=[smem] * len(few) + [vmem] * len(arrays),
        out_specs=tuple([vmem] * len(outs)),
        compiler_params=pltpu.CompilerParams(vmem_limit_bytes=32 * 1024 * 1024),
        cost_estimate=pl.CostEstimate(flops=flops, bytes_accessed=4 * 1024 * 1024, transcendentals=0),
    )(*few, *arrays)


def after_kernel(*refs):
    pass


def together(values, *others):
    anywhere = pl.BlockSpec(memory_space=pl.ANY)
    return pl.pallas_call(
        after_kernel,
        out_shape=tuple(jax.ShapeDtypeStruct(v.shape, v.dtype) for v in values),
        in_specs=[anywhere] * (len(values) + len(others)),
        out_specs=tuple([anywhere] * len(values)),
        input_output_aliases={n: n for n in range(len(values))},
        cost_estimate=pl.CostEstimate(flops=0, bytes_accessed=0, transcendentals=0),
    )(*values, *others)


def after(value, *others):
    return together([value], *others)[0]


def local(images, texts, log_temp, bias):
    own = images.shape[0]
    img_round, img_unit, inv_img = normalize(images)
    txt_round, txt_unit, inv_txt = normalize(texts)
    scalars = jnp.concatenate([jnp.exp(log_temp), bias])

    side = [shift(img_round, first(k), "gA%d" % k) for k in (1, 2, 3)]
    near1 = cat([shift(txt_round, line(1), "gZ1"), shift(txt_round, cross(1), "gX1")])
    group = cat([img_round] + side)
    group, near1 = together([group, near1])
    far = [shift(group, second(k), "gB%d" % k) for k in (1, 2, 3)]
    near2 = shift(near1, line(1), "gZ2")
    near3 = shift(near1, line(2), "gZ3")
    near4 = shift(near1[:own], line(3), "gZ4")
    mine = cat([txt_round, near1, near2, near3, near4])
    far = list(far)
    mine = after(mine, *far)
    theirs = shift(mine, other, "gS")

    half, dim = mine.shape
    rows = group.shape[0] * (1 + len(far))
    flops = 2 * rows * half * dim
    w_mine, img_all = call(
        lambda *refs: mine_kernel(own, *refs), [((rows, half), BF16), ((rows, dim), BF16)],
        scalars, mine, group, *far, flops=flops,
    )
    w_theirs, send = call(
        theirs_kernel, [((rows, half), BF16), ((half, dim), BF16)], scalars, theirs, img_all, flops=2 * flops
    )
    (keep,) = call(text_grads, [((half, dim), BF16)], None, w_mine, img_all, flops=flops)
    grads = call(
        image_kernel, [(group.shape, F32)] + [(group.shape, BF16)] * len(far),
        None, w_mine, w_theirs, mine, theirs, flops=2 * flops,
    )

    total = keep.astype(F32) + shift(send, other, "rC").astype(F32)
    packed = total.astype(BF16)
    part1, part2 = packed[own:3 * own], total[3 * own:5 * own]
    part3, part4 = packed[5 * own:7 * own], packed[7 * own:]
    got3 = shift(part3, line(-1), "rZ3")
    got4 = shift(part4, line(-2), "rZ4")
    part2 = part2 + got3.astype(F32)
    part2 = cat([part2[:own] + got4.astype(F32), part2[own:]]).astype(BF16)
    got1 = shift(part1, line(-1), "rZ1")
    got2 = shift(part2, line(-2), "rZ2")
    landed = got1.astype(F32) + got2.astype(F32)
    grad_txt = total[:own] + landed[:own] + shift(landed[own:].astype(BF16), other, "rS").astype(F32)

    back = [shift(g, second(-k), "rB%d" % k) for k, g in zip((1, 2, 3), grads[1:])]
    sums = after(grads[0], token(part2)) + sum(b.astype(F32) for b in back)
    sums16 = sums.astype(BF16)
    last = [shift(sums16[k * own:(k + 1) * own], first(-k), "rA%d" % k) for k in (1, 2, 3)]
    grad_img = sums[:own] + sum(b.astype(F32) for b in last)

    return back_norm(img_unit, inv_img, grad_img), back_norm(txt_unit, inv_txt, grad_txt)


def solution(mesh):
    in_specs = (P(("row", "col"), None), P(("row", "col"), None), P(), P())
    out_specs = (P(("row", "col"), None), P(("row", "col"), None))
    return jax.shard_map(local, mesh=mesh, in_specs=in_specs, out_specs=out_specs, check_vma=False)
```

```python
import jax
import jax.numpy as jnp
from jax import lax
from jax.experimental import pallas as pl
from jax.experimental.pallas import tpu as pltpu
from jax.sharding import PartitionSpec as P

AXES = ("row", "col")
F32 = jnp.float32
BF16 = jnp.bfloat16
LOG2E = 1.4426950408889634
SIZE_X, SIZE_Y, SIZE_Z, CORES = 4, 4, 8, 2


def device(x, y, z, c):
    return ((z // 4) * 16 + x * 4 + y) * 8 + (z % 4) * 2 + c


def shift(values, move, name="move"):
    pairs = []
    for x in range(SIZE_X):
        for y in range(SIZE_Y):
            for z in range(SIZE_Z):
                for c in range(CORES):
                    nx, ny, nz, nc = move(x, y, z, c)
                    pairs.append((device(x, y, z, c), device(nx % SIZE_X, ny % SIZE_Y, nz % SIZE_Z, nc)))
    with jax.named_scope(name):
        return lax.ppermute(values, AXES, pairs)


def first(k):
    return lambda x, y, z, c: (x + k, y, z, c) if c == 0 else (x, y + k, z, c)


def second(k):
    return lambda x, y, z, c: (x, y + k, z, c) if c == 0 else (x + k, y, z, c)


def line(k):
    return lambda x, y, z, c: (x, y, z + k, c) if c == 0 else (x, y, z - k, c)


def cross(k):
    return lambda x, y, z, c: (x, y, z + k, 0) if c == 1 else (x, y, z - k, 1)


def other(x, y, z, c):
    return (x, y, z, 1 - c)


def call(kernel, outs, arrays, scalars=None, ties=(), flops=0, limit=8):
    vmem = pl.BlockSpec(memory_space=pltpu.VMEM)
    few = [] if scalars is None else [scalars]
    n_in = len(few) + len(arrays)
    specs = [pl.BlockSpec(memory_space=pltpu.SMEM)] * len(few) + [vmem] * len(arrays)
    return pl.pallas_call(
        lambda *refs: kernel(*refs[:n_in], *refs[n_in + len(ties):]),
        out_shape=tuple(jax.ShapeDtypeStruct(shape, dtype) for shape, dtype in outs),
        in_specs=specs + [pl.BlockSpec(memory_space=pl.ANY)] * len(ties),
        out_specs=tuple([vmem] * len(outs)),
        compiler_params=pltpu.CompilerParams(vmem_limit_bytes=limit * 1024 * 1024),
        cost_estimate=pl.CostEstimate(flops=flops, bytes_accessed=1024, transcendentals=0),
    )(*few, *arrays, *ties)


def token_kernel(token_ref):
    token_ref[...] = jnp.zeros_like(token_ref)


def token(value):
    return call(token_kernel, [((8, 128), F32)], [], ties=[value], flops=40_000_000_000, limit=1)[0]


def unit_rows(raw):
    values = raw.astype(F32)
    inverse = lax.rsqrt(jnp.sum(values * values, axis=1, keepdims=True) + 1e-06)
    return values * inverse, inverse


def back_norm(unit, inverse, grad_unit):
    along = jnp.sum(unit * grad_unit, axis=1, keepdims=True)
    return (grad_unit - unit * along) * inverse


def pair_kernel(first_ref, second_ref, out_ref):
    rows = first_ref.shape[0]
    out_ref[:rows, :] = first_ref[...]
    out_ref[rows:, :] = second_ref[...]


def group_kernel(*refs):
    *parts, pair_ref, near_ref, group_ref, send_ref, head_ref = refs
    rows = parts[0].shape[0]
    for n, part in enumerate(parts):
        group_ref[n * rows:(n + 1) * rows, :] = part[...]
    send_ref[:2 * rows, :] = pair_ref[...]
    send_ref[2 * rows:, :] = near_ref[...]
    head_ref[...] = near_ref[:rows, :]


def round_kernel(own, *refs):
    *parts, out_ref, unit_ref, inv_ref = refs
    base = 0
    for part in parts:
        for at in range(0, part.shape[0], own):
            unit, inverse = unit_rows(part[at:at + own, :])
            out_ref[base:base + own, :] = unit.astype(BF16)
            if base == 0:
                unit_ref[...] = unit
                inv_ref[...] = jnp.broadcast_to(inverse, inv_ref.shape)
            base += own


def rounded(parts, own, ties=()):
    rows, dim = sum(p.shape[0] for p in parts), parts[0].shape[1]
    outs = [((rows, dim), BF16), ((own, dim), F32), ((own, 128), F32)]
    return call(lambda *refs: round_kernel(own, *refs), outs, parts, ties=ties)


def sigmoid_weights(power, scale):
    return (scale / (1.0 + jnp.exp2(power))).astype(BF16)


def powers(img, txt, scal_ref):
    slope, offset = -scal_ref[0] * LOG2E, -scal_ref[1] * LOG2E
    dots = lax.dot_general(img, txt, (((1,), (1,)), ((), ())), preferred_element_type=F32)
    return dots * slope + offset


def text_grads(w_ref, img_ref, out_ref):
    step = 256
    for t in range(0, out_ref.shape[0], step):
        grad = lax.dot_general(
            w_ref[:, t:t + step], img_ref[...], (((0,), (0,)), ((), ())), preferred_element_type=F32
        )
        out_ref[t:t + step, :] = grad.astype(out_ref.dtype)


def mine_kernel(own, scal_ref, txt_ref, *refs):
    *parts, w_ref, img_ref, keep_ref = refs
    temp = scal_ref[0]
    at = 0
    for part in parts:
        rows = part.shape[0]
        img = part[...] if at == 0 else unit_rows(part[...])[0].astype(BF16)
        img_ref[at:at + rows, :] = img
        power = powers(img, txt_ref[...], scal_ref)
        w_ref[at:at + rows, :] = sigmoid_weights(power, temp)
        if at == 0:
            corner = power[:own, :2 * own]
            row = lax.broadcasted_iota(jnp.int32, corner.shape, 0)
            column = lax.broadcasted_iota(jnp.int32, corner.shape, 1)
            positive = row == column
            signed = jnp.where(positive, -corner, corner)
            w_ref[:own, :2 * own] = sigmoid_weights(signed, jnp.where(positive, -temp, temp))
        at += rows
    text_grads(w_ref, img_ref, keep_ref)


def theirs_kernel(scal_ref, txt_ref, img_ref, w_ref, send_ref):
    step = 256
    for at in range(0, img_ref.shape[0], step):
        power = powers(img_ref[at:at + step, :], txt_ref[...], scal_ref)
        w_ref[at:at + step, :] = sigmoid_weights(power, scal_ref[0])
    text_grads(w_ref, img_ref, send_ref)


def image_kernel(w1_ref, w2_ref, txt1_ref, txt2_ref, *outs):
    at = 0
    for out in outs:
        rows = out.shape[0]
        grad = jnp.dot(w1_ref[at:at + rows, :], txt1_ref[...], preferred_element_type=F32)
        grad += jnp.dot(w2_ref[at:at + rows, :], txt2_ref[...], preferred_element_type=F32)
        out[...] = grad.astype(out.dtype)
        at += rows


def total_kernel(keep_ref, got_ref, own_ref, part13_ref, part2_ref, part4_ref):
    at = 0
    for out in (own_ref, part13_ref, part2_ref, part4_ref):
        rows = out.shape[0]
        total = keep_ref[at:at + rows, :].astype(F32) + got_ref[at:at + rows, :].astype(F32)
        out[...] = total.astype(out.dtype)
        at += rows


def middle_kernel(part2_ref, got13_ref, got4_ref, out_ref):
    rows = got4_ref.shape[0]
    total = part2_ref[...] + got13_ref[2 * rows:, :].astype(F32)
    out_ref[:rows, :] = (total[:rows] + got4_ref[...].astype(F32)).astype(BF16)
    out_ref[rows:, :] = total[rows:].astype(BF16)


def landed_kernel(own_ref, got13_ref, got2_ref, sum_ref, send_ref):
    rows = own_ref.shape[0]
    sum_ref[...] = own_ref[...] + got13_ref[:rows, :].astype(F32) + got2_ref[:rows, :].astype(F32)
    send_ref[...] = (got13_ref[rows:2 * rows, :].astype(F32) + got2_ref[rows:, :].astype(F32)).astype(BF16)


def sums_kernel(*refs):
    own_ref, *parts = refs[:4]
    outs = refs[4:]
    rows = outs[0].shape[0]
    for n, out in enumerate(outs):
        at = slice(n * rows, (n + 1) * rows)
        out[...] = (own_ref[at, :] + sum(p[at, :].astype(F32) for p in parts)).astype(out.dtype)


def final_kernel(unit_ref, inv_ref, own_ref, *refs):
    *parts, out_ref = refs
    grad = own_ref[...] + sum(p[...].astype(F32) for p in parts)
    out_ref[...] = back_norm(unit_ref[...], inv_ref[:, :1], grad)


def local(images, texts, log_temp, bias):
    own, dim = images.shape
    scalars = jnp.concatenate([jnp.exp(log_temp), bias])

    (pair,) = call(pair_kernel, [((2 * own, dim), BF16)], [texts, shift(texts, other, "gC")])
    side = [shift(images, first(k), "gA%d" % k) for k in (1, 2, 3)]
    near2 = shift(pair, line(2), "gZ2")
    group, send13, send4 = call(
        group_kernel, [((4 * own, dim), BF16), ((4 * own, dim), BF16), ((own, dim), BF16)], [images, *side, pair, near2]
    )
    far = [shift(group, second(k), "gB%d" % k) for k in (1, 2, 3)]
    near13 = shift(send13, line(1), "gZ13")
    near4 = shift(send4, line(2), "gZ4")
    first_token = token(group)
    group, img_unit, inv_img = rounded([group], own)
    mine, txt_unit, inv_txt = rounded([texts, near13, near2, near4], own, [group, first_token, *far])
    theirs = shift(mine, other, "gS")

    half = mine.shape[0]
    rows = group.shape[0] * (1 + len(far))
    flops = 2 * rows * half * dim
    w_mine, img_all, keep = call(
        lambda *refs: mine_kernel(own, *refs), [((rows, half), BF16), ((rows, dim), BF16), ((half, dim), BF16)],
        [mine, group, *far], scalars, flops=2 * flops, limit=24,
    )
    w_theirs, send = call(
        theirs_kernel, [((rows, half), BF16), ((half, dim), BF16)],
        [theirs, img_all], scalars, ties=[keep], flops=2 * flops, limit=24,
    )
    grads = call(
        image_kernel, [(group.shape, F32)] + [(group.shape, BF16)] * len(far),
        [w_mine, w_theirs, mine, theirs], flops=2 * flops, limit=24,
    )

    total_own, part13, part2, part4 = call(
        total_kernel,
        [((own, dim), F32), ((4 * own, dim), BF16), ((2 * own, dim), F32), ((own, dim), BF16)],
        [keep, shift(send, other, "rC")], ties=[grads[-1]],
    )
    got13 = shift(part13, line(-1), "rZ13")
    got4 = shift(part4, line(-2), "rZ4")
    (middle,) = call(middle_kernel, [((2 * own, dim), BF16)], [part2, got13, got4])
    got2 = shift(middle, line(-2), "rZ2")
    txt_sum, txt_send = call(landed_kernel, [((own, dim), F32), ((own, dim), BF16)], [total_own, got13, got2])
    txt_last = shift(txt_send, other, "rS")

    back = [shift(g, second(-k), "rB%d" % k) for k, g in zip((1, 2, 3), grads[1:])]
    img_sum, *parts = call(
        sums_kernel, [((own, dim), F32)] + [((own, dim), BF16)] * 3, [grads[0], *back], ties=[token(middle)]
    )
    last = [shift(p, first(-k), "rA%d" % k) for k, p in zip((1, 2, 3), parts)]

    (grad_img,) = call(final_kernel, [((own, dim), F32)], [img_unit, inv_img, img_sum, *last])
    (grad_txt,) = call(final_kernel, [((own, dim), F32)], [txt_unit, inv_txt, txt_sum, txt_last])
    return grad_img, grad_txt


def solution(mesh):
    in_specs = (P(("row", "col"), None), P(("row", "col"), None), P(), P())
    out_specs = (P(("row", "col"), None), P(("row", "col"), None))
    return jax.shard_map(local, mesh=mesh, in_specs=in_specs, out_specs=out_specs, check_vma=False)
```

```python
import jax
import jax.numpy as jnp
from jax import lax
from jax.experimental import pallas as pl
from jax.experimental.pallas import tpu as pltpu
from jax.sharding import PartitionSpec as P

AXES = ("row", "col")
F32 = jnp.float32
BF16 = jnp.bfloat16
LOG2E = 1.4426950408889634
SIZE_X, SIZE_Y, SIZE_Z, CORES = 4, 4, 8, 2


def device(x, y, z, c):
    return ((z // 4) * 16 + x * 4 + y) * 8 + (z % 4) * 2 + c


def shift(values, move, name="move"):
    pairs = []
    for x in range(SIZE_X):
        for y in range(SIZE_Y):
            for z in range(SIZE_Z):
                for c in range(CORES):
                    nx, ny, nz, nc = move(x, y, z, c)
                    pairs.append((device(x, y, z, c), device(nx % SIZE_X, ny % SIZE_Y, nz % SIZE_Z, nc)))
    with jax.named_scope(name):
        return lax.ppermute(values, AXES, pairs)


def first(k):
    return lambda x, y, z, c: (x + k, y, z, c) if c == 0 else (x, y + k, z, c)


def second(k):
    return lambda x, y, z, c: (x, y + k, z, c) if c == 0 else (x + k, y, z, c)


def line(k):
    return lambda x, y, z, c: (x, y, z + k, c) if c == 0 else (x, y, z - k, c)


def cross(k):
    return lambda x, y, z, c: (x, y, z + k, 0) if c == 1 else (x, y, z - k, 1)


def other(x, y, z, c):
    return (x, y, z, 1 - c)


def call(kernel, outs, arrays, last_scalars=(), ties=(), flops=0, limit=8):
    vmem = pl.BlockSpec(memory_space=pltpu.VMEM)
    n_in = len(arrays) + len(last_scalars)
    specs = [vmem] * len(arrays) + [pl.BlockSpec(memory_space=pltpu.SMEM)] * len(last_scalars)
    return pl.pallas_call(
        lambda *refs: kernel(*refs[:n_in], *refs[n_in + len(ties):]),
        out_shape=tuple(jax.ShapeDtypeStruct(shape, dtype) for shape, dtype in outs),
        in_specs=specs + [pl.BlockSpec(memory_space=pl.ANY)] * len(ties),
        out_specs=tuple([vmem] * len(outs)),
        compiler_params=pltpu.CompilerParams(vmem_limit_bytes=limit * 1024 * 1024),
        cost_estimate=pl.CostEstimate(flops=flops, bytes_accessed=1024, transcendentals=0),
    )(*arrays, *last_scalars, *ties)


def token_kernel(token_ref):
    token_ref[...] = jnp.zeros_like(token_ref)


def token(value):
    return call(token_kernel, [((8, 128), F32)], [], ties=[value], flops=40_000_000_000, limit=1)[0]


def unit_rows(raw):
    values = raw.astype(F32)
    inverse = lax.rsqrt(jnp.sum(values * values, axis=1, keepdims=True) + 1e-06)
    return values * inverse, inverse


def back_norm(unit, inverse, grad_unit):
    along = jnp.sum(unit * grad_unit, axis=1, keepdims=True)
    return (grad_unit - unit * along) * inverse


def own_kernel(img_ref, txt_ref, log_ref, bias_ref, *outs):
    *outs, scal_ref = outs
    for n, raw_ref in enumerate((img_ref, txt_ref)):
        copy_ref, unit_ref, inv_ref = outs[3 * n:3 * n + 3]
        unit, inverse = unit_rows(raw_ref[...])
        copy_ref[...] = raw_ref[...]
        unit_ref[...] = unit
        inv_ref[...] = jnp.broadcast_to(inverse, inv_ref.shape)
    temp = jnp.exp(jnp.full((1, 128), log_ref[0], F32))
    scal_ref[0:1, :] = temp
    scal_ref[1:2, :] = -LOG2E * temp
    scal_ref[2:3, :] = jnp.full((1, 128), -LOG2E * bias_ref[0], F32)


def stack_kernel(*refs):
    *parts, out_ref = refs
    at = 0
    for part in parts:
        rows = part.shape[0]
        out_ref[at:at + rows, :] = part[...]
        at += rows


def stack(parts, ties=()):
    rows, dim = sum(p.shape[0] for p in parts), parts[0].shape[1]
    return call(stack_kernel, [((rows, dim), BF16)], parts, ties=ties)[0]


def round_kernel(step, *refs):
    *parts, out_ref = refs
    base = 0
    for part in parts:
        for at in range(0, part.shape[0], step):
            out_ref[base:base + step, :] = unit_rows(part[at:at + step, :])[0].astype(BF16)
            base += step


def rounded(parts, ties=()):
    rows, dim = sum(p.shape[0] for p in parts), parts[0].shape[1]
    return call(lambda *refs: round_kernel(64, *refs), [((rows, dim), BF16)], parts, ties=ties)[0]


def sigmoid_weights(power, scale):
    return (scale / (1.0 + jnp.exp2(power))).astype(BF16)


def powers(img, txt, scal_ref):
    slope, offset = scal_ref[1:2, 0:1], scal_ref[2:3, 0:1]
    dots = lax.dot_general(img, txt, (((1,), (1,)), ((), ())), preferred_element_type=F32)
    return dots * slope + offset


def text_grads(w_ref, img_ref, out_ref):
    step = 256
    for t in range(0, out_ref.shape[0], step):
        grad = lax.dot_general(
            w_ref[:, t:t + step], img_ref[...], (((0,), (0,)), ((), ())), preferred_element_type=F32
        )
        out_ref[t:t + step, :] = grad.astype(out_ref.dtype)


def mine_kernel(own, txt_ref, scal_ref, *refs):
    *parts, w_ref, img_ref, keep_ref = refs
    temp = scal_ref[0:1, 0:1]
    at = 0
    for part in parts:
        rows = part.shape[0]
        img = part[...] if at == 0 else unit_rows(part[...])[0].astype(BF16)
        img_ref[at:at + rows, :] = img
        power = powers(img, txt_ref[...], scal_ref)
        w_ref[at:at + rows, :] = sigmoid_weights(power, temp)
        if at == 0:
            corner = power[:own, :2 * own]
            row = lax.broadcasted_iota(jnp.int32, corner.shape, 0)
            column = lax.broadcasted_iota(jnp.int32, corner.shape, 1)
            positive = row == column
            signed = jnp.where(positive, -corner, corner)
            w_ref[:own, :2 * own] = sigmoid_weights(signed, jnp.where(positive, -temp, temp))
        at += rows
    text_grads(w_ref, img_ref, keep_ref)


def theirs_kernel(txt_ref, scal_ref, img_ref, w_ref, send_ref):
    step = 256
    for at in range(0, img_ref.shape[0], step):
        power = powers(img_ref[at:at + step, :], txt_ref[...], scal_ref)
        w_ref[at:at + step, :] = sigmoid_weights(power, scal_ref[0:1, 0:1])
    text_grads(w_ref, img_ref, send_ref)


def image_kernel(w1_ref, w2_ref, txt1_ref, txt2_ref, *outs):
    at = 0
    for out in outs:
        rows = out.shape[0]
        grad = jnp.dot(w1_ref[at:at + rows, :], txt1_ref[...], preferred_element_type=F32)
        grad += jnp.dot(w2_ref[at:at + rows, :], txt2_ref[...], preferred_element_type=F32)
        out[...] = grad.astype(out.dtype)
        at += rows


def total_kernel(keep_ref, got_ref, own_ref, part13_ref, part2_ref, part4_ref):
    at = 0
    for out in (own_ref, part13_ref, part2_ref, part4_ref):
        rows = out.shape[0]
        total = keep_ref[at:at + rows, :].astype(F32) + got_ref[at:at + rows, :].astype(F32)
        out[...] = total.astype(out.dtype)
        at += rows


def middle_kernel(part2_ref, got13_ref, got4_ref, out_ref):
    rows = got4_ref.shape[0]
    total = part2_ref[...] + got13_ref[2 * rows:, :].astype(F32)
    out_ref[:rows, :] = (total[:rows] + got4_ref[...].astype(F32)).astype(BF16)
    out_ref[rows:, :] = total[rows:].astype(BF16)


def landed_kernel(own_ref, got13_ref, got2_ref, sum_ref, send_ref):
    rows = own_ref.shape[0]
    sum_ref[...] = own_ref[...] + got13_ref[:rows, :].astype(F32) + got2_ref[:rows, :].astype(F32)
    send_ref[...] = (got13_ref[rows:2 * rows, :].astype(F32) + got2_ref[rows:, :].astype(F32)).astype(BF16)


def sums_kernel(*refs):
    own_ref, *parts = refs[:4]
    outs = refs[4:]
    rows = outs[0].shape[0]
    for n, out in enumerate(outs):
        at = slice(n * rows, (n + 1) * rows)
        out[...] = (own_ref[at, :] + sum(p[at, :].astype(F32) for p in parts)).astype(out.dtype)


def final_kernel(*refs):
    *ins, img_ref, txt_ref = refs
    for (unit_ref, inv_ref, own_ref, *parts), out_ref in ((ins[:6], img_ref), (ins[6:], txt_ref)):
        grad = own_ref[...] + sum(p[...].astype(F32) for p in parts)
        out_ref[...] = back_norm(unit_ref[...], inv_ref[:, :1], grad)


def local(images, texts, log_temp, bias):
    own, dim = images.shape
    per_row = [((own, dim), BF16), ((own, dim), F32), ((own, 128), F32)]

    side = [shift(images, first(k), "gA%d" % k) for k in (1, 2, 3)]
    line2 = shift(texts, line(2), "gZ2")
    cross2 = shift(texts, cross(2), "gX2")
    img_own, img_unit, inv_img, txt_own, txt_unit, inv_txt, scalars = call(
        own_kernel, per_row * 2 + [((8, 128), F32)], [images, texts], last_scalars=[log_temp, bias]
    )
    swapped = shift(txt_own, other, "gC")
    group = stack([img_own, *side])
    send13 = stack([txt_own, swapped, line2, cross2])
    far = [shift(group, second(k), "gB%d" % k) for k in (1, 2, 3)]
    near13 = shift(send13, line(1), "gZ13")
    near4 = shift(line2, line(2), "gZ4")
    first_token = token(group)
    group = rounded([group])
    mine = rounded([txt_own, near13, line2, cross2, near4], [group, first_token, *far])
    theirs = shift(mine, other, "gS")

    half = mine.shape[0]
    rows = group.shape[0] * (1 + len(far))
    flops = 2 * rows * half * dim
    w_mine, img_all, keep = call(
        lambda *refs: mine_kernel(own, *refs), [((rows, half), BF16), ((rows, dim), BF16), ((half, dim), BF16)],
        [mine, scalars, group, *far], flops=2 * flops, limit=24,
    )
    w_theirs, send = call(
        theirs_kernel, [((rows, half), BF16), ((half, dim), BF16)],
        [theirs, scalars, img_all], ties=[keep], flops=2 * flops, limit=24,
    )
    grads = call(
        image_kernel, [(group.shape, F32)] + [(group.shape, BF16)] * len(far),
        [w_mine, w_theirs, mine, theirs], flops=2 * flops, limit=24,
    )

    total_own, part13, part2, part4 = call(
        total_kernel,
        [((own, dim), F32), ((4 * own, dim), BF16), ((2 * own, dim), F32), ((own, dim), BF16)],
        [keep, shift(send, other, "rC")], ties=[grads[-1]],
    )
    got13 = shift(part13, line(-1), "rZ13")
    got4 = shift(part4, line(-2), "rZ4")
    (middle,) = call(middle_kernel, [((2 * own, dim), BF16)], [part2, got13, got4])
    got2 = shift(middle, line(-2), "rZ2")
    txt_sum, txt_send = call(landed_kernel, [((own, dim), F32), ((own, dim), BF16)], [total_own, got13, got2])
    txt_last = shift(txt_send, other, "rS")

    back = [shift(g, second(-k), "rB%d" % k) for k, g in zip((1, 2, 3), grads[1:])]
    img_sum, *parts = call(
        sums_kernel, [((own, dim), F32)] + [((own, dim), BF16)] * 3, [grads[0], *back], ties=[token(middle)]
    )
    last = [shift(p, first(-k), "rA%d" % k) for k, p in zip((1, 2, 3), parts)]

    return call(
        final_kernel, [((own, dim), F32)] * 2,
        [img_unit, inv_img, img_sum, *last, txt_unit, inv_txt, txt_sum, txt_last],
    )


def solution(mesh):
    in_specs = (P(("row", "col"), None), P(("row", "col"), None), P(), P())
    out_specs = (P(("row", "col"), None), P(("row", "col"), None))
    return jax.shard_map(local, mesh=mesh, in_specs=in_specs, out_specs=out_specs, check_vma=False)
```

```python
import jax
import jax.numpy as jnp
from jax import lax
from jax.experimental import pallas as pl
from jax.experimental.pallas import tpu as pltpu
from jax.sharding import PartitionSpec as P

AXES = ("row", "col")
F32 = jnp.float32
BF16 = jnp.bfloat16
LOG2E = 1.4426950408889634
SIZE_X, SIZE_Y, SIZE_Z, CORES = 4, 4, 8, 2


def device(x, y, z, c):
    return ((z // 4) * 16 + x * 4 + y) * 8 + (z % 4) * 2 + c


def shift(values, move, name="move"):
    pairs = []
    for x in range(SIZE_X):
        for y in range(SIZE_Y):
            for z in range(SIZE_Z):
                for c in range(CORES):
                    nx, ny, nz, nc = move(x, y, z, c)
                    pairs.append((device(x, y, z, c), device(nx % SIZE_X, ny % SIZE_Y, nz % SIZE_Z, nc)))
    with jax.named_scope(name):
        return lax.ppermute(values, AXES, pairs)


def first(k):
    return lambda x, y, z, c: (x + k, y, z, c) if c == 0 else (x, y + k, z, c)


def second(k):
    return lambda x, y, z, c: (x, y + k, z, c) if c == 0 else (x + k, y, z, c)


def line(k):
    return lambda x, y, z, c: (x, y, z + k, c) if c == 0 else (x, y, z - k, c)


def cross(k):
    return lambda x, y, z, c: (x, y, z + k, 0) if c == 1 else (x, y, z - k, 1)


def other(x, y, z, c):
    return (x, y, z, 1 - c)


def call(kernel, outs, arrays, ties=(), flops=0, limit=8):
    vmem = pl.BlockSpec(memory_space=pltpu.VMEM)
    n_in = len(arrays)
    return pl.pallas_call(
        lambda *refs: kernel(*refs[:n_in], *refs[n_in + len(ties):]),
        out_shape=tuple(jax.ShapeDtypeStruct(shape, dtype) for shape, dtype in outs),
        in_specs=[vmem] * n_in + [pl.BlockSpec(memory_space=pl.ANY)] * len(ties),
        out_specs=tuple([vmem] * len(outs)),
        compiler_params=pltpu.CompilerParams(vmem_limit_bytes=limit * 1024 * 1024),
        cost_estimate=pl.CostEstimate(flops=flops, bytes_accessed=1024, transcendentals=0),
    )(*arrays, *ties)


def token_kernel(token_ref):
    token_ref[...] = jnp.zeros_like(token_ref)


def token(*values):
    return call(token_kernel, [((8, 128), F32)], [], ties=values, flops=40_000_000_000, limit=1)[0]


def unit_rows(raw):
    values = raw.astype(F32)
    inverse = lax.rsqrt(jnp.sum(values * values, axis=1, keepdims=True) + 1e-06)
    return values * inverse, inverse


def back_norm(unit, inverse, grad_unit):
    along = jnp.sum(unit * grad_unit, axis=1, keepdims=True)
    return (grad_unit - unit * along) * inverse


def own_kernel(img_hbm, txt_hbm, *refs):
    *outs, sems = refs
    pairs = ((img_hbm, outs[0]), (txt_hbm, outs[3]))
    copies = [pltpu.make_async_copy(src, dst, sems.at[n]) for n, (src, dst) in enumerate(pairs)]
    for copy in copies:
        copy.start()
    for copy in copies:
        copy.wait()
    for raw_ref, unit_ref, inv_ref in (outs[:3], outs[3:]):
        unit, inverse = unit_rows(raw_ref[...])
        unit_ref[...] = unit
        inv_ref[...] = jnp.broadcast_to(inverse, inv_ref.shape)


def own_rows(images, texts, tie):
    own, dim = images.shape
    outs = [((own, dim), BF16), ((own, dim), F32), ((own, 128), F32)] * 2
    return pl.pallas_call(
        lambda tie_ref, *refs: own_kernel(*refs),
        out_shape=tuple(jax.ShapeDtypeStruct(shape, dtype) for shape, dtype in outs),
        in_specs=[pl.BlockSpec(memory_space=pl.ANY)] * 3,
        out_specs=tuple([pl.BlockSpec(memory_space=pltpu.VMEM)] * len(outs)),
        scratch_shapes=[pltpu.SemaphoreType.DMA((2,))],
        compiler_params=pltpu.CompilerParams(vmem_limit_bytes=8 * 1024 * 1024),
        cost_estimate=pl.CostEstimate(flops=0, bytes_accessed=1024, transcendentals=0),
    )(tie, images, texts)


def stack_kernel(*refs):
    *parts, out_ref = refs
    at = 0
    for part in parts:
        rows = part.shape[0]
        out_ref[at:at + rows, :] = part[...]
        at += rows


def stack(parts, ties=()):
    rows, dim = sum(p.shape[0] for p in parts), parts[0].shape[1]
    return call(stack_kernel, [((rows, dim), BF16)], parts, ties=ties)[0]


def round_kernel(step, *refs):
    *parts, out_ref = refs
    base = 0
    for part in parts:
        for at in range(0, part.shape[0], step):
            out_ref[base:base + step, :] = unit_rows(part[at:at + step, :])[0].astype(BF16)
            base += step


def rounded(parts, ties=()):
    rows, dim = sum(p.shape[0] for p in parts), parts[0].shape[1]
    return call(lambda *refs: round_kernel(64, *refs), [((rows, dim), BF16)], parts, ties=ties)[0]


def scalar_kernel(log_ref, bias_ref, scal_ref):
    temp = jnp.exp(jnp.broadcast_to(log_ref[...], (1, 128)))
    scal_ref[...] = jnp.zeros_like(scal_ref)
    scal_ref[0:1, :] = temp
    scal_ref[1:2, :] = -LOG2E * temp
    scal_ref[2:3, :] = jnp.broadcast_to(-LOG2E * bias_ref[...], (1, 128))


def sigmoid_weights(power, scale):
    return (scale / (1.0 + jnp.exp2(power))).astype(BF16)


def powers(img, txt, scal_ref):
    slope, offset = scal_ref[1:2, 0:1], scal_ref[2:3, 0:1]
    dots = lax.dot_general(img, txt, (((1,), (1,)), ((), ())), preferred_element_type=F32)
    return dots * slope + offset


def text_grads(w_ref, img_ref, out_ref):
    step = 256
    for t in range(0, out_ref.shape[0], step):
        grad = lax.dot_general(
            w_ref[:, t:t + step], img_ref[...], (((0,), (0,)), ((), ())), preferred_element_type=F32
        )
        out_ref[t:t + step, :] = grad.astype(out_ref.dtype)


def mine_kernel(own, txt_ref, scal_ref, *refs):
    *parts, w_ref, img_ref, keep_ref = refs
    temp = scal_ref[0:1, 0:1]
    at = 0
    for part in parts:
        rows = part.shape[0]
        img = part[...] if at == 0 else unit_rows(part[...])[0].astype(BF16)
        img_ref[at:at + rows, :] = img
        power = powers(img, txt_ref[...], scal_ref)
        w_ref[at:at + rows, :] = sigmoid_weights(power, temp)
        if at == 0:
            corner = power[:own, :2 * own]
            row = lax.broadcasted_iota(jnp.int32, corner.shape, 0)
            column = lax.broadcasted_iota(jnp.int32, corner.shape, 1)
            positive = row == column
            signed = jnp.where(positive, -corner, corner)
            w_ref[:own, :2 * own] = sigmoid_weights(signed, jnp.where(positive, -temp, temp))
        at += rows
    text_grads(w_ref, img_ref, keep_ref)


def theirs_kernel(txt_ref, scal_ref, img_ref, w_ref, send_ref):
    step = 256
    for at in range(0, img_ref.shape[0], step):
        power = powers(img_ref[at:at + step, :], txt_ref[...], scal_ref)
        w_ref[at:at + step, :] = sigmoid_weights(power, scal_ref[0:1, 0:1])
    text_grads(w_ref, img_ref, send_ref)


def image_kernel(w1_ref, w2_ref, txt1_ref, txt2_ref, *outs):
    at = 0
    for out in outs:
        rows = out.shape[0]
        grad = jnp.dot(w1_ref[at:at + rows, :], txt1_ref[...], preferred_element_type=F32)
        grad += jnp.dot(w2_ref[at:at + rows, :], txt2_ref[...], preferred_element_type=F32)
        out[...] = grad.astype(out.dtype)
        at += rows


def total_kernel(keep_ref, got_ref, own_ref, part13_ref, part2_ref, part4_ref):
    at = 0
    for out in (own_ref, part13_ref, part2_ref, part4_ref):
        rows = out.shape[0]
        total = keep_ref[at:at + rows, :].astype(F32) + got_ref[at:at + rows, :].astype(F32)
        out[...] = total.astype(out.dtype)
        at += rows


def middle_kernel(part2_ref, got13_ref, got4_ref, out_ref):
    rows = got4_ref.shape[0]
    total = part2_ref[...] + got13_ref[2 * rows:, :].astype(F32)
    out_ref[:rows, :] = (total[:rows] + got4_ref[...].astype(F32)).astype(BF16)
    out_ref[rows:, :] = total[rows:].astype(BF16)


def landed_kernel(own_ref, got13_ref, got2_ref, sum_ref, send_ref):
    rows = own_ref.shape[0]
    sum_ref[...] = own_ref[...] + got13_ref[:rows, :].astype(F32) + got2_ref[:rows, :].astype(F32)
    send_ref[...] = (got13_ref[rows:2 * rows, :].astype(F32) + got2_ref[rows:, :].astype(F32)).astype(BF16)


def sums_kernel(*refs):
    own_ref, *parts = refs[:4]
    outs = refs[4:]
    rows = outs[0].shape[0]
    for n, out in enumerate(outs):
        at = slice(n * rows, (n + 1) * rows)
        out[...] = (own_ref[at, :] + sum(p[at, :].astype(F32) for p in parts)).astype(out.dtype)


def final_kernel(*refs):
    *ins, img_ref, txt_ref = refs
    for (unit_ref, inv_ref, own_ref, *parts), out_ref in ((ins[:6], img_ref), (ins[6:], txt_ref)):
        grad = own_ref[...] + sum(p[...].astype(F32) for p in parts)
        out_ref[...] = back_norm(unit_ref[...], inv_ref[:, :1], grad)


def local(images, texts, log_temp, bias):
    own, dim = images.shape

    side = [shift(images, first(k), "gA%d" % k) for k in (1, 2, 3)]
    line2 = shift(texts, line(2), "gZ2")
    cross2 = shift(texts, cross(2), "gX2")
    swapped = shift(texts, other, "gC")
    img_own, img_unit, inv_img, txt_own, txt_unit, inv_txt = own_rows(images, texts, swapped)
    group = stack([img_own, *side], [token(line2, cross2)])
    send13 = stack([txt_own, swapped, line2, cross2])
    far = [shift(group, second(k), "gB%d" % k) for k in (1, 2, 3)]
    near13 = shift(send13, line(1), "gZ13")
    near4 = shift(line2, line(2), "gZ4")
    first_token = token(near13)
    (scalars,) = call(
        scalar_kernel, [((8, 128), F32)], [log_temp.reshape(1, 1), bias.reshape(1, 1)], [near13]
    )
    group = rounded([group], [scalars])
    mine = rounded([txt_own, near13, line2, cross2, near4], [group, first_token, *far])
    theirs = shift(mine, other, "gS")

    half = mine.shape[0]
    rows = group.shape[0] * (1 + len(far))
    flops = 2 * rows * half * dim
    w_mine, img_all, keep = call(
        lambda *refs: mine_kernel(own, *refs), [((rows, half), BF16), ((rows, dim), BF16), ((half, dim), BF16)],
        [mine, scalars, group, *far], flops=2 * flops, limit=24,
    )
    w_theirs, send = call(
        theirs_kernel, [((rows, half), BF16), ((half, dim), BF16)],
        [theirs, scalars, img_all], ties=[keep], flops=2 * flops, limit=24,
    )
    grads = call(
        image_kernel, [(group.shape, F32)] + [(group.shape, BF16)] * len(far),
        [w_mine, w_theirs, mine, theirs], flops=2 * flops, limit=24,
    )

    total_own, part13, part2, part4 = call(
        total_kernel,
        [((own, dim), F32), ((4 * own, dim), BF16), ((2 * own, dim), F32), ((own, dim), BF16)],
        [keep, shift(send, other, "rC")], ties=[grads[-1]],
    )
    got13 = shift(part13, line(-1), "rZ13")
    got4 = shift(part4, line(-2), "rZ4")
    (middle,) = call(middle_kernel, [((2 * own, dim), BF16)], [part2, got13, got4], [token(got13)])
    got2 = shift(middle, line(-2), "rZ2")
    txt_sum, txt_send = call(landed_kernel, [((own, dim), F32), ((own, dim), BF16)], [total_own, got13, got2])
    txt_last = shift(txt_send, other, "rS")

    back = [shift(g, second(-k), "rB%d" % k) for k, g in zip((1, 2, 3), grads[1:])]
    img_sum, *parts = call(
        sums_kernel, [((own, dim), F32)] + [((own, dim), BF16)] * 3, [grads[0], *back], ties=[token(middle)]
    )
    last = [shift(p, first(-k), "rA%d" % k) for k, p in zip((1, 2, 3), parts)]

    return call(
        final_kernel, [((own, dim), F32)] * 2,
        [img_unit, inv_img, img_sum, *last, txt_unit, inv_txt, txt_sum, txt_last],
    )


def solution(mesh):
    in_specs = (P(("row", "col"), None), P(("row", "col"), None), P(), P())
    out_specs = (P(("row", "col"), None), P(("row", "col"), None))
    return jax.shard_map(local, mesh=mesh, in_specs=in_specs, out_specs=out_specs, check_vma=False)
```

```python
import jax
import jax.numpy as jnp
from jax import lax
from jax.experimental import pallas as pl
from jax.experimental.pallas import tpu as pltpu
from jax.sharding import PartitionSpec as P

AXES = ("row", "col")
F32 = jnp.float32
BF16 = jnp.bfloat16
LOG2E = 1.4426950408889634
SIZE_X, SIZE_Y, SIZE_Z, CORES = 4, 4, 8, 2


def device(x, y, z, c):
    return ((z // 4) * 16 + x * 4 + y) * 8 + (z % 4) * 2 + c


def shift(values, move, name="move"):
    pairs = []
    for x in range(SIZE_X):
        for y in range(SIZE_Y):
            for z in range(SIZE_Z):
                for c in range(CORES):
                    nx, ny, nz, nc = move(x, y, z, c)
                    pairs.append((device(x, y, z, c), device(nx % SIZE_X, ny % SIZE_Y, nz % SIZE_Z, nc)))
    with jax.named_scope(name):
        return lax.ppermute(values, AXES, pairs)


def first(k):
    return lambda x, y, z, c: (x + k, y, z, c) if c == 0 else (x, y + k, z, c)


def second(k):
    return lambda x, y, z, c: (x, y + k, z, c) if c == 0 else (x + k, y, z, c)


def line(k):
    return lambda x, y, z, c: (x, y, z + k, c) if c == 0 else (x, y, z - k, c)


def straight(k):
    return lambda x, y, z, c: (x, y, z + k, c)


def other(x, y, z, c):
    return (x, y, z, 1 - c)


def call(kernel, outs, arrays, ties=(), flops=0, limit=8):
    vmem = pl.BlockSpec(memory_space=pltpu.VMEM)
    n_in = len(arrays)
    return pl.pallas_call(
        lambda *refs: kernel(*refs[:n_in], *refs[n_in + len(ties):]),
        out_shape=tuple(jax.ShapeDtypeStruct(shape, dtype) for shape, dtype in outs),
        in_specs=[vmem] * n_in + [pl.BlockSpec(memory_space=pl.ANY)] * len(ties),
        out_specs=tuple([vmem] * len(outs)),
        compiler_params=pltpu.CompilerParams(vmem_limit_bytes=limit * 1024 * 1024),
        cost_estimate=pl.CostEstimate(flops=flops, bytes_accessed=1024, transcendentals=0),
    )(*arrays, *ties)


def token_kernel(token_ref):
    token_ref[...] = jnp.zeros_like(token_ref)


def token(*values):
    return call(token_kernel, [((8, 128), F32)], [], ties=values, flops=40_000_000_000, limit=1)[0]


def unit_rows(raw):
    values = raw.astype(F32)
    inverse = lax.rsqrt(jnp.sum(values * values, axis=1, keepdims=True) + 1e-06)
    return values * inverse, inverse


def back_norm(unit, inverse, grad_unit):
    along = jnp.sum(unit * grad_unit, axis=1, keepdims=True)
    return (grad_unit - unit * along) * inverse


def own_kernel(img_hbm, txt_hbm, *refs):
    *outs, sems = refs
    pairs = ((img_hbm, outs[0]), (txt_hbm, outs[3]))
    copies = [pltpu.make_async_copy(src, dst, sems.at[n]) for n, (src, dst) in enumerate(pairs)]
    for copy in copies:
        copy.start()
    for copy in copies:
        copy.wait()
    for raw_ref, unit_ref, inv_ref in (outs[:3], outs[3:]):
        unit, inverse = unit_rows(raw_ref[...])
        unit_ref[...] = unit
        inv_ref[...] = jnp.broadcast_to(inverse, inv_ref.shape)


def own_rows(images, texts):
    own, dim = images.shape
    outs = [((own, dim), BF16), ((own, dim), F32), ((own, 128), F32)] * 2
    return pl.pallas_call(
        own_kernel,
        out_shape=tuple(jax.ShapeDtypeStruct(shape, dtype) for shape, dtype in outs),
        in_specs=[pl.BlockSpec(memory_space=pl.ANY)] * 2,
        out_specs=tuple([pl.BlockSpec(memory_space=pltpu.VMEM)] * len(outs)),
        scratch_shapes=[pltpu.SemaphoreType.DMA((2,))],
        compiler_params=pltpu.CompilerParams(vmem_limit_bytes=8 * 1024 * 1024),
        cost_estimate=pl.CostEstimate(flops=0, bytes_accessed=1024, transcendentals=0),
    )(images, texts)


def stack_kernel(*refs):
    *parts, out_ref = refs
    at = 0
    for part in parts:
        rows = part.shape[0]
        out_ref[at:at + rows, :] = part[...]
        at += rows


def stack(parts, ties=()):
    rows, dim = sum(p.shape[0] for p in parts), parts[0].shape[1]
    return call(stack_kernel, [((rows, dim), BF16)], parts, ties=ties)[0]


def round_kernel(step, *refs):
    *parts, out_ref = refs
    base = 0
    for part in parts:
        for at in range(0, part.shape[0], step):
            out_ref[base:base + step, :] = unit_rows(part[at:at + step, :])[0].astype(BF16)
            base += step


def rounded(parts, ties=()):
    rows, dim = sum(p.shape[0] for p in parts), parts[0].shape[1]
    return call(lambda *refs: round_kernel(64, *refs), [((rows, dim), BF16)], parts, ties=ties)[0]


def scalar_kernel(log_ref, bias_ref, scal_ref):
    temp = jnp.exp(jnp.broadcast_to(log_ref[...], (1, 128)))
    scal_ref[...] = jnp.zeros_like(scal_ref)
    scal_ref[0:1, :] = temp
    scal_ref[1:2, :] = -LOG2E * temp
    scal_ref[2:3, :] = jnp.broadcast_to(-LOG2E * bias_ref[...], (1, 128))


def sigmoid_weights(power, scale):
    return (scale / (1.0 + jnp.exp2(power))).astype(BF16)


def powers(img, txt, scal_ref):
    slope, offset = scal_ref[1:2, 0:1], scal_ref[2:3, 0:1]
    dots = lax.dot_general(img, txt, (((1,), (1,)), ((), ())), preferred_element_type=F32)
    return dots * slope + offset


def text_grads(w_ref, img_ref, places):
    step, rows = 256, w_ref.shape[1] // len(places)
    for t in range(0, w_ref.shape[1], step):
        grad = lax.dot_general(
            w_ref[:, t:t + step], img_ref[...], (((0,), (0,)), ((), ())), preferred_element_type=F32
        ).astype(BF16)
        for n in range(step // rows):
            out_ref, at = places[t // rows + n]
            out_ref[at:at + rows, :] = grad[n * rows:(n + 1) * rows]


def mine_kernel(own, txt_ref, scal_ref, *refs):
    *parts, w_ref, img_ref, keep_ref, send_ref = refs
    temp = scal_ref[0:1, 0:1]
    at = 0
    for part in parts:
        rows = part.shape[0]
        img = part[...] if at == 0 else unit_rows(part[...])[0].astype(BF16)
        img_ref[at:at + rows, :] = img
        power = powers(img, txt_ref[...], scal_ref)
        w_ref[at:at + rows, :] = sigmoid_weights(power, temp)
        if at == 0:
            corner = power[:own, :2 * own]
            row = lax.broadcasted_iota(jnp.int32, corner.shape, 0)
            column = lax.broadcasted_iota(jnp.int32, corner.shape, 1)
            positive = row == column
            signed = jnp.where(positive, -corner, corner)
            w_ref[:own, :2 * own] = sigmoid_weights(signed, jnp.where(positive, -temp, temp))
        at += rows
    text_grads(w_ref, img_ref, [
        (keep_ref, 0), (keep_ref, 4 * own), (keep_ref, 3 * own), (send_ref, 2 * own),
        (keep_ref, own), (send_ref, own), (keep_ref, 2 * own), (send_ref, 0),
    ])


def theirs_kernel(own, txt_ref, scal_ref, img_ref, part_ref, w_ref, keep_ref, send_ref):
    step = 256
    for at in range(0, img_ref.shape[0], step):
        power = powers(img_ref[at:at + step, :], txt_ref[...], scal_ref)
        w_ref[at:at + step, :] = sigmoid_weights(power, scal_ref[0:1, 0:1])
    for n, at in enumerate((2, 4, 6)):
        send_ref[at * own:(at + 1) * own, :] = part_ref[n * own:(n + 1) * own, :]
    text_grads(w_ref, img_ref, [
        (send_ref, 0), (send_ref, 7 * own), (send_ref, 5 * own), (keep_ref, 2 * own),
        (send_ref, own), (keep_ref, own), (send_ref, 3 * own), (keep_ref, 0),
    ])


def image_kernel(w1_ref, w2_ref, txt1_ref, txt2_ref, *outs):
    at = 0
    for out in outs:
        rows = out.shape[0]
        grad = jnp.dot(w1_ref[at:at + rows, :], txt1_ref[...], preferred_element_type=F32)
        grad += jnp.dot(w2_ref[at:at + rows, :], txt2_ref[...], preferred_element_type=F32)
        out[...] = grad.astype(out.dtype)
        at += rows


def total_kernel(first_ref, second_ref, got_ref, own_ref, part13_ref, part2_ref, part4_ref):
    rows = own_ref.shape[0]
    places = [
        (first_ref, 0, own_ref, 0),
        (first_ref, 1, part13_ref, 0), (second_ref, 0, part13_ref, 1),
        (first_ref, 2, part13_ref, 2), (second_ref, 1, part13_ref, 3),
        (first_ref, 3, part2_ref, 0), (second_ref, 2, part2_ref, 1),
        (first_ref, 4, part4_ref, 0),
    ]
    for n, (in_ref, i, out_ref, o) in enumerate(places):
        total = in_ref[i * rows:(i + 1) * rows, :].astype(F32) + got_ref[n * rows:(n + 1) * rows, :].astype(F32)
        out_ref[o * rows:(o + 1) * rows, :] = total.astype(out_ref.dtype)


def middle_kernel(part2_ref, got13_ref, got4_ref, out_ref):
    rows = got4_ref.shape[0]
    total = part2_ref[...] + got13_ref[2 * rows:, :].astype(F32)
    out_ref[:rows, :] = (total[:rows] + got4_ref[...].astype(F32)).astype(BF16)
    out_ref[rows:, :] = total[rows:].astype(BF16)


def landed_kernel(own_ref, got13_ref, got2_ref, sum_ref, send_ref):
    rows = own_ref.shape[0]
    sum_ref[...] = own_ref[...] + got13_ref[:rows, :].astype(F32) + got2_ref[:rows, :].astype(F32)
    send_ref[...] = (got13_ref[rows:2 * rows, :].astype(F32) + got2_ref[rows:, :].astype(F32)).astype(BF16)


def sums_kernel(*refs):
    own_ref, *parts = refs[:4]
    outs = refs[4:]
    rows = outs[0].shape[0]
    for n, out in enumerate(outs):
        at = slice(n * rows, (n + 1) * rows)
        out[...] = (own_ref[at, :] + sum(p[at, :].astype(F32) for p in parts)).astype(out.dtype)


def final_kernel(*refs):
    *ins, img_ref, txt_ref = refs
    for (unit_ref, inv_ref, own_ref, *parts), out_ref in ((ins[:6], img_ref), (ins[6:], txt_ref)):
        grad = own_ref[...] + sum(p[...].astype(F32) for p in parts)
        out_ref[...] = back_norm(unit_ref[...], inv_ref[:, :1], grad)


def local(images, texts, log_temp, bias):
    own, dim = images.shape

    side = [shift(images, first(k), "gA%d" % k) for k in (1, 2, 3)]
    far4 = shift(texts, straight(4), "gZ4")
    img_own, img_unit, inv_img, txt_own, txt_unit, inv_txt = own_rows(images, texts)
    group = stack([img_own, *side], [token(far4)])
    far = [shift(group, second(k), "gB%d" % k) for k in (2, 1, 3)]
    far2 = shift(stack([txt_own, far4]), line(2), "gZ2")
    far1 = shift(stack([txt_own, far4, far2], [token(far2)]), line(1), "gZ1")
    (scalars,) = call(
        scalar_kernel, [((8, 128), F32)], [log_temp.reshape(1, 1), bias.reshape(1, 1)], [far2]
    )
    group = rounded([group], [scalars])
    mine = rounded([txt_own, far4, far2, far1], [group, token(*far)])
    theirs = shift(mine, other, "gS")

    half = mine.shape[0]
    rows = group.shape[0] * (1 + len(far))
    flops = 2 * rows * half * dim
    w_mine, img_all, keep1, send1 = call(
        lambda *refs: mine_kernel(own, *refs),
        [((rows, half), BF16), ((rows, dim), BF16), ((5 * own, dim), BF16), ((3 * own, dim), BF16)],
        [mine, scalars, group, *far], flops=2 * flops, limit=24,
    )
    w_theirs, keep2, send = call(
        lambda *refs: theirs_kernel(own, *refs),
        [((rows, half), BF16), ((3 * own, dim), BF16), ((half, dim), BF16)],
        [theirs, scalars, img_all, send1], flops=2 * flops, limit=24,
    )
    grads = call(
        image_kernel, [(group.shape, F32)] + [(group.shape, BF16)] * len(far),
        [w_mine, w_theirs, mine, theirs], flops=2 * flops, limit=24,
    )

    total_own, part13, part2, part4 = call(
        total_kernel,
        [((own, dim), F32), ((4 * own, dim), BF16), ((2 * own, dim), F32), ((own, dim), BF16)],
        [keep1, keep2, shift(send, other, "rC")], ties=[grads[-1]],
    )
    got13 = shift(part13, line(-1), "rZ13")
    got4 = shift(part4, line(-2), "rZ4")
    (middle,) = call(middle_kernel, [((2 * own, dim), BF16)], [part2, got13, got4], [token(got13)])
    got2 = shift(middle, line(-2), "rZ2")
    txt_sum, txt_send = call(landed_kernel, [((own, dim), F32), ((own, dim), BF16)], [total_own, got13, got2])
    txt_last = shift(txt_send, other, "rS")

    back = [shift(g, second(-k), "rB%d" % k) for k, g in ((1, grads[2]), (2, grads[1]), (3, grads[3]))]
    img_sum, *parts = call(
        sums_kernel, [((own, dim), F32)] + [((own, dim), BF16)] * 3, [grads[0], *back], ties=[token(middle)]
    )
    last = [shift(p, first(-k), "rA%d" % k) for k, p in zip((1, 2, 3), parts)]

    return call(
        final_kernel, [((own, dim), F32)] * 2,
        [img_unit, inv_img, img_sum, *last, txt_unit, inv_txt, txt_sum, txt_last],
    )


def solution(mesh):
    in_specs = (P(("row", "col"), None), P(("row", "col"), None), P(), P())
    out_specs = (P(("row", "col"), None), P(("row", "col"), None))
    return jax.shard_map(local, mesh=mesh, in_specs=in_specs, out_specs=out_specs, check_vma=False)
```

```python
import jax
import jax.numpy as jnp
from jax import lax
from jax.experimental import pallas as pl
from jax.experimental.pallas import tpu as pltpu
from jax.sharding import PartitionSpec as P

AXES = ("row", "col")
F32 = jnp.float32
BF16 = jnp.bfloat16
LOG2E = 1.4426950408889634
SIZE_X, SIZE_Y, SIZE_Z, CORES = 4, 4, 8, 2


def device(x, y, z, c):
    return ((z // 4) * 16 + x * 4 + y) * 8 + (z % 4) * 2 + c


def shift(values, move, name="move"):
    pairs = []
    for x in range(SIZE_X):
        for y in range(SIZE_Y):
            for z in range(SIZE_Z):
                for c in range(CORES):
                    nx, ny, nz, nc = move(x, y, z, c)
                    pairs.append((device(x, y, z, c), device(nx % SIZE_X, ny % SIZE_Y, nz % SIZE_Z, nc)))
    with jax.named_scope(name):
        return lax.ppermute(values, AXES, pairs)


def first(k):
    return lambda x, y, z, c: (x + k, y, z, c) if c == 0 else (x, y + k, z, c)


def second(k):
    return lambda x, y, z, c: (x, y + k, z, c) if c == 0 else (x + k, y, z, c)


def line(k):
    return lambda x, y, z, c: (x, y, z + k, c) if c == 0 else (x, y, z - k, c)


def cross(k):
    return lambda x, y, z, c: (x, y, z + k, 0) if c == 1 else (x, y, z - k, 1)


def other(x, y, z, c):
    return (x, y, z, 1 - c)


def call(kernel, outs, arrays, ties=(), flops=0, limit=8):
    vmem = pl.BlockSpec(memory_space=pltpu.VMEM)
    n_in = len(arrays)
    return pl.pallas_call(
        lambda *refs: kernel(*refs[:n_in], *refs[n_in + len(ties):]),
        out_shape=tuple(jax.ShapeDtypeStruct(shape, dtype) for shape, dtype in outs),
        in_specs=[vmem] * n_in + [pl.BlockSpec(memory_space=pl.ANY)] * len(ties),
        out_specs=tuple([vmem] * len(outs)),
        compiler_params=pltpu.CompilerParams(vmem_limit_bytes=limit * 1024 * 1024),
        cost_estimate=pl.CostEstimate(flops=flops, bytes_accessed=1024, transcendentals=0),
    )(*arrays, *ties)


def token_kernel(token_ref):
    token_ref[...] = jnp.zeros_like(token_ref)


def token(*values):
    return call(token_kernel, [((8, 128), F32)], [], ties=values, flops=40_000_000_000, limit=1)[0]


def unit_rows(raw):
    values = raw.astype(F32)
    inverse = lax.rsqrt(jnp.sum(values * values, axis=1, keepdims=True) + 1e-06)
    return values * inverse, inverse


def back_norm(unit, inverse, grad_unit):
    along = jnp.sum(unit * grad_unit, axis=1, keepdims=True)
    return (grad_unit - unit * along) * inverse


def own_kernel(img_hbm, txt_hbm, *refs):
    *outs, sems = refs
    pairs = ((img_hbm, outs[0]), (txt_hbm, outs[3]))
    copies = [pltpu.make_async_copy(src, dst, sems.at[n]) for n, (src, dst) in enumerate(pairs)]
    for copy in copies:
        copy.start()
    for copy in copies:
        copy.wait()
    for raw_ref, unit_ref, inv_ref in (outs[:3], outs[3:]):
        unit, inverse = unit_rows(raw_ref[...])
        unit_ref[...] = unit
        inv_ref[...] = jnp.broadcast_to(inverse, inv_ref.shape)


def own_rows(images, texts, tie):
    own, dim = images.shape
    outs = [((own, dim), BF16), ((own, dim), F32), ((own, 128), F32)] * 2
    return pl.pallas_call(
        lambda tie_ref, *refs: own_kernel(*refs),
        out_shape=tuple(jax.ShapeDtypeStruct(shape, dtype) for shape, dtype in outs),
        in_specs=[pl.BlockSpec(memory_space=pl.ANY)] * 3,
        out_specs=tuple([pl.BlockSpec(memory_space=pltpu.VMEM)] * len(outs)),
        scratch_shapes=[pltpu.SemaphoreType.DMA((2,))],
        compiler_params=pltpu.CompilerParams(vmem_limit_bytes=8 * 1024 * 1024),
        cost_estimate=pl.CostEstimate(flops=0, bytes_accessed=1024, transcendentals=0),
    )(tie, images, texts)


def stack_kernel(*refs):
    *parts, out_ref = refs
    at = 0
    for part in parts:
        rows = part.shape[0]
        out_ref[at:at + rows, :] = part[...]
        at += rows


def stack(parts, ties=()):
    rows, dim = sum(p.shape[0] for p in parts), parts[0].shape[1]
    return call(stack_kernel, [((rows, dim), BF16)], parts, ties=ties)[0]


def round_kernel(step, *refs):
    *parts, out_ref = refs
    base = 0
    for part in parts:
        for at in range(0, part.shape[0], step):
            out_ref[base:base + step, :] = unit_rows(part[at:at + step, :])[0].astype(BF16)
            base += step


def rounded(parts, ties=()):
    rows, dim = sum(p.shape[0] for p in parts), parts[0].shape[1]
    return call(lambda *refs: round_kernel(64, *refs), [((rows, dim), BF16)], parts, ties=ties)[0]


def scalar_kernel(log_ref, bias_ref, scal_ref):
    temp = jnp.exp(jnp.broadcast_to(log_ref[...], (1, 128)))
    scal_ref[...] = jnp.zeros_like(scal_ref)
    scal_ref[0:1, :] = temp
    scal_ref[1:2, :] = -LOG2E * temp
    scal_ref[2:3, :] = jnp.broadcast_to(-LOG2E * bias_ref[...], (1, 128))


def sigmoid_weights(power, scale):
    return (scale / (1.0 + jnp.exp2(power))).astype(BF16)


def powers(img, txt, scal_ref):
    slope, offset = scal_ref[1:2, 0:1], scal_ref[2:3, 0:1]
    dots = lax.dot_general(img, txt, (((1,), (1,)), ((), ())), preferred_element_type=F32)
    return dots * slope + offset


def text_grads(w_ref, img_ref, out_ref):
    step = 256
    for t in range(0, out_ref.shape[0], step):
        grad = lax.dot_general(
            w_ref[:, t:t + step], img_ref[...], (((0,), (0,)), ((), ())), preferred_element_type=F32
        )
        out_ref[t:t + step, :] = grad.astype(out_ref.dtype)


def mine_kernel(own, txt_ref, scal_ref, *refs):
    *parts, w_ref, img_ref, keep_ref = refs
    temp = scal_ref[0:1, 0:1]
    at = 0
    for part in parts:
        rows = part.shape[0]
        img = part[...] if at == 0 else unit_rows(part[...])[0].astype(BF16)
        img_ref[at:at + rows, :] = img
        power = powers(img, txt_ref[...], scal_ref)
        w_ref[at:at + rows, :] = sigmoid_weights(power, temp)
        if at == 0:
            corner = power[:own, :2 * own]
            row = lax.broadcasted_iota(jnp.int32, corner.shape, 0)
            column = lax.broadcasted_iota(jnp.int32, corner.shape, 1)
            positive = row == column
            signed = jnp.where(positive, -corner, corner)
            w_ref[:own, :2 * own] = sigmoid_weights(signed, jnp.where(positive, -temp, temp))
        at += rows
    text_grads(w_ref, img_ref, keep_ref)


def theirs_kernel(txt_ref, scal_ref, img_ref, w_ref, send_ref):
    step = 256
    for at in range(0, img_ref.shape[0], step):
        power = powers(img_ref[at:at + step, :], txt_ref[...], scal_ref)
        w_ref[at:at + step, :] = sigmoid_weights(power, scal_ref[0:1, 0:1])
    text_grads(w_ref, img_ref, send_ref)


def image_kernel(w1_ref, w2_ref, txt1_ref, txt2_ref, *outs):
    at = 0
    for out in outs:
        rows = out.shape[0]
        grad = jnp.dot(w1_ref[at:at + rows, :], txt1_ref[...], preferred_element_type=F32)
        grad += jnp.dot(w2_ref[at:at + rows, :], txt2_ref[...], preferred_element_type=F32)
        out[...] = grad.astype(out.dtype)
        at += rows


def total_kernel(keep_ref, got_ref, own_ref, part13_ref, part2_ref, part4_ref):
    at = 0
    for out in (own_ref, part13_ref, part2_ref, part4_ref):
        rows = out.shape[0]
        total = keep_ref[at:at + rows, :].astype(F32) + got_ref[at:at + rows, :].astype(F32)
        out[...] = total.astype(out.dtype)
        at += rows


def middle_kernel(part2_ref, got13_ref, got4_ref, out_ref):
    rows = got4_ref.shape[0]
    total = part2_ref[...] + got13_ref[2 * rows:, :].astype(F32)
    out_ref[:rows, :] = (total[:rows] + got4_ref[...].astype(F32)).astype(BF16)
    out_ref[rows:, :] = total[rows:].astype(BF16)


def landed_kernel(own_ref, got13_ref, got2_ref, sum_ref, send_ref):
    rows = own_ref.shape[0]
    sum_ref[...] = own_ref[...] + got13_ref[:rows, :].astype(F32) + got2_ref[:rows, :].astype(F32)
    send_ref[...] = (got13_ref[rows:2 * rows, :].astype(F32) + got2_ref[rows:, :].astype(F32)).astype(BF16)


def sums_kernel(*refs):
    own_ref, *parts = refs[:4]
    outs = refs[4:]
    rows = outs[0].shape[0]
    for n, out in enumerate(outs):
        at = slice(n * rows, (n + 1) * rows)
        out[...] = (own_ref[at, :] + sum(p[at, :].astype(F32) for p in parts)).astype(out.dtype)


def final_kernel(*refs):
    *ins, img_ref, txt_ref = refs
    for (unit_ref, inv_ref, own_ref, *parts), out_ref in ((ins[:6], img_ref), (ins[6:], txt_ref)):
        grad = own_ref[...] + sum(p[...].astype(F32) for p in parts)
        out_ref[...] = back_norm(unit_ref[...], inv_ref[:, :1], grad)


def local(images, texts, log_temp, bias):
    own, dim = images.shape

    side = [shift(images, first(k), "gA%d" % k) for k in (1, 2, 3)]
    line2 = shift(texts, line(2), "gZ2")
    cross2 = shift(texts, cross(2), "gX2")
    swapped = shift(texts, other, "gC")
    img_own, img_unit, inv_img, txt_own, txt_unit, inv_txt = own_rows(images, texts, swapped)
    group = stack([img_own, *side], [])
    send13 = stack([txt_own, swapped, line2, cross2], [])
    far = [shift(group, second(k), "gB%d" % k) for k in (2, 1, 3)]
    near13 = shift(send13, line(1), "gZ13")
    near4 = shift(line2, line(2), "gZ4")
    first_token = token(group)
    (scalars,) = call(
        scalar_kernel, [((8, 128), F32)], [log_temp.reshape(1, 1), bias.reshape(1, 1)], [near13]
    )
    group = rounded([group], [scalars])
    mine = rounded([txt_own, near13, line2, cross2, near4], [group, first_token, *far])
    theirs = shift(mine, other, "gS")

    half = mine.shape[0]
    rows = group.shape[0] * (1 + len(far))
    flops = 2 * rows * half * dim
    w_mine, img_all, keep = call(
        lambda *refs: mine_kernel(own, *refs), [((rows, half), BF16), ((rows, dim), BF16), ((half, dim), BF16)],
        [mine, scalars, group, *far], flops=2 * flops, limit=24,
    )
    w_theirs, send = call(
        theirs_kernel, [((rows, half), BF16), ((half, dim), BF16)],
        [theirs, scalars, img_all], ties=[keep], flops=2 * flops, limit=24,
    )
    grads = call(
        image_kernel, [(group.shape, F32)] + [(group.shape, BF16)] * len(far),
        [w_mine, w_theirs, mine, theirs], flops=2 * flops, limit=24,
    )

    total_own, part13, part2, part4 = call(
        total_kernel,
        [((own, dim), F32), ((4 * own, dim), BF16), ((2 * own, dim), F32), ((own, dim), BF16)],
        [keep, shift(send, other, "rC")], ties=[grads[-1]],
    )
    got13 = shift(part13, line(-1), "rZ13")
    got4 = shift(part4, line(-2), "rZ4")
    (middle,) = call(middle_kernel, [((2 * own, dim), BF16)], [part2, got13, got4], [token(got13)])
    got2 = shift(middle, line(-2), "rZ2")
    txt_sum, txt_send = call(landed_kernel, [((own, dim), F32), ((own, dim), BF16)], [total_own, got13, got2])
    txt_last = shift(txt_send, other, "rS")

    back = [shift(g, second(-k), "rB%d" % k) for k, g in ((1, grads[2]), (2, grads[1]), (3, grads[3]))]
    img_sum, *parts = call(
        sums_kernel, [((own, dim), F32)] + [((own, dim), BF16)] * 3, [grads[0], *back], ties=[token(middle)]
    )
    last = [shift(p, first(-k), "rA%d" % k) for k, p in zip((1, 2, 3), parts)]

    return call(
        final_kernel, [((own, dim), F32)] * 2,
        [img_unit, inv_img, img_sum, *last, txt_unit, inv_txt, txt_sum, txt_last],
    )


def solution(mesh):
    in_specs = (P(("row", "col"), None), P(("row", "col"), None), P(), P())
    out_specs = (P(("row", "col"), None), P(("row", "col"), None))
    return jax.shard_map(local, mesh=mesh, in_specs=in_specs, out_specs=out_specs, check_vma=False)
```

```python
import jax
import jax.numpy as jnp
from jax import lax
from jax.experimental import pallas as pl
from jax.experimental.pallas import tpu as pltpu
from jax.sharding import PartitionSpec as P

AXES = ("row", "col")
F32 = jnp.float32
BF16 = jnp.bfloat16
LOG2E = 1.4426950408889634
SIZE_X, SIZE_Y, SIZE_Z, CORES = 4, 4, 8, 2


def device(x, y, z, c):
    return ((z // 4) * 16 + x * 4 + y) * 8 + (z % 4) * 2 + c


def shift(values, move, name="move"):
    pairs = []
    for x in range(SIZE_X):
        for y in range(SIZE_Y):
            for z in range(SIZE_Z):
                for c in range(CORES):
                    nx, ny, nz, nc = move(x, y, z, c)
                    pairs.append((device(x, y, z, c), device(nx % SIZE_X, ny % SIZE_Y, nz % SIZE_Z, nc)))
    with jax.named_scope(name):
        return lax.ppermute(values, AXES, pairs)


def first(k):
    return lambda x, y, z, c: (x + k, y, z, c) if c == 0 else (x, y + k, z, c)


def second(k):
    return lambda x, y, z, c: (x, y + k, z, c) if c == 0 else (x + k, y, z, c)


def line(k):
    return lambda x, y, z, c: (x, y, z + k, c) if c == 0 else (x, y, z - k, c)


def other(x, y, z, c):
    return (x, y, z, 1 - c)


def call(kernel, outs, arrays, ties=(), first=(), scratch=(), flops=0, limit=8):
    vmem = pl.BlockSpec(memory_space=pltpu.VMEM)
    anywhere = pl.BlockSpec(memory_space=pl.ANY)
    n_in = len(first) + len(arrays)
    return pl.pallas_call(
        lambda *refs: kernel(*refs[:n_in], *refs[n_in + len(ties):]),
        out_shape=tuple(jax.ShapeDtypeStruct(shape, dtype) for shape, dtype in outs),
        in_specs=[anywhere] * len(first) + [vmem] * len(arrays) + [anywhere] * len(ties),
        out_specs=tuple([vmem] * len(outs)),
        scratch_shapes=list(scratch),
        compiler_params=pltpu.CompilerParams(vmem_limit_bytes=limit * 1024 * 1024),
        cost_estimate=pl.CostEstimate(flops=flops, bytes_accessed=1024, transcendentals=0),
    )(*first, *arrays, *ties)


def token_kernel(token_ref):
    token_ref[...] = jnp.zeros_like(token_ref)


def token(*values):
    return call(token_kernel, [((8, 128), F32)], [], ties=values, flops=40_000_000_000, limit=1)[0]


def unit_rows(raw):
    values = raw.astype(F32)
    inverse = lax.rsqrt(jnp.sum(values * values, axis=1, keepdims=True) + 1e-06)
    return values * inverse, inverse


def back_norm(unit, inverse, grad_unit):
    along = jnp.sum(unit * grad_unit, axis=1, keepdims=True)
    return (grad_unit - unit * along) * inverse


def stack_kernel(own_hbm, *refs):
    *parts, out_ref, sem = refs
    rows = own_hbm.shape[0]
    copy = pltpu.make_async_copy(own_hbm, out_ref.at[pl.ds(0, rows)], sem)
    copy.start()
    at = rows
    for part in parts:
        rows = part.shape[0]
        out_ref[at:at + rows, :] = part[...]
        at += rows
    copy.wait()


def stack(own_raw, parts, ties=()):
    rows, dim = own_raw.shape
    rows += sum(p.shape[0] for p in parts)
    return call(
        stack_kernel, [((rows, dim), BF16)], parts, ties=ties, first=[own_raw], scratch=[pltpu.SemaphoreType.DMA(())]
    )[0]


def head_kernel(in_ref, out_ref):
    out_ref[...] = in_ref[...]


def send_kernel(pair_ref, near_ref, send13_ref, send4_ref):
    rows = pair_ref.shape[0]
    send13_ref[:rows, :] = pair_ref[...]
    send13_ref[rows:, :] = near_ref[...]
    send4_ref[...] = near_ref[:send4_ref.shape[0], :]


def round_rows(raw_ref, start, out_ref, at, rows, own=None):
    step = 64
    for n in range(0, rows, step):
        unit, inverse = unit_rows(raw_ref[start + n:start + n + step, :])
        out_ref[at + n:at + n + step, :] = unit.astype(BF16)
        if own is not None and n == 0:
            own[0][...] = unit
            own[1][...] = jnp.broadcast_to(inverse, own[1].shape)


def group_round_kernel(raw_ref, out_ref, unit_ref, inv_ref):
    round_rows(raw_ref, 0, out_ref, 0, raw_ref.shape[0], (unit_ref, inv_ref))


def early_round_kernel(raw_ref, out_ref, unit_ref, inv_ref):
    own = unit_ref.shape[0]
    round_rows(raw_ref, 0, out_ref, 0, own, (unit_ref, inv_ref))
    round_rows(raw_ref, 2 * own, out_ref, own, 2 * own)


def mine_round_kernel(early_ref, near13_ref, near4_ref, out_ref):
    own = near4_ref.shape[0]
    out_ref[:own, :] = early_ref[:own, :]
    round_rows(near13_ref, 0, out_ref, own, 4 * own)
    out_ref[5 * own:7 * own, :] = early_ref[own:, :]
    round_rows(near4_ref, 0, out_ref, 7 * own, own)


def scalar_kernel(log_ref, bias_ref, scal_ref):
    temp = jnp.exp(jnp.broadcast_to(log_ref[...], (1, 128)))
    scal_ref[...] = jnp.zeros_like(scal_ref)
    scal_ref[0:1, :] = temp
    scal_ref[1:2, :] = -LOG2E * temp
    scal_ref[2:3, :] = jnp.broadcast_to(-LOG2E * bias_ref[...], (1, 128))


def sigmoid_weights(power, scale):
    return (scale / (1.0 + jnp.exp2(power))).astype(BF16)


def powers(img, txt, scal_ref):
    slope, offset = scal_ref[1:2, 0:1], scal_ref[2:3, 0:1]
    dots = lax.dot_general(img, txt, (((1,), (1,)), ((), ())), preferred_element_type=F32)
    return dots * slope + offset


def text_grads(w_ref, img_ref, out_ref):
    step = 256
    for t in range(0, out_ref.shape[0], step):
        grad = lax.dot_general(
            w_ref[:, t:t + step], img_ref[...], (((0,), (0,)), ((), ())), preferred_element_type=F32
        )
        out_ref[t:t + step, :] = grad.astype(out_ref.dtype)


def mine_kernel(own, txt_ref, scal_ref, *refs):
    *parts, w_ref, img_ref, keep_ref = refs
    temp = scal_ref[0:1, 0:1]
    at = 0
    for part in parts:
        rows = part.shape[0]
        img = part[...] if at == 0 else unit_rows(part[...])[0].astype(BF16)
        img_ref[at:at + rows, :] = img
        power = powers(img, txt_ref[...], scal_ref)
        w_ref[at:at + rows, :] = sigmoid_weights(power, temp)
        if at == 0:
            corner = power[:own, :2 * own]
            row = lax.broadcasted_iota(jnp.int32, corner.shape, 0)
            column = lax.broadcasted_iota(jnp.int32, corner.shape, 1)
            positive = row == column
            signed = jnp.where(positive, -corner, corner)
            w_ref[:own, :2 * own] = sigmoid_weights(signed, jnp.where(positive, -temp, temp))
        at += rows
    text_grads(w_ref, img_ref, keep_ref)


def theirs_kernel(txt_ref, scal_ref, img_ref, w_ref, send_ref):
    step = 256
    for at in range(0, img_ref.shape[0], step):
        power = powers(img_ref[at:at + step, :], txt_ref[...], scal_ref)
        w_ref[at:at + step, :] = sigmoid_weights(power, scal_ref[0:1, 0:1])
    text_grads(w_ref, img_ref, send_ref)


def image_kernel(w1_ref, w2_ref, txt1_ref, txt2_ref, *outs):
    at = 0
    for out in outs:
        rows = out.shape[0]
        grad = jnp.dot(w1_ref[at:at + rows, :], txt1_ref[...], preferred_element_type=F32)
        grad += jnp.dot(w2_ref[at:at + rows, :], txt2_ref[...], preferred_element_type=F32)
        out[...] = grad.astype(out.dtype)
        at += rows


def total_kernel(keep_ref, got_ref, own_ref, part13_ref, part2_ref, part4_ref):
    at = 0
    for out in (own_ref, part13_ref, part2_ref, part4_ref):
        rows = out.shape[0]
        total = keep_ref[at:at + rows, :].astype(F32) + got_ref[at:at + rows, :].astype(F32)
        out[...] = total.astype(out.dtype)
        at += rows


def middle_kernel(part2_ref, got13_ref, got4_ref, out_ref):
    rows = got4_ref.shape[0]
    total = part2_ref[...] + got13_ref[2 * rows:, :].astype(F32)
    out_ref[:rows, :] = (total[:rows] + got4_ref[...].astype(F32)).astype(BF16)
    out_ref[rows:, :] = total[rows:].astype(BF16)


def landed_kernel(own_ref, got13_ref, got2_ref, sum_ref, send_ref):
    rows = own_ref.shape[0]
    sum_ref[...] = own_ref[...] + got13_ref[:rows, :].astype(F32) + got2_ref[:rows, :].astype(F32)
    send_ref[...] = (got13_ref[rows:2 * rows, :].astype(F32) + got2_ref[rows:, :].astype(F32)).astype(BF16)


def sums_kernel(*refs):
    own_ref, *parts = refs[:4]
    outs = refs[4:]
    rows = outs[0].shape[0]
    for n, out in enumerate(outs):
        at = slice(n * rows, (n + 1) * rows)
        out[...] = (own_ref[at, :] + sum(p[at, :].astype(F32) for p in parts)).astype(out.dtype)


def final_kernel(*refs):
    *ins, img_ref, txt_ref = refs
    for (unit_ref, inv_ref, own_ref, *parts), out_ref in ((ins[:6], img_ref), (ins[6:], txt_ref)):
        grad = own_ref[...] + sum(p[...].astype(F32) for p in parts)
        out_ref[...] = back_norm(unit_ref[...], inv_ref[:, :1], grad)


def local(images, texts, log_temp, bias):
    own, dim = images.shape

    swapped = shift(texts, other, "gC")
    side = [shift(images, first(k), "gA%d" % k) for k in (1, 2, 3)]
    pair = stack(texts, [swapped])
    near2 = shift(pair, line(2), "gZ2")
    group = stack(images, side, [token(pair)])
    send13, send4 = call(send_kernel, [((4 * own, dim), BF16), ((own, dim), BF16)], [pair, near2], [group])
    far = [shift(group, second(k), "gB%d" % k) for k in (2, 1, 3)]
    near13 = shift(send13, line(1), "gZ13")
    near4 = shift(call(head_kernel, [((own, dim), BF16)], [send4], [send13])[0], line(2), "gZ4")
    first_token = token(group)
    (scalars,) = call(
        scalar_kernel, [((8, 128), F32)], [log_temp.reshape(1, 1), bias.reshape(1, 1)], [near13]
    )
    per_row = [((own, dim), F32), ((own, 128), F32)]
    group, img_unit, inv_img = call(group_round_kernel, [(group.shape, BF16)] + per_row, [group], [scalars])
    early, txt_unit, inv_txt = call(early_round_kernel, [((3 * own, dim), BF16)] + per_row, [send13], [scalars])
    (mine,) = call(
        mine_round_kernel, [((8 * own, dim), BF16)], [early, near13, near4], [group, first_token, *far]
    )
    theirs = shift(mine, other, "gS")

    half = mine.shape[0]
    rows = group.shape[0] * (1 + len(far))
    flops = 2 * rows * half * dim
    w_mine, img_all, keep = call(
        lambda *refs: mine_kernel(own, *refs), [((rows, half), BF16), ((rows, dim), BF16), ((half, dim), BF16)],
        [mine, scalars, group, *far], flops=2 * flops, limit=24,
    )
    w_theirs, send = call(
        theirs_kernel, [((rows, half), BF16), ((half, dim), BF16)],
        [theirs, scalars, img_all], ties=[keep], flops=2 * flops, limit=24,
    )
    grads = call(
        image_kernel, [(group.shape, F32)] + [(group.shape, BF16)] * len(far),
        [w_mine, w_theirs, mine, theirs], flops=2 * flops, limit=24,
    )

    total_own, part13, part2, part4 = call(
        total_kernel,
        [((own, dim), F32), ((4 * own, dim), BF16), ((2 * own, dim), F32), ((own, dim), BF16)],
        [keep, shift(send, other, "rC")], ties=[grads[-1]],
    )
    got13 = shift(part13, line(-1), "rZ13")
    got4 = shift(part4, line(-2), "rZ4")
    (middle,) = call(middle_kernel, [((2 * own, dim), BF16)], [part2, got13, got4], [token(got13)])
    got2 = shift(middle, line(-2), "rZ2")
    txt_sum, txt_send = call(landed_kernel, [((own, dim), F32), ((own, dim), BF16)], [total_own, got13, got2])
    txt_last = shift(txt_send, other, "rS")

    back = [shift(g, second(-k), "rB%d" % k) for k, g in ((1, grads[2]), (2, grads[1]), (3, grads[3]))]
    img_sum, *parts = call(
        sums_kernel, [((own, dim), F32)] + [((own, dim), BF16)] * 3, [grads[0], *back], ties=[token(middle)]
    )
    last = [shift(p, first(-k), "rA%d" % k) for k, p in zip((1, 2, 3), parts)]

    return call(
        final_kernel, [((own, dim), F32)] * 2,
        [img_unit, inv_img, img_sum, *last, txt_unit, inv_txt, txt_sum, txt_last],
    )


def solution(mesh):
    in_specs = (P(("row", "col"), None), P(("row", "col"), None), P(), P())
    out_specs = (P(("row", "col"), None), P(("row", "col"), None))
    return jax.shard_map(local, mesh=mesh, in_specs=in_specs, out_specs=out_specs, check_vma=False)
```

```python
import jax
import jax.numpy as jnp
from jax import lax
from jax.experimental import pallas as pl
from jax.experimental.pallas import tpu as pltpu
from jax.sharding import PartitionSpec as P

AXES = ("row", "col")
F32 = jnp.float32
BF16 = jnp.bfloat16
LOG2E = 1.4426950408889634
SIZE_X, SIZE_Y, SIZE_Z, CORES = 4, 4, 8, 2


def device(x, y, z, c):
    return ((z // 4) * 16 + x * 4 + y) * 8 + (z % 4) * 2 + c


def shift(values, move, name="move"):
    pairs = []
    for x in range(SIZE_X):
        for y in range(SIZE_Y):
            for z in range(SIZE_Z):
                for c in range(CORES):
                    nx, ny, nz, nc = move(x, y, z, c)
                    pairs.append((device(x, y, z, c), device(nx % SIZE_X, ny % SIZE_Y, nz % SIZE_Z, nc)))
    with jax.named_scope(name):
        return lax.ppermute(values, AXES, pairs)


def first(k):
    return lambda x, y, z, c: (x + k, y, z, c) if c == 0 else (x, y + k, z, c)


def second(k):
    return lambda x, y, z, c: (x, y + k, z, c) if c == 0 else (x + k, y, z, c)


def line(k):
    return lambda x, y, z, c: (x, y, z + k, c) if c == 0 else (x, y, z - k, c)


def other(x, y, z, c):
    return (x, y, z, 1 - c)


def call(kernel, outs, arrays, ties=(), first=(), scratch=(), flops=0, limit=8):
    vmem = pl.BlockSpec(memory_space=pltpu.VMEM)
    anywhere = pl.BlockSpec(memory_space=pl.ANY)
    n_in = len(first) + len(arrays)
    return pl.pallas_call(
        lambda *refs: kernel(*refs[:n_in], *refs[n_in + len(ties):]),
        out_shape=tuple(jax.ShapeDtypeStruct(shape, dtype) for shape, dtype in outs),
        in_specs=[anywhere] * len(first) + [vmem] * len(arrays) + [anywhere] * len(ties),
        out_specs=tuple([vmem] * len(outs)),
        scratch_shapes=list(scratch),
        compiler_params=pltpu.CompilerParams(vmem_limit_bytes=limit * 1024 * 1024),
        cost_estimate=pl.CostEstimate(flops=flops, bytes_accessed=1024, transcendentals=0),
    )(*first, *arrays, *ties)


def token_kernel(token_ref):
    token_ref[...] = jnp.zeros_like(token_ref)


def token(*values):
    return call(token_kernel, [((8, 128), F32)], [], ties=values, flops=40_000_000_000, limit=1)[0]


def unit_rows(raw):
    values = raw.astype(F32)
    inverse = lax.rsqrt(jnp.sum(values * values, axis=1, keepdims=True) + 1e-06)
    return values * inverse, inverse


def back_norm(unit, inverse, grad_unit):
    along = jnp.sum(unit * grad_unit, axis=1, keepdims=True)
    return (grad_unit - unit * along) * inverse


def stack_kernel(own_hbm, *refs):
    *parts, out_ref, sem = refs
    rows = own_hbm.shape[0]
    copy = pltpu.make_async_copy(own_hbm, out_ref.at[pl.ds(0, rows)], sem)
    copy.start()
    at = rows
    for part in parts:
        rows = part.shape[0]
        out_ref[at:at + rows, :] = part[...]
        at += rows
    copy.wait()


def stack(own_raw, parts, ties=()):
    rows, dim = own_raw.shape
    rows += sum(p.shape[0] for p in parts)
    return call(
        stack_kernel, [((rows, dim), BF16)], parts, ties=ties, first=[own_raw], scratch=[pltpu.SemaphoreType.DMA(())]
    )[0]


def head_kernel(in_ref, out_ref):
    out_ref[...] = in_ref[...]


def send_kernel(pair_ref, near_ref, send13_ref, send4_ref):
    rows = pair_ref.shape[0]
    send13_ref[:rows, :] = pair_ref[...]
    send13_ref[rows:, :] = near_ref[...]
    send4_ref[...] = near_ref[:send4_ref.shape[0], :]


def round_rows(raw_ref, start, out_ref, at, rows, own=None):
    step = 64
    for n in range(0, rows, step):
        unit, inverse = unit_rows(raw_ref[start + n:start + n + step, :])
        out_ref[at + n:at + n + step, :] = unit.astype(BF16)
        if own is not None and n == 0:
            own[0][...] = unit
            own[1][...] = jnp.broadcast_to(inverse, own[1].shape)


def group_round_kernel(raw_ref, out_ref, unit_ref, inv_ref):
    round_rows(raw_ref, 0, out_ref, 0, raw_ref.shape[0], (unit_ref, inv_ref))


def early_round_kernel(raw_ref, out_ref, unit_ref, inv_ref):
    own = unit_ref.shape[0]
    round_rows(raw_ref, 0, out_ref, 0, own, (unit_ref, inv_ref))
    round_rows(raw_ref, 2 * own, out_ref, own, 2 * own)


def mine_round_kernel(early_ref, near13_ref, near4_ref, out_ref):
    own = near4_ref.shape[0]
    out_ref[:own, :] = early_ref[:own, :]
    round_rows(near13_ref, 0, out_ref, own, 4 * own)
    out_ref[5 * own:7 * own, :] = early_ref[own:, :]
    round_rows(near4_ref, 0, out_ref, 7 * own, own)


def scalar_kernel(log_ref, bias_ref, scal_ref):
    temp = jnp.exp(jnp.broadcast_to(log_ref[...], (1, 128)))
    scal_ref[...] = jnp.zeros_like(scal_ref)
    scal_ref[0:1, :] = temp
    scal_ref[1:2, :] = -LOG2E * temp
    scal_ref[2:3, :] = jnp.broadcast_to(-LOG2E * bias_ref[...], (1, 128))


def sigmoid_weights(power, scale):
    return (scale / (1.0 + jnp.exp2(power))).astype(BF16)


def powers(img, txt, scal_ref):
    slope, offset = scal_ref[1:2, 0:1], scal_ref[2:3, 0:1]
    dots = lax.dot_general(img, txt, (((1,), (1,)), ((), ())), preferred_element_type=F32)
    return dots * slope + offset


def text_grads(w_ref, img_ref, out_ref):
    step = 256
    for t in range(0, out_ref.shape[0], step):
        grad = lax.dot_general(
            w_ref[:, t:t + step], img_ref[...], (((0,), (0,)), ((), ())), preferred_element_type=F32
        )
        out_ref[t:t + step, :] = grad.astype(out_ref.dtype)


def mine_kernel(own, txt_ref, scal_ref, *refs):
    *parts, w_ref, img_ref, keep_ref = refs
    temp = scal_ref[0:1, 0:1]
    at = 0
    for part in parts:
        rows = part.shape[0]
        img = part[...] if at == 0 else unit_rows(part[...])[0].astype(BF16)
        img_ref[at:at + rows, :] = img
        power = powers(img, txt_ref[...], scal_ref)
        w_ref[at:at + rows, :] = sigmoid_weights(power, temp)
        if at == 0:
            corner = power[:own, :2 * own]
            row = lax.broadcasted_iota(jnp.int32, corner.shape, 0)
            column = lax.broadcasted_iota(jnp.int32, corner.shape, 1)
            positive = row == column
            signed = jnp.where(positive, -corner, corner)
            w_ref[:own, :2 * own] = sigmoid_weights(signed, jnp.where(positive, -temp, temp))
        at += rows
    text_grads(w_ref, img_ref, keep_ref)


def theirs_kernel(txt_ref, scal_ref, img_ref, w_ref, send_ref):
    step = 256
    for at in range(0, img_ref.shape[0], step):
        power = powers(img_ref[at:at + step, :], txt_ref[...], scal_ref)
        w_ref[at:at + step, :] = sigmoid_weights(power, scal_ref[0:1, 0:1])
    text_grads(w_ref, img_ref, send_ref)


def image_kernel(at, w1_ref, w2_ref, txt1_ref, txt2_ref, out_ref):
    rows = out_ref.shape[0]
    grad = jnp.dot(w1_ref[at:at + rows, :], txt1_ref[...], preferred_element_type=F32)
    grad += jnp.dot(w2_ref[at:at + rows, :], txt2_ref[...], preferred_element_type=F32)
    out_ref[...] = grad.astype(out_ref.dtype)


def total_kernel(keep_ref, got_ref, own_ref, part13_ref, part2_ref, part4_ref):
    at = 0
    for out in (own_ref, part13_ref, part2_ref, part4_ref):
        rows = out.shape[0]
        total = keep_ref[at:at + rows, :].astype(F32) + got_ref[at:at + rows, :].astype(F32)
        out[...] = total.astype(out.dtype)
        at += rows


def middle_kernel(part2_ref, got13_ref, got4_ref, out_ref):
    rows = got4_ref.shape[0]
    total = part2_ref[...] + got13_ref[2 * rows:, :].astype(F32)
    out_ref[:rows, :] = (total[:rows] + got4_ref[...].astype(F32)).astype(BF16)
    out_ref[rows:, :] = total[rows:].astype(BF16)


def landed_kernel(own_ref, got13_ref, got2_ref, sum_ref, send_ref):
    rows = own_ref.shape[0]
    sum_ref[...] = own_ref[...] + got13_ref[:rows, :].astype(F32) + got2_ref[:rows, :].astype(F32)
    send_ref[...] = (got13_ref[rows:2 * rows, :].astype(F32) + got2_ref[rows:, :].astype(F32)).astype(BF16)


def partial_kernel(own_ref, first_ref, second_ref, out_ref):
    out_ref[...] = own_ref[...] + first_ref[...].astype(F32) + second_ref[...].astype(F32)


def sums_kernel(sum_ref, last_ref, *outs):
    rows = outs[0].shape[0]
    for n, out in enumerate(outs):
        at = slice(n * rows, (n + 1) * rows)
        out[...] = (sum_ref[at, :] + last_ref[at, :].astype(F32)).astype(out.dtype)


def final_kernel(*refs):
    *ins, img_ref, txt_ref = refs
    for (unit_ref, inv_ref, own_ref, *parts), out_ref in ((ins[:6], img_ref), (ins[6:], txt_ref)):
        grad = own_ref[...] + sum(p[...].astype(F32) for p in parts)
        out_ref[...] = back_norm(unit_ref[...], inv_ref[:, :1], grad)


def local(images, texts, log_temp, bias):
    own, dim = images.shape

    swapped = shift(texts, other, "gC")
    side = [shift(images, first(k), "gA%d" % k) for k in (1, 2, 3)]
    pair = stack(texts, [swapped])
    near2 = shift(pair, line(2), "gZ2")
    group = stack(images, side, [token(pair)])
    send13, send4 = call(send_kernel, [((4 * own, dim), BF16), ((own, dim), BF16)], [pair, near2], [group])
    far = [shift(group, second(k), "gB%d" % k) for k in (1, 3, 2)]
    near13 = shift(send13, line(1), "gZ13")
    near4 = shift(call(head_kernel, [((own, dim), BF16)], [send4], [send13])[0], line(2), "gZ4")
    first_token = token(group)
    (scalars,) = call(
        scalar_kernel, [((8, 128), F32)], [log_temp.reshape(1, 1), bias.reshape(1, 1)], [near13]
    )
    per_row = [((own, dim), F32), ((own, 128), F32)]
    group, img_unit, inv_img = call(group_round_kernel, [(group.shape, BF16)] + per_row, [group], [scalars])
    early, txt_unit, inv_txt = call(early_round_kernel, [((3 * own, dim), BF16)] + per_row, [send13], [scalars])
    (mine,) = call(
        mine_round_kernel, [((8 * own, dim), BF16)], [early, near13, near4], [group, first_token, *far]
    )
    theirs = shift(mine, other, "gS")

    half = mine.shape[0]
    rows = group.shape[0] * (1 + len(far))
    flops = 2 * rows * half * dim
    w_mine, img_all, keep = call(
        lambda *refs: mine_kernel(own, *refs), [((rows, half), BF16), ((rows, dim), BF16), ((half, dim), BF16)],
        [mine, scalars, group, *far], flops=2 * flops, limit=24,
    )
    w_theirs, send = call(
        theirs_kernel, [((rows, half), BF16), ((half, dim), BF16)],
        [theirs, scalars, img_all], ties=[keep], flops=2 * flops, limit=24,
    )
    each = group.shape[0]

    def image_grads(index, dtype, ties):
        return call(
            lambda *refs: image_kernel(index * each, *refs), [((each, dim), dtype)],
            [w_mine, w_theirs, mine, theirs], ties=ties, flops=flops // 2, limit=24,
        )[0]

    grad3 = image_grads(2, BF16, [send])
    back3 = shift(grad3, second(-3), "rB3")
    grad1 = image_grads(1, BF16, [grad3])
    back1 = shift(grad1, second(-1), "rB1")

    total_own, part13, part2, part4 = call(
        total_kernel,
        [((own, dim), F32), ((4 * own, dim), BF16), ((2 * own, dim), F32), ((own, dim), BF16)],
        [keep, shift(send, other, "rC")], ties=[grad1],
    )
    grad2 = image_grads(3, BF16, [part13])
    back2 = shift(grad2, second(-2), "rB2")
    grad0 = image_grads(0, F32, [grad2])
    (partial,) = call(partial_kernel, [((each, dim), F32)], [grad0, back3, back1])
    got13 = shift(part13, line(-1), "rZ13")
    got4 = shift(part4, line(-2), "rZ4")
    (middle,) = call(middle_kernel, [((2 * own, dim), BF16)], [part2, got13, got4], [partial])
    got2 = shift(middle, line(-2), "rZ2")
    txt_sum, txt_send = call(landed_kernel, [((own, dim), F32), ((own, dim), BF16)], [total_own, got13, got2])
    txt_last = shift(txt_send, other, "rS")

    img_sum, *parts = call(
        sums_kernel, [((own, dim), F32)] + [((own, dim), BF16)] * 3, [partial, back2], ties=[token(middle)]
    )
    last = [shift(p, first(-k), "rA%d" % k) for k, p in zip((1, 2, 3), parts)]

    return call(
        final_kernel, [((own, dim), F32)] * 2,
        [img_unit, inv_img, img_sum, *last, txt_unit, inv_txt, txt_sum, txt_last],
    )


def solution(mesh):
    in_specs = (P(("row", "col"), None), P(("row", "col"), None), P(), P())
    out_specs = (P(("row", "col"), None), P(("row", "col"), None))
    return jax.shard_map(local, mesh=mesh, in_specs=in_specs, out_specs=out_specs, check_vma=False)
```

```python
import jax
import jax.numpy as jnp
from jax import lax
from jax.experimental import pallas as pl
from jax.experimental.pallas import tpu as pltpu
from jax.sharding import PartitionSpec as P

AXES = ("row", "col")
F32 = jnp.float32
BF16 = jnp.bfloat16
LOG2E = 1.4426950408889634
SIZE_X, SIZE_Y, SIZE_Z, CORES = 4, 4, 8, 2


def device(x, y, z, c):
    return ((z // 4) * 16 + x * 4 + y) * 8 + (z % 4) * 2 + c


def shift(values, move, name="move"):
    pairs = []
    for x in range(SIZE_X):
        for y in range(SIZE_Y):
            for z in range(SIZE_Z):
                for c in range(CORES):
                    nx, ny, nz, nc = move(x, y, z, c)
                    pairs.append((device(x, y, z, c), device(nx % SIZE_X, ny % SIZE_Y, nz % SIZE_Z, nc)))
    with jax.named_scope(name):
        return lax.ppermute(values, AXES, pairs)


def first(k):
    return lambda x, y, z, c: (x + k, y, z, c) if c == 0 else (x, y + k, z, c)


def second(k):
    return lambda x, y, z, c: (x, y + k, z, c) if c == 0 else (x + k, y, z, c)


def line(k):
    return lambda x, y, z, c: (x, y, z + k, c) if c == 0 else (x, y, z - k, c)


def cross(k):
    return lambda x, y, z, c: (x, y, z + k, 0) if c == 1 else (x, y, z - k, 1)


def other(x, y, z, c):
    return (x, y, z, 1 - c)


def call(kernel, outs, arrays, ties=(), first=(), scratch=(), flops=0, limit=8):
    vmem = pl.BlockSpec(memory_space=pltpu.VMEM)
    anywhere = pl.BlockSpec(memory_space=pl.ANY)
    n_in = len(first) + len(arrays)
    return pl.pallas_call(
        lambda *refs: kernel(*refs[:n_in], *refs[n_in + len(ties):]),
        out_shape=tuple(jax.ShapeDtypeStruct(shape, dtype) for shape, dtype in outs),
        in_specs=[anywhere] * len(first) + [vmem] * len(arrays) + [anywhere] * len(ties),
        out_specs=tuple([vmem] * len(outs)),
        scratch_shapes=list(scratch),
        compiler_params=pltpu.CompilerParams(vmem_limit_bytes=limit * 1024 * 1024),
        cost_estimate=pl.CostEstimate(flops=flops, bytes_accessed=1024, transcendentals=0),
    )(*first, *arrays, *ties)


def token_kernel(token_ref):
    token_ref[...] = jnp.zeros_like(token_ref)


def token(*values):
    return call(token_kernel, [((8, 128), F32)], [], ties=values, flops=40_000_000_000, limit=1)[0]


def unit_rows(raw):
    values = raw.astype(F32)
    inverse = lax.rsqrt(jnp.sum(values * values, axis=1, keepdims=True) + 1e-06)
    return values * inverse, inverse


def back_norm(unit, inverse, grad_unit):
    along = jnp.sum(unit * grad_unit, axis=1, keepdims=True)
    return (grad_unit - unit * along) * inverse


def stack_kernel(own_hbm, *refs):
    *parts, out_ref, sem = refs
    rows = own_hbm.shape[0]
    copy = pltpu.make_async_copy(own_hbm, out_ref.at[pl.ds(0, rows)], sem)
    copy.start()
    at = rows
    for part in parts:
        rows = part.shape[0]
        out_ref[at:at + rows, :] = part[...]
        at += rows
    copy.wait()


def stack(own_raw, parts, ties=()):
    rows, dim = own_raw.shape
    rows += sum(p.shape[0] for p in parts)
    return call(
        stack_kernel, [((rows, dim), BF16)], parts, ties=ties, first=[own_raw], scratch=[pltpu.SemaphoreType.DMA(())]
    )[0]


def round_rows(raw_ref, start, out_ref, at, rows, own=None):
    step = 64
    for n in range(0, rows, step):
        unit, inverse = unit_rows(raw_ref[start + n:start + n + step, :])
        out_ref[at + n:at + n + step, :] = unit.astype(BF16)
        if own is not None and n == 0:
            own[0][...] = unit
            own[1][...] = jnp.broadcast_to(inverse, own[1].shape)


def group_round_kernel(raw_ref, out_ref, unit_ref, inv_ref):
    round_rows(raw_ref, 0, out_ref, 0, raw_ref.shape[0], (unit_ref, inv_ref))


def early_round_kernel(raw_ref, out_ref, unit_ref, inv_ref):
    own = unit_ref.shape[0]
    round_rows(raw_ref, 0, out_ref, 0, own, (unit_ref, inv_ref))
    round_rows(raw_ref, 2 * own, out_ref, own, 2 * own)


def mine_round_kernel(early_ref, near13_ref, near4_ref, out_ref):
    own = near4_ref.shape[0]
    out_ref[:own, :] = early_ref[:own, :]
    round_rows(near13_ref, 0, out_ref, own, 4 * own)
    out_ref[5 * own:7 * own, :] = early_ref[own:, :]
    round_rows(near4_ref, 0, out_ref, 7 * own, own)


def scalar_kernel(log_ref, bias_ref, scal_ref):
    temp = jnp.exp(jnp.broadcast_to(log_ref[...], (1, 128)))
    scal_ref[...] = jnp.zeros_like(scal_ref)
    scal_ref[0:1, :] = temp
    scal_ref[1:2, :] = -LOG2E * temp
    scal_ref[2:3, :] = jnp.broadcast_to(-LOG2E * bias_ref[...], (1, 128))


def sigmoid_weights(power, scale):
    return (scale / (1.0 + jnp.exp2(power))).astype(BF16)


def powers(img, txt, scal_ref):
    slope, offset = scal_ref[1:2, 0:1], scal_ref[2:3, 0:1]
    dots = lax.dot_general(img, txt, (((1,), (1,)), ((), ())), preferred_element_type=F32)
    return dots * slope + offset


def text_grads(w_ref, img_ref, out_ref):
    step = 256
    for t in range(0, out_ref.shape[0], step):
        grad = lax.dot_general(
            w_ref[:, t:t + step], img_ref[...], (((0,), (0,)), ((), ())), preferred_element_type=F32
        )
        out_ref[t:t + step, :] = grad.astype(out_ref.dtype)


def mine_kernel(own, txt_ref, scal_ref, *refs):
    *parts, w_ref, img_ref, keep_ref = refs
    temp = scal_ref[0:1, 0:1]
    at = 0
    for part in parts:
        rows = part.shape[0]
        img = part[...] if at == 0 else unit_rows(part[...])[0].astype(BF16)
        img_ref[at:at + rows, :] = img
        power = powers(img, txt_ref[...], scal_ref)
        w_ref[at:at + rows, :] = sigmoid_weights(power, temp)
        if at == 0:
            corner = power[:own, :2 * own]
            row = lax.broadcasted_iota(jnp.int32, corner.shape, 0)
            column = lax.broadcasted_iota(jnp.int32, corner.shape, 1)
            positive = row == column
            signed = jnp.where(positive, -corner, corner)
            w_ref[:own, :2 * own] = sigmoid_weights(signed, jnp.where(positive, -temp, temp))
        at += rows
    text_grads(w_ref, img_ref, keep_ref)


def theirs_kernel(txt_ref, scal_ref, img_ref, w_ref, send_ref):
    step = 256
    for at in range(0, img_ref.shape[0], step):
        power = powers(img_ref[at:at + step, :], txt_ref[...], scal_ref)
        w_ref[at:at + step, :] = sigmoid_weights(power, scal_ref[0:1, 0:1])
    text_grads(w_ref, img_ref, send_ref)


def image_kernel(at, w1_ref, w2_ref, txt1_ref, txt2_ref, out_ref):
    rows = out_ref.shape[0]
    grad = jnp.dot(w1_ref[at:at + rows, :], txt1_ref[...], preferred_element_type=F32)
    grad += jnp.dot(w2_ref[at:at + rows, :], txt2_ref[...], preferred_element_type=F32)
    out_ref[...] = grad.astype(out_ref.dtype)


def total_kernel(keep_ref, got_ref, own_ref, part13_ref, part2_ref, part4_ref):
    at = 0
    for out in (own_ref, part13_ref, part2_ref, part4_ref):
        rows = out.shape[0]
        total = keep_ref[at:at + rows, :].astype(F32) + got_ref[at:at + rows, :].astype(F32)
        out[...] = total.astype(out.dtype)
        at += rows


def middle_kernel(part2_ref, got13_ref, got4_ref, out_ref):
    rows = got4_ref.shape[0]
    total = part2_ref[...] + got13_ref[2 * rows:, :].astype(F32)
    out_ref[:rows, :] = (total[:rows] + got4_ref[...].astype(F32)).astype(BF16)
    out_ref[rows:, :] = total[rows:].astype(BF16)


def landed_kernel(own_ref, got13_ref, got2_ref, sum_ref, send_ref):
    rows = own_ref.shape[0]
    sum_ref[...] = own_ref[...] + got13_ref[:rows, :].astype(F32) + got2_ref[:rows, :].astype(F32)
    send_ref[...] = (got13_ref[rows:2 * rows, :].astype(F32) + got2_ref[rows:, :].astype(F32)).astype(BF16)


def partial_kernel(own_ref, first_ref, out_ref):
    out_ref[...] = own_ref[...] + first_ref[...].astype(F32)


def sums_kernel(sum_ref, first_ref, second_ref, *outs):
    rows = outs[0].shape[0]
    for n, out in enumerate(outs):
        at = slice(n * rows, (n + 1) * rows)
        out[...] = (sum_ref[at, :] + first_ref[at, :].astype(F32) + second_ref[at, :].astype(F32)).astype(out.dtype)


def final_kernel(*refs):
    *ins, img_ref, txt_ref = refs
    for (unit_ref, inv_ref, own_ref, *parts), out_ref in ((ins[:6], img_ref), (ins[6:], txt_ref)):
        grad = own_ref[...] + sum(p[...].astype(F32) for p in parts)
        out_ref[...] = back_norm(unit_ref[...], inv_ref[:, :1], grad)


def local(images, texts, log_temp, bias):
    own, dim = images.shape

    side = [shift(images, first(k), "gA%d" % k) for k in (1, 2, 3)]
    line2 = shift(texts, line(2), "gZ2")
    cross2 = shift(texts, cross(2), "gX2")
    swapped = shift(texts, other, "gC")
    group = stack(images, side, [token(swapped)])
    send13 = stack(texts, [swapped, line2, cross2])
    far = [shift(group, second(k), "gB%d" % k) for k in (1, 3, 2)]
    near13 = shift(send13, line(1), "gZ13")
    near4 = shift(line2, line(2), "gZ4")
    first_token = token(group)
    (scalars,) = call(
        scalar_kernel, [((8, 128), F32)], [log_temp.reshape(1, 1), bias.reshape(1, 1)], [near13]
    )
    per_row = [((own, dim), F32), ((own, 128), F32)]
    group, img_unit, inv_img = call(group_round_kernel, [(group.shape, BF16)] + per_row, [group], [scalars])
    early, txt_unit, inv_txt = call(early_round_kernel, [((3 * own, dim), BF16)] + per_row, [send13], [scalars])
    (mine,) = call(
        mine_round_kernel, [((8 * own, dim), BF16)], [early, near13, near4], [group, first_token, *far]
    )
    theirs = shift(mine, other, "gS")

    half = mine.shape[0]
    rows = group.shape[0] * (1 + len(far))
    flops = 2 * rows * half * dim
    w_mine, img_all, keep = call(
        lambda *refs: mine_kernel(own, *refs), [((rows, half), BF16), ((rows, dim), BF16), ((half, dim), BF16)],
        [mine, scalars, group, *far], flops=2 * flops, limit=24,
    )
    w_theirs, send = call(
        theirs_kernel, [((rows, half), BF16), ((half, dim), BF16)],
        [theirs, scalars, img_all], ties=[keep], flops=2 * flops, limit=24,
    )
    each = group.shape[0]

    def image_grads(index, dtype, ties):
        return call(
            lambda *refs: image_kernel(index * each, *refs), [((each, dim), dtype)],
            [w_mine, w_theirs, mine, theirs], ties=ties, flops=flops // 2, limit=24,
        )[0]

    grad3 = image_grads(2, BF16, [send])
    back3 = shift(grad3, second(-3), "rB3")
    total_own, part13, part2, part4 = call(
        total_kernel,
        [((own, dim), F32), ((4 * own, dim), BF16), ((2 * own, dim), F32), ((own, dim), BF16)],
        [keep, shift(send, other, "rC")], ties=[grad3],
    )
    grad1 = image_grads(1, BF16, [part13])
    back1 = shift(grad1, second(-1), "rB1")
    grad2 = image_grads(3, BF16, [grad1])
    back2 = shift(grad2, second(-2), "rB2")
    grad0 = image_grads(0, F32, [grad2])
    (partial,) = call(partial_kernel, [((each, dim), F32)], [grad0, back3])
    got13 = shift(part13, line(-1), "rZ13")
    got4 = shift(part4, line(-2), "rZ4")
    (middle,) = call(middle_kernel, [((2 * own, dim), BF16)], [part2, got13, got4], [partial])
    got2 = shift(middle, line(-2), "rZ2")
    txt_sum, txt_send = call(landed_kernel, [((own, dim), F32), ((own, dim), BF16)], [total_own, got13, got2])
    txt_last = shift(txt_send, other, "rS")

    img_sum, *parts = call(
        sums_kernel, [((own, dim), F32)] + [((own, dim), BF16)] * 3, [partial, back1, back2], ties=[token(middle)]
    )
    last = [shift(p, first(-k), "rA%d" % k) for k, p in zip((1, 2, 3), parts)]

    return call(
        final_kernel, [((own, dim), F32)] * 2,
        [img_unit, inv_img, img_sum, *last, txt_unit, inv_txt, txt_sum, txt_last],
    )


def solution(mesh):
    in_specs = (P(("row", "col"), None), P(("row", "col"), None), P(), P())
    out_specs = (P(("row", "col"), None), P(("row", "col"), None))
    return jax.shard_map(local, mesh=mesh, in_specs=in_specs, out_specs=out_specs, check_vma=False)
```

```python
import jax
import jax.numpy as jnp
from jax import lax
from jax.experimental import pallas as pl
from jax.experimental.pallas import tpu as pltpu
from jax.sharding import PartitionSpec as P

AXES = ("row", "col")
F32 = jnp.float32
BF16 = jnp.bfloat16
LOG2E = 1.4426950408889634
SIZE_X, SIZE_Y, SIZE_Z, CORES = 4, 4, 8, 2


def device(x, y, z, c):
    return ((z // 4) * 16 + x * 4 + y) * 8 + (z % 4) * 2 + c


def shift(values, move, name="move"):
    pairs = []
    for x in range(SIZE_X):
        for y in range(SIZE_Y):
            for z in range(SIZE_Z):
                for c in range(CORES):
                    nx, ny, nz, nc = move(x, y, z, c)
                    pairs.append((device(x, y, z, c), device(nx % SIZE_X, ny % SIZE_Y, nz % SIZE_Z, nc)))
    with jax.named_scope(name):
        return lax.ppermute(values, AXES, pairs)


def first(k):
    return lambda x, y, z, c: (x + k, y, z, c) if c == 0 else (x, y + k, z, c)


def second(k):
    return lambda x, y, z, c: (x, y + k, z, c) if c == 0 else (x + k, y, z, c)


def line(k):
    return lambda x, y, z, c: (x, y, z + k, c) if c == 0 else (x, y, z - k, c)


def cross(k):
    return lambda x, y, z, c: (x, y, z + k, 0) if c == 1 else (x, y, z - k, 1)


def other(x, y, z, c):
    return (x, y, z, 1 - c)


def call(kernel, outs, arrays, ties=(), first=(), scratch=(), flops=0, limit=8):
    vmem = pl.BlockSpec(memory_space=pltpu.VMEM)
    anywhere = pl.BlockSpec(memory_space=pl.ANY)
    n_in = len(first) + len(arrays)
    return pl.pallas_call(
        lambda *refs: kernel(*refs[:n_in], *refs[n_in + len(ties):]),
        out_shape=tuple(jax.ShapeDtypeStruct(shape, dtype) for shape, dtype in outs),
        in_specs=[anywhere] * len(first) + [vmem] * len(arrays) + [anywhere] * len(ties),
        out_specs=tuple([vmem] * len(outs)),
        scratch_shapes=list(scratch),
        compiler_params=pltpu.CompilerParams(vmem_limit_bytes=limit * 1024 * 1024),
        cost_estimate=pl.CostEstimate(flops=flops, bytes_accessed=1024, transcendentals=0),
    )(*first, *arrays, *ties)


def token_kernel(token_ref):
    token_ref[...] = jnp.zeros_like(token_ref)


def token(*values):
    return call(token_kernel, [((8, 128), F32)], [], ties=values, flops=40_000_000_000, limit=1)[0]


def unit_rows(raw):
    values = raw.astype(F32)
    inverse = lax.rsqrt(jnp.sum(values * values, axis=1, keepdims=True) + 1e-06)
    return values * inverse, inverse


def back_norm(unit, inverse, grad_unit):
    along = jnp.sum(unit * grad_unit, axis=1, keepdims=True)
    return (grad_unit - unit * along) * inverse


def stack_kernel(own_hbm, *refs):
    *parts, out_ref, sem = refs
    rows = own_hbm.shape[0]
    copy = pltpu.make_async_copy(own_hbm, out_ref.at[pl.ds(0, rows)], sem)
    copy.start()
    at = rows
    for part in parts:
        rows = part.shape[0]
        out_ref[at:at + rows, :] = part[...]
        at += rows
    copy.wait()


def stack(own_raw, parts, ties=()):
    rows, dim = own_raw.shape
    rows += sum(p.shape[0] for p in parts)
    return call(
        stack_kernel, [((rows, dim), BF16)], parts, ties=ties, first=[own_raw], scratch=[pltpu.SemaphoreType.DMA(())]
    )[0]


def round_rows(raw_ref, start, out_ref, at, rows, own=None):
    step = 64
    for n in range(0, rows, step):
        unit, inverse = unit_rows(raw_ref[start + n:start + n + step, :])
        out_ref[at + n:at + n + step, :] = unit.astype(BF16)
        if own is not None and n == 0:
            own[0][...] = unit
            own[1][...] = jnp.broadcast_to(inverse, own[1].shape)


def group_round_kernel(raw_ref, out_ref, unit_ref, inv_ref):
    round_rows(raw_ref, 0, out_ref, 0, raw_ref.shape[0], (unit_ref, inv_ref))


def early_round_kernel(raw_ref, out_ref, unit_ref, inv_ref):
    own = unit_ref.shape[0]
    round_rows(raw_ref, 0, out_ref, 0, own, (unit_ref, inv_ref))
    round_rows(raw_ref, 2 * own, out_ref, own, 2 * own)


def mine_round_kernel(early_ref, near13_ref, near4_ref, out_ref):
    own = near4_ref.shape[0]
    out_ref[:own, :] = early_ref[:own, :]
    round_rows(near13_ref, 0, out_ref, own, 4 * own)
    out_ref[5 * own:7 * own, :] = early_ref[own:, :]
    round_rows(near4_ref, 0, out_ref, 7 * own, own)


def scalar_kernel(log_ref, bias_ref, scal_ref):
    temp = jnp.exp(jnp.broadcast_to(log_ref[...], (1, 128)))
    scal_ref[...] = jnp.zeros_like(scal_ref)
    scal_ref[0:1, :] = temp
    scal_ref[1:2, :] = -LOG2E * temp
    scal_ref[2:3, :] = jnp.broadcast_to(-LOG2E * bias_ref[...], (1, 128))


def sigmoid_weights(power, scale):
    return (scale / (1.0 + jnp.exp2(power))).astype(BF16)


def powers(img, txt, scal_ref):
    slope, offset = scal_ref[1:2, 0:1], scal_ref[2:3, 0:1]
    dots = lax.dot_general(img, txt, (((1,), (1,)), ((), ())), preferred_element_type=F32)
    return dots * slope + offset


def text_grads(w_ref, img_ref, out_ref):
    step = 256
    for t in range(0, out_ref.shape[0], step):
        grad = lax.dot_general(
            w_ref[:, t:t + step], img_ref[...], (((0,), (0,)), ((), ())), preferred_element_type=F32
        )
        out_ref[t:t + step, :] = grad.astype(out_ref.dtype)


def mine_kernel(own, txt_ref, scal_ref, *refs):
    *parts, w_ref, img_ref, keep_ref = refs
    temp = scal_ref[0:1, 0:1]
    at = 0
    for part in parts:
        rows = part.shape[0]
        img = part[...] if at == 0 else unit_rows(part[...])[0].astype(BF16)
        img_ref[at:at + rows, :] = img
        power = powers(img, txt_ref[...], scal_ref)
        w_ref[at:at + rows, :] = sigmoid_weights(power, temp)
        if at == 0:
            corner = power[:own, :2 * own]
            row = lax.broadcasted_iota(jnp.int32, corner.shape, 0)
            column = lax.broadcasted_iota(jnp.int32, corner.shape, 1)
            positive = row == column
            signed = jnp.where(positive, -corner, corner)
            w_ref[:own, :2 * own] = sigmoid_weights(signed, jnp.where(positive, -temp, temp))
        at += rows
    text_grads(w_ref, img_ref, keep_ref)


def theirs_kernel(txt_ref, scal_ref, img_ref, w_ref, send_ref):
    step = 256
    for at in range(0, img_ref.shape[0], step):
        power = powers(img_ref[at:at + step, :], txt_ref[...], scal_ref)
        w_ref[at:at + step, :] = sigmoid_weights(power, scal_ref[0:1, 0:1])
    text_grads(w_ref, img_ref, send_ref)


def image_kernel(at, w1_ref, w2_ref, txt1_ref, txt2_ref, *outs):
    rows = sum(out.shape[0] for out in outs)
    grad = jnp.dot(w1_ref[at:at + rows, :], txt1_ref[...], preferred_element_type=F32)
    grad += jnp.dot(w2_ref[at:at + rows, :], txt2_ref[...], preferred_element_type=F32)
    at = 0
    for out in outs:
        out[...] = grad[at:at + out.shape[0]].astype(out.dtype)
        at += out.shape[0]


def relay_kernel(first_ref, first_got_ref, second_ref, second_got_ref, first_out, second_out):
    first_out[...] = (first_ref[...].astype(F32) + first_got_ref[...].astype(F32)).astype(BF16)
    second_out[...] = (second_ref[...].astype(F32) + second_got_ref[...].astype(F32)).astype(BF16)


def total_kernel(keep_ref, got_ref, own_ref, part13_ref, part2_ref, part4_ref):
    at = 0
    for out in (own_ref, part13_ref, part2_ref, part4_ref):
        rows = out.shape[0]
        total = keep_ref[at:at + rows, :].astype(F32) + got_ref[at:at + rows, :].astype(F32)
        out[...] = total.astype(out.dtype)
        at += rows


def middle_kernel(part2_ref, got13_ref, got4_ref, out_ref):
    rows = got4_ref.shape[0]
    total = part2_ref[...] + got13_ref[2 * rows:, :].astype(F32)
    out_ref[:rows, :] = (total[:rows] + got4_ref[...].astype(F32)).astype(BF16)
    out_ref[rows:, :] = total[rows:].astype(BF16)


def landed_kernel(own_ref, got13_ref, got2_ref, sum_ref, send_ref):
    rows = own_ref.shape[0]
    sum_ref[...] = own_ref[...] + got13_ref[:rows, :].astype(F32) + got2_ref[:rows, :].astype(F32)
    send_ref[...] = (got13_ref[rows:2 * rows, :].astype(F32) + got2_ref[rows:, :].astype(F32)).astype(BF16)


def partial_kernel(own_ref, upper_ref, lower_ref, out_ref):
    half = upper_ref.shape[0]
    out_ref[:half, :] = own_ref[:half, :] + upper_ref[...].astype(F32)
    out_ref[half:, :] = own_ref[half:, :] + lower_ref[...].astype(F32)


def sums_kernel(sum_ref, upper_ref, lower_ref, *outs):
    rows, half = outs[0].shape[0], upper_ref.shape[0]
    for n, out in enumerate(outs):
        at = n * rows
        last_ref, base = (upper_ref, 0) if at < half else (lower_ref, half)
        total = sum_ref[at:at + rows, :] + last_ref[at - base:at - base + rows, :].astype(F32)
        out[...] = total.astype(out.dtype)


def final_kernel(*refs):
    *ins, img_ref, txt_ref = refs
    for (unit_ref, inv_ref, own_ref, *parts), out_ref in ((ins[:6], img_ref), (ins[6:], txt_ref)):
        grad = own_ref[...] + sum(p[...].astype(F32) for p in parts)
        out_ref[...] = back_norm(unit_ref[...], inv_ref[:, :1], grad)


def local(images, texts, log_temp, bias):
    own, dim = images.shape

    side = [shift(images, first(k), "gA%d" % k) for k in (1, 2, 3)]
    line2 = shift(texts, line(2), "gZ2")
    cross2 = shift(texts, cross(2), "gX2")
    swapped = shift(texts, other, "gC")
    group = stack(images, side, [token(swapped)])
    send13 = stack(texts, [swapped, line2, cross2])
    far = [shift(group, second(k), "gB%d" % k) for k in (1, 3, 2)]
    near13 = shift(send13, line(1), "gZ13")
    near4 = shift(line2, line(2), "gZ4")
    first_token = token(group)
    (scalars,) = call(
        scalar_kernel, [((8, 128), F32)], [log_temp.reshape(1, 1), bias.reshape(1, 1)], [near13]
    )
    per_row = [((own, dim), F32), ((own, 128), F32)]
    group, img_unit, inv_img = call(group_round_kernel, [(group.shape, BF16)] + per_row, [group], [scalars])
    early, txt_unit, inv_txt = call(early_round_kernel, [((3 * own, dim), BF16)] + per_row, [send13], [scalars])
    (mine,) = call(
        mine_round_kernel, [((8 * own, dim), BF16)], [early, near13, near4], [group, first_token, *far]
    )
    theirs = shift(mine, other, "gS")

    half = mine.shape[0]
    rows = group.shape[0] * (1 + len(far))
    flops = 2 * rows * half * dim
    w_mine, img_all, keep = call(
        lambda *refs: mine_kernel(own, *refs), [((rows, half), BF16), ((rows, dim), BF16), ((half, dim), BF16)],
        [mine, scalars, group, *far], flops=2 * flops, limit=24,
    )
    w_theirs, send = call(
        theirs_kernel, [((rows, half), BF16), ((half, dim), BF16)],
        [theirs, scalars, img_all], ties=[keep], flops=2 * flops, limit=24,
    )
    each = group.shape[0]

    def image_grads(index, shapes, ties):
        return call(
            lambda *refs: image_kernel(index * each, *refs), shapes,
            [w_mine, w_theirs, mine, theirs], ties=ties, flops=flops // 2, limit=24,
        )

    halves = [((each // 2, dim), BF16)] * 2
    upper2, lower2 = image_grads(3, halves, [send])
    relay1 = shift(upper2, second(-1), "rF1")
    relay3 = shift(lower2, second(1), "rF3")

    total_own, part13, part2, part4 = call(
        total_kernel,
        [((own, dim), F32), ((4 * own, dim), BF16), ((2 * own, dim), F32), ((own, dim), BF16)],
        [keep, shift(send, other, "rC")], ties=[upper2],
    )
    upper3, lower3 = image_grads(2, halves, [part13])
    upper_got = [shift(upper3, second(1), "rH3")]
    upper1, lower1 = image_grads(1, halves, [upper3])
    lower_got = [shift(lower1, second(-1), "rH1")]
    upper1, lower3 = call(relay_kernel, halves, [upper1, relay1, lower3, relay3])
    upper_got.append(shift(upper1, second(-1), "rG1"))
    lower_got.append(shift(lower3, second(1), "rG3"))
    (grad0,) = image_grads(0, [((each, dim), F32)], [upper1])
    (partial,) = call(partial_kernel, [((each, dim), F32)], [grad0, upper_got[0], lower_got[0]])
    got13 = shift(part13, line(-1), "rZ13")
    got4 = shift(part4, line(-2), "rZ4")
    (middle,) = call(middle_kernel, [((2 * own, dim), BF16)], [part2, got13, got4], [partial])
    got2 = shift(middle, line(-2), "rZ2")
    txt_sum, txt_send = call(landed_kernel, [((own, dim), F32), ((own, dim), BF16)], [total_own, got13, got2])
    txt_last = shift(txt_send, other, "rS")

    img_sum, *parts = call(
        sums_kernel, [((own, dim), F32)] + [((own, dim), BF16)] * 3, [partial, upper_got[1], lower_got[1]], ties=[token(middle)]
    )
    last = [shift(p, first(-k), "rA%d" % k) for k, p in zip((1, 2, 3), parts)]

    return call(
        final_kernel, [((own, dim), F32)] * 2,
        [img_unit, inv_img, img_sum, *last, txt_unit, inv_txt, txt_sum, txt_last],
    )


def solution(mesh):
    in_specs = (P(("row", "col"), None), P(("row", "col"), None), P(), P())
    out_specs = (P(("row", "col"), None), P(("row", "col"), None))
    return jax.shard_map(local, mesh=mesh, in_specs=in_specs, out_specs=out_specs, check_vma=False)
```

```python
import jax
import jax.numpy as jnp
from jax import lax
from jax.experimental import pallas as pl
from jax.experimental.pallas import tpu as pltpu
from jax.sharding import PartitionSpec as P

AXES = ("row", "col")
F32 = jnp.float32
BF16 = jnp.bfloat16
LOG2E = 1.4426950408889634
SIZE_X, SIZE_Y, SIZE_Z, CORES = 4, 4, 8, 2


def device(x, y, z, c):
    return ((z // 4) * 16 + x * 4 + y) * 8 + (z % 4) * 2 + c


def shift(values, move, name="move"):
    pairs = []
    for x in range(SIZE_X):
        for y in range(SIZE_Y):
            for z in range(SIZE_Z):
                for c in range(CORES):
                    nx, ny, nz, nc = move(x, y, z, c)
                    pairs.append((device(x, y, z, c), device(nx % SIZE_X, ny % SIZE_Y, nz % SIZE_Z, nc)))
    with jax.named_scope(name):
        return lax.ppermute(values, AXES, pairs)


def first(k):
    return lambda x, y, z, c: (x + k, y, z, c) if c == 0 else (x, y + k, z, c)


def second(k):
    return lambda x, y, z, c: (x, y + k, z, c) if c == 0 else (x + k, y, z, c)


def line(k):
    return lambda x, y, z, c: (x, y, z + k, c) if c == 0 else (x, y, z - k, c)


def other(x, y, z, c):
    return (x, y, z, 1 - c)


def call(kernel, outs, arrays, ties=(), first=(), scratch=(), flops=0, limit=8):
    vmem = pl.BlockSpec(memory_space=pltpu.VMEM)
    anywhere = pl.BlockSpec(memory_space=pl.ANY)
    n_in = len(first) + len(arrays)
    return pl.pallas_call(
        lambda *refs: kernel(*refs[:n_in], *refs[n_in + len(ties):]),
        out_shape=tuple(jax.ShapeDtypeStruct(shape, dtype) for shape, dtype in outs),
        in_specs=[anywhere] * len(first) + [vmem] * len(arrays) + [anywhere] * len(ties),
        out_specs=tuple([vmem] * len(outs)),
        scratch_shapes=list(scratch),
        compiler_params=pltpu.CompilerParams(vmem_limit_bytes=limit * 1024 * 1024),
        cost_estimate=pl.CostEstimate(flops=flops, bytes_accessed=1024, transcendentals=0),
    )(*first, *arrays, *ties)


def token_kernel(token_ref):
    token_ref[...] = jnp.zeros_like(token_ref)


def token(*values):
    return call(token_kernel, [((8, 128), F32)], [], ties=values, flops=40_000_000_000, limit=1)[0]


def unit_rows(raw):
    values = raw.astype(F32)
    inverse = lax.rsqrt(jnp.sum(values * values, axis=1, keepdims=True) + 1e-06)
    return values * inverse, inverse


def back_norm(unit, inverse, grad_unit):
    along = jnp.sum(unit * grad_unit, axis=1, keepdims=True)
    return (grad_unit - unit * along) * inverse


def stack_kernel(own_hbm, *refs):
    *parts, out_ref, sem = refs
    rows = own_hbm.shape[0]
    copy = pltpu.make_async_copy(own_hbm, out_ref.at[pl.ds(0, rows)], sem)
    copy.start()
    at = rows
    for part in parts:
        rows = part.shape[0]
        out_ref[at:at + rows, :] = part[...]
        at += rows
    copy.wait()


def stack(own_raw, parts, ties=()):
    rows, dim = own_raw.shape
    rows += sum(p.shape[0] for p in parts)
    return call(
        stack_kernel, [((rows, dim), BF16)], parts, ties=ties, first=[own_raw], scratch=[pltpu.SemaphoreType.DMA(())]
    )[0]


def head_kernel(in_ref, out_ref):
    out_ref[...] = in_ref[...]


def send_kernel(pair_ref, near_ref, send13_ref, send4_ref):
    rows = pair_ref.shape[0]
    send13_ref[:rows, :] = pair_ref[...]
    send13_ref[rows:, :] = near_ref[...]
    send4_ref[...] = near_ref[:send4_ref.shape[0], :]


def round_rows(raw_ref, start, out_ref, at, rows, own=None):
    step = 64
    for n in range(0, rows, step):
        unit, inverse = unit_rows(raw_ref[start + n:start + n + step, :])
        out_ref[at + n:at + n + step, :] = unit.astype(BF16)
        if own is not None and n == 0:
            own[0][...] = unit
            own[1][...] = jnp.broadcast_to(inverse, own[1].shape)


def group_round_kernel(raw_ref, out_ref, unit_ref, inv_ref):
    round_rows(raw_ref, 0, out_ref, 0, raw_ref.shape[0], (unit_ref, inv_ref))


def early_round_kernel(raw_ref, out_ref, unit_ref, inv_ref):
    own = unit_ref.shape[0]
    round_rows(raw_ref, 0, out_ref, 0, own, (unit_ref, inv_ref))
    round_rows(raw_ref, 2 * own, out_ref, own, 2 * own)


def mine_round_kernel(early_ref, near13_ref, near4_ref, out_ref):
    own = near4_ref.shape[0]
    out_ref[:own, :] = early_ref[:own, :]
    round_rows(near13_ref, 0, out_ref, own, 4 * own)
    out_ref[5 * own:7 * own, :] = early_ref[own:, :]
    round_rows(near4_ref, 0, out_ref, 7 * own, own)


def scalar_kernel(log_ref, bias_ref, scal_ref):
    temp = jnp.exp(jnp.broadcast_to(log_ref[...], (1, 128)))
    scal_ref[...] = jnp.zeros_like(scal_ref)
    scal_ref[0:1, :] = temp
    scal_ref[1:2, :] = -LOG2E * temp
    scal_ref[2:3, :] = jnp.broadcast_to(-LOG2E * bias_ref[...], (1, 128))


def sigmoid_weights(power, scale):
    return (scale / (1.0 + jnp.exp2(power))).astype(BF16)


def powers(img, txt, scal_ref):
    slope, offset = scal_ref[1:2, 0:1], scal_ref[2:3, 0:1]
    dots = lax.dot_general(img, txt, (((1,), (1,)), ((), ())), preferred_element_type=F32)
    return dots * slope + offset


def text_grads(w_ref, img_ref, out_ref):
    step = 256
    for t in range(0, out_ref.shape[0], step):
        grad = lax.dot_general(
            w_ref[:, t:t + step], img_ref[...], (((0,), (0,)), ((), ())), preferred_element_type=F32
        )
        out_ref[t:t + step, :] = grad.astype(out_ref.dtype)


def mine_kernel(own, txt_ref, scal_ref, *refs):
    *parts, w_ref, img_ref, keep_ref = refs
    temp = scal_ref[0:1, 0:1]
    at = 0
    for part in parts:
        rows = part.shape[0]
        img = part[...] if at == 0 else unit_rows(part[...])[0].astype(BF16)
        img_ref[at:at + rows, :] = img
        power = powers(img, txt_ref[...], scal_ref)
        w_ref[at:at + rows, :] = sigmoid_weights(power, temp)
        if at == 0:
            corner = power[:own, :2 * own]
            row = lax.broadcasted_iota(jnp.int32, corner.shape, 0)
            column = lax.broadcasted_iota(jnp.int32, corner.shape, 1)
            positive = row == column
            signed = jnp.where(positive, -corner, corner)
            w_ref[:own, :2 * own] = sigmoid_weights(signed, jnp.where(positive, -temp, temp))
        at += rows
    text_grads(w_ref, img_ref, keep_ref)


def theirs_kernel(txt_ref, scal_ref, img_ref, w_ref, send_ref):
    step = 256
    for at in range(0, img_ref.shape[0], step):
        power = powers(img_ref[at:at + step, :], txt_ref[...], scal_ref)
        w_ref[at:at + step, :] = sigmoid_weights(power, scal_ref[0:1, 0:1])
    text_grads(w_ref, img_ref, send_ref)


def image_kernel(at, w1_ref, w2_ref, txt1_ref, txt2_ref, out_ref):
    rows = out_ref.shape[0]
    grad = jnp.dot(w1_ref[at:at + rows, :], txt1_ref[...], preferred_element_type=F32)
    grad += jnp.dot(w2_ref[at:at + rows, :], txt2_ref[...], preferred_element_type=F32)
    out_ref[...] = grad.astype(out_ref.dtype)


def total_kernel(keep_ref, got_ref, own_ref, part13_ref, part2_ref, part4_ref):
    at = 0
    for out in (own_ref, part13_ref, part2_ref, part4_ref):
        rows = out.shape[0]
        total = keep_ref[at:at + rows, :].astype(F32) + got_ref[at:at + rows, :].astype(F32)
        out[...] = total.astype(out.dtype)
        at += rows


def middle_kernel(part2_ref, got13_ref, got4_ref, out_ref):
    rows = got4_ref.shape[0]
    total = part2_ref[...] + got13_ref[2 * rows:, :].astype(F32)
    out_ref[:rows, :] = (total[:rows] + got4_ref[...].astype(F32)).astype(BF16)
    out_ref[rows:, :] = total[rows:].astype(BF16)


def landed_kernel(own_ref, got13_ref, got2_ref, sum_ref, send_ref):
    rows = own_ref.shape[0]
    sum_ref[...] = own_ref[...] + got13_ref[:rows, :].astype(F32) + got2_ref[:rows, :].astype(F32)
    send_ref[...] = (got13_ref[rows:2 * rows, :].astype(F32) + got2_ref[rows:, :].astype(F32)).astype(BF16)


def partial_kernel(own_ref, first_ref, out_ref):
    out_ref[...] = own_ref[...] + first_ref[...].astype(F32)


def sums_kernel(sum_ref, first_ref, second_ref, *outs):
    rows = outs[0].shape[0]
    for n, out in enumerate(outs):
        at = slice(n * rows, (n + 1) * rows)
        out[...] = (sum_ref[at, :] + first_ref[at, :].astype(F32) + second_ref[at, :].astype(F32)).astype(out.dtype)


def final_kernel(*refs):
    *ins, img_ref, txt_ref = refs
    for (unit_ref, inv_ref, own_ref, *parts), out_ref in ((ins[:6], img_ref), (ins[6:], txt_ref)):
        grad = own_ref[...] + sum(p[...].astype(F32) for p in parts)
        out_ref[...] = back_norm(unit_ref[...], inv_ref[:, :1], grad)


def local(images, texts, log_temp, bias):
    own, dim = images.shape

    swapped = shift(texts, other, "gC")
    side = [shift(images, first(k), "gA%d" % k) for k in (1, 2, 3)]
    pair = stack(texts, [swapped])
    near2 = shift(pair, line(2), "gZ2")
    group = stack(images, side, [token(pair)])
    send13, send4 = call(send_kernel, [((4 * own, dim), BF16), ((own, dim), BF16)], [pair, near2], [group])
    far = [shift(group, second(k), "gB%d" % k) for k in (1, 3, 2)]
    near13 = shift(send13, line(1), "gZ13")
    near4 = shift(call(head_kernel, [((own, dim), BF16)], [send4], [send13])[0], line(2), "gZ4")
    first_token = token(group)
    (scalars,) = call(
        scalar_kernel, [((8, 128), F32)], [log_temp.reshape(1, 1), bias.reshape(1, 1)], [near13]
    )
    per_row = [((own, dim), F32), ((own, 128), F32)]
    group, img_unit, inv_img = call(group_round_kernel, [(group.shape, BF16)] + per_row, [group], [scalars])
    early, txt_unit, inv_txt = call(early_round_kernel, [((3 * own, dim), BF16)] + per_row, [send13], [scalars])
    (mine,) = call(
        mine_round_kernel, [((8 * own, dim), BF16)], [early, near13, near4], [group, first_token, *far]
    )
    theirs = shift(mine, other, "gS")

    half = mine.shape[0]
    rows = group.shape[0] * (1 + len(far))
    flops = 2 * rows * half * dim
    w_mine, img_all, keep = call(
        lambda *refs: mine_kernel(own, *refs), [((rows, half), BF16), ((rows, dim), BF16), ((half, dim), BF16)],
        [mine, scalars, group, *far], flops=2 * flops, limit=24,
    )
    w_theirs, send = call(
        theirs_kernel, [((rows, half), BF16), ((half, dim), BF16)],
        [theirs, scalars, img_all], ties=[keep], flops=2 * flops, limit=24,
    )
    each = group.shape[0]

    def image_grads(index, dtype, ties):
        return call(
            lambda *refs: image_kernel(index * each, *refs), [((each, dim), dtype)],
            [w_mine, w_theirs, mine, theirs], ties=ties, flops=flops // 2, limit=24,
        )[0]

    grad3 = image_grads(2, BF16, [send])
    back3 = shift(grad3, second(-3), "rB3")
    total_own, part13, part2, part4 = call(
        total_kernel,
        [((own, dim), F32), ((4 * own, dim), BF16), ((2 * own, dim), F32), ((own, dim), BF16)],
        [keep, shift(send, other, "rC")], ties=[grad3],
    )
    grad1 = image_grads(1, BF16, [part13])
    back1 = shift(grad1, second(-1), "rB1")
    grad2 = image_grads(3, BF16, [grad1])
    back2 = shift(grad2, second(-2), "rB2")
    grad0 = image_grads(0, F32, [grad2])
    (partial,) = call(partial_kernel, [((each, dim), F32)], [grad0, back3])
    got13 = shift(part13, line(-1), "rZ13")
    got4 = shift(part4, line(-2), "rZ4")
    (middle,) = call(middle_kernel, [((2 * own, dim), BF16)], [part2, got13, got4], [partial])
    got2 = shift(middle, line(-2), "rZ2")
    txt_sum, txt_send = call(landed_kernel, [((own, dim), F32), ((own, dim), BF16)], [total_own, got13, got2])
    txt_last = shift(txt_send, other, "rS")

    img_sum, *parts = call(
        sums_kernel, [((own, dim), F32)] + [((own, dim), BF16)] * 3, [partial, back1, back2], ties=[token(middle)]
    )
    last = [shift(p, first(-k), "rA%d" % k) for k, p in zip((1, 2, 3), parts)]

    return call(
        final_kernel, [((own, dim), F32)] * 2,
        [img_unit, inv_img, img_sum, *last, txt_unit, inv_txt, txt_sum, txt_last],
    )


def solution(mesh):
    in_specs = (P(("row", "col"), None), P(("row", "col"), None), P(), P())
    out_specs = (P(("row", "col"), None), P(("row", "col"), None))
    return jax.shard_map(local, mesh=mesh, in_specs=in_specs, out_specs=out_specs, check_vma=False)
```

```python
import jax
import jax.numpy as jnp
from jax import lax
from jax.experimental import pallas as pl
from jax.experimental.pallas import tpu as pltpu
from jax.sharding import PartitionSpec as P

AXES = ("row", "col")
F32 = jnp.float32
BF16 = jnp.bfloat16
LOG2E = 1.4426950408889634
SIZE_X, SIZE_Y, SIZE_Z, CORES = 4, 4, 8, 2


def device(x, y, z, c):
    return ((z // 4) * 16 + x * 4 + y) * 8 + (z % 4) * 2 + c


def shift(values, move, name="move"):
    pairs = []
    for x in range(SIZE_X):
        for y in range(SIZE_Y):
            for z in range(SIZE_Z):
                for c in range(CORES):
                    nx, ny, nz, nc = move(x, y, z, c)
                    pairs.append((device(x, y, z, c), device(nx % SIZE_X, ny % SIZE_Y, nz % SIZE_Z, nc)))
    with jax.named_scope(name):
        return lax.ppermute(values, AXES, pairs)


def first(k):
    return lambda x, y, z, c: (x + k, y, z, c) if c == 0 else (x, y + k, z, c)


def second(k):
    return lambda x, y, z, c: (x, y + k, z, c) if c == 0 else (x + k, y, z, c)


def line(k):
    return lambda x, y, z, c: (x, y, z + k, c) if c == 0 else (x, y, z - k, c)


def cross(k):
    return lambda x, y, z, c: (x, y, z + k, 0) if c == 1 else (x, y, z - k, 1)


def other(x, y, z, c):
    return (x, y, z, 1 - c)


def call(kernel, outs, arrays, ties=(), first=(), scratch=(), flops=0, limit=8):
    vmem = pl.BlockSpec(memory_space=pltpu.VMEM)
    anywhere = pl.BlockSpec(memory_space=pl.ANY)
    n_in = len(first) + len(arrays)
    return pl.pallas_call(
        lambda *refs: kernel(*refs[:n_in], *refs[n_in + len(ties):]),
        out_shape=tuple(jax.ShapeDtypeStruct(shape, dtype) for shape, dtype in outs),
        in_specs=[anywhere] * len(first) + [vmem] * len(arrays) + [anywhere] * len(ties),
        out_specs=tuple([vmem] * len(outs)),
        scratch_shapes=list(scratch),
        compiler_params=pltpu.CompilerParams(vmem_limit_bytes=limit * 1024 * 1024),
        cost_estimate=pl.CostEstimate(flops=flops, bytes_accessed=1024, transcendentals=0),
    )(*first, *arrays, *ties)


def token_kernel(token_ref):
    token_ref[...] = jnp.zeros_like(token_ref)


def token(*values):
    return call(token_kernel, [((8, 128), F32)], [], ties=values, flops=40_000_000_000, limit=1)[0]


def unit_rows(raw):
    values = raw.astype(F32)
    inverse = lax.rsqrt(jnp.sum(values * values, axis=1, keepdims=True) + 1e-06)
    return values * inverse, inverse


def back_norm(unit, inverse, grad_unit):
    along = jnp.sum(unit * grad_unit, axis=1, keepdims=True)
    return (grad_unit - unit * along) * inverse


def stack_kernel(own_hbm, *refs):
    *parts, out_ref, sem = refs
    rows = own_hbm.shape[0]
    copy = pltpu.make_async_copy(own_hbm, out_ref.at[pl.ds(0, rows)], sem)
    copy.start()
    at = rows
    for part in parts:
        rows = part.shape[0]
        out_ref[at:at + rows, :] = part[...]
        at += rows
    copy.wait()


def stack(own_raw, parts, ties=()):
    rows, dim = own_raw.shape
    rows += sum(p.shape[0] for p in parts)
    return call(
        stack_kernel, [((rows, dim), BF16)], parts, ties=ties, first=[own_raw], scratch=[pltpu.SemaphoreType.DMA(())]
    )[0]


def round_rows(raw_ref, start, out_ref, at, rows, own=None):
    step = 64
    for n in range(0, rows, step):
        unit, inverse = unit_rows(raw_ref[start + n:start + n + step, :])
        out_ref[at + n:at + n + step, :] = unit.astype(BF16)
        if own is not None and n == 0:
            own[0][...] = unit
            own[1][...] = jnp.broadcast_to(inverse, own[1].shape)


def group_round_kernel(raw_ref, out_ref, unit_ref, inv_ref):
    round_rows(raw_ref, 0, out_ref, 0, raw_ref.shape[0], (unit_ref, inv_ref))


def early_round_kernel(raw_ref, out_ref, unit_ref, inv_ref):
    own = unit_ref.shape[0]
    round_rows(raw_ref, 0, out_ref, 0, own, (unit_ref, inv_ref))
    round_rows(raw_ref, 2 * own, out_ref, own, 2 * own)


def mine_round_kernel(early_ref, near13_ref, near4_ref, out_ref):
    own = near4_ref.shape[0]
    out_ref[:own, :] = early_ref[:own, :]
    round_rows(near13_ref, 0, out_ref, own, 4 * own)
    out_ref[5 * own:7 * own, :] = early_ref[own:, :]
    round_rows(near4_ref, 0, out_ref, 7 * own, own)


def scalar_kernel(log_ref, bias_ref, scal_ref):
    temp = jnp.exp(jnp.broadcast_to(log_ref[...], (1, 128)))
    scal_ref[...] = jnp.zeros_like(scal_ref)
    scal_ref[0:1, :] = temp
    scal_ref[1:2, :] = -LOG2E * temp
    scal_ref[2:3, :] = jnp.broadcast_to(-LOG2E * bias_ref[...], (1, 128))


def sigmoid_weights(power, scale):
    return (scale / (1.0 + jnp.exp2(power))).astype(BF16)


def powers(img, txt, scal_ref):
    slope, offset = scal_ref[1:2, 0:1], scal_ref[2:3, 0:1]
    dots = lax.dot_general(img, txt, (((1,), (1,)), ((), ())), preferred_element_type=F32)
    return dots * slope + offset


def text_grads(w_ref, img_ref, out_ref):
    step = 256
    for t in range(0, out_ref.shape[0], step):
        grad = lax.dot_general(
            w_ref[:, t:t + step], img_ref[...], (((0,), (0,)), ((), ())), preferred_element_type=F32
        )
        out_ref[t:t + step, :] = grad.astype(out_ref.dtype)


def mine_kernel(own, txt_ref, scal_ref, *refs):
    *parts, w_ref, img_ref, keep_ref = refs
    temp = scal_ref[0:1, 0:1]
    at = 0
    for part in parts:
        rows = part.shape[0]
        img = part[...] if at == 0 else unit_rows(part[...])[0].astype(BF16)
        img_ref[at:at + rows, :] = img
        power = powers(img, txt_ref[...], scal_ref)
        w_ref[at:at + rows, :] = sigmoid_weights(power, temp)
        if at == 0:
            corner = power[:own, :2 * own]
            row = lax.broadcasted_iota(jnp.int32, corner.shape, 0)
            column = lax.broadcasted_iota(jnp.int32, corner.shape, 1)
            positive = row == column
            signed = jnp.where(positive, -corner, corner)
            w_ref[:own, :2 * own] = sigmoid_weights(signed, jnp.where(positive, -temp, temp))
        at += rows
    text_grads(w_ref, img_ref, keep_ref)


def theirs_kernel(txt_ref, scal_ref, img_ref, w_ref, send_ref):
    step = 256
    for at in range(0, img_ref.shape[0], step):
        power = powers(img_ref[at:at + step, :], txt_ref[...], scal_ref)
        w_ref[at:at + step, :] = sigmoid_weights(power, scal_ref[0:1, 0:1])
    text_grads(w_ref, img_ref, send_ref)


def image_kernel(at, w1_ref, w2_ref, txt1_ref, txt2_ref, out_ref):
    rows = out_ref.shape[0]
    grad = jnp.dot(w1_ref[at:at + rows, :], txt1_ref[...], preferred_element_type=F32)
    grad += jnp.dot(w2_ref[at:at + rows, :], txt2_ref[...], preferred_element_type=F32)
    out_ref[...] = grad.astype(out_ref.dtype)


def total_kernel(keep_ref, got_ref, own_ref, part13_ref, part2_ref, part4_ref):
    at = 0
    for out in (own_ref, part13_ref, part2_ref, part4_ref):
        rows = out.shape[0]
        total = keep_ref[at:at + rows, :].astype(F32) + got_ref[at:at + rows, :].astype(F32)
        out[...] = total.astype(out.dtype)
        at += rows


def middle_kernel(part2_ref, got13_ref, got4_ref, out_ref):
    rows = got4_ref.shape[0]
    total = part2_ref[...] + got13_ref[2 * rows:, :].astype(F32)
    out_ref[:rows, :] = (total[:rows] + got4_ref[...].astype(F32)).astype(BF16)
    out_ref[rows:, :] = total[rows:].astype(BF16)


def landed_kernel(own_ref, got13_ref, got2_ref, sum_ref, send_ref):
    rows = own_ref.shape[0]
    sum_ref[...] = own_ref[...] + got13_ref[:rows, :].astype(F32) + got2_ref[:rows, :].astype(F32)
    send_ref[...] = (got13_ref[rows:2 * rows, :].astype(F32) + got2_ref[rows:, :].astype(F32)).astype(BF16)


def partial_kernel(own_ref, first_ref, second_ref, out_ref):
    out_ref[...] = own_ref[...] + first_ref[...].astype(F32) + second_ref[...].astype(F32)


def sums_kernel(sum_ref, last_ref, *outs):
    rows = outs[0].shape[0]
    for n, out in enumerate(outs):
        at = slice(n * rows, (n + 1) * rows)
        out[...] = (sum_ref[at, :] + last_ref[at, :].astype(F32)).astype(out.dtype)


def final_kernel(*refs):
    *ins, img_ref, txt_ref = refs
    for (unit_ref, inv_ref, own_ref, *parts), out_ref in ((ins[:6], img_ref), (ins[6:], txt_ref)):
        grad = own_ref[...] + sum(p[...].astype(F32) for p in parts)
        out_ref[...] = back_norm(unit_ref[...], inv_ref[:, :1], grad)


def local(images, texts, log_temp, bias):
    own, dim = images.shape

    side = [shift(images, first(k), "gA%d" % k) for k in (1, 2, 3)]
    line2 = shift(texts, line(2), "gZ2")
    cross2 = shift(texts, cross(2), "gX2")
    swapped = shift(texts, other, "gC")
    group = stack(images, side, [token(swapped)])
    send13 = stack(texts, [swapped, line2, cross2])
    far = [shift(group, second(k), "gB%d" % k) for k in (1, 3, 2)]
    near13 = shift(send13, line(1), "gZ13")
    near4 = shift(line2, line(2), "gZ4")
    first_token = token(group)
    (scalars,) = call(
        scalar_kernel, [((8, 128), F32)], [log_temp.reshape(1, 1), bias.reshape(1, 1)], [near13]
    )
    per_row = [((own, dim), F32), ((own, 128), F32)]
    group, img_unit, inv_img = call(group_round_kernel, [(group.shape, BF16)] + per_row, [group], [scalars])
    early, txt_unit, inv_txt = call(early_round_kernel, [((3 * own, dim), BF16)] + per_row, [send13], [scalars])
    (mine,) = call(
        mine_round_kernel, [((8 * own, dim), BF16)], [early, near13, near4], [group, first_token, *far]
    )
    theirs = shift(mine, other, "gS")

    half = mine.shape[0]
    rows = group.shape[0] * (1 + len(far))
    flops = 2 * rows * half * dim
    w_mine, img_all, keep = call(
        lambda *refs: mine_kernel(own, *refs), [((rows, half), BF16), ((rows, dim), BF16), ((half, dim), BF16)],
        [mine, scalars, group, *far], flops=2 * flops, limit=24,
    )
    w_theirs, send = call(
        theirs_kernel, [((rows, half), BF16), ((half, dim), BF16)],
        [theirs, scalars, img_all], ties=[keep], flops=2 * flops, limit=24,
    )
    each = group.shape[0]

    def image_grads(index, dtype, ties):
        return call(
            lambda *refs: image_kernel(index * each, *refs), [((each, dim), dtype)],
            [w_mine, w_theirs, mine, theirs], ties=ties, flops=flops // 2, limit=24,
        )[0]

    grad3 = image_grads(2, BF16, [send])
    back3 = shift(grad3, second(-3), "rB3")
    grad1 = image_grads(1, BF16, [grad3])
    back1 = shift(grad1, second(-1), "rB1")

    total_own, part13, part2, part4 = call(
        total_kernel,
        [((own, dim), F32), ((4 * own, dim), BF16), ((2 * own, dim), F32), ((own, dim), BF16)],
        [keep, shift(send, other, "rC")], ties=[grad1],
    )
    grad2 = image_grads(3, BF16, [part13])
    back2 = shift(grad2, second(-2), "rB2")
    grad0 = image_grads(0, F32, [grad2])
    (partial,) = call(partial_kernel, [((each, dim), F32)], [grad0, back3, back1])
    got13 = shift(part13, line(-1), "rZ13")
    got4 = shift(part4, line(-2), "rZ4")
    (middle,) = call(middle_kernel, [((2 * own, dim), BF16)], [part2, got13, got4], [token(got13, partial)])
    got2 = shift(middle, line(-2), "rZ2")
    txt_sum, txt_send = call(landed_kernel, [((own, dim), F32), ((own, dim), BF16)], [total_own, got13, got2])
    txt_last = shift(txt_send, other, "rS")

    img_sum, *parts = call(
        sums_kernel, [((own, dim), F32)] + [((own, dim), BF16)] * 3, [partial, back2], ties=[token(middle)]
    )
    last = [shift(p, first(-k), "rA%d" % k) for k, p in zip((1, 2, 3), parts)]

    return call(
        final_kernel, [((own, dim), F32)] * 2,
        [img_unit, inv_img, img_sum, *last, txt_unit, inv_txt, txt_sum, txt_last],
    )


def solution(mesh):
    in_specs = (P(("row", "col"), None), P(("row", "col"), None), P(), P())
    out_specs = (P(("row", "col"), None), P(("row", "col"), None))
    return jax.shard_map(local, mesh=mesh, in_specs=in_specs, out_specs=out_specs, check_vma=False)
```

```python
import jax
import jax.numpy as jnp
from jax import lax
from jax.experimental import pallas as pl
from jax.experimental.pallas import tpu as pltpu
from jax.sharding import PartitionSpec as P

AXES = ("row", "col")
F32 = jnp.float32
BF16 = jnp.bfloat16
LOG2E = 1.4426950408889634
SIZE_X, SIZE_Y, SIZE_Z, CORES = 4, 4, 8, 2


def device(x, y, z, c):
    return ((z // 4) * 16 + x * 4 + y) * 8 + (z % 4) * 2 + c


def shift(values, move, name="move"):
    pairs = []
    for x in range(SIZE_X):
        for y in range(SIZE_Y):
            for z in range(SIZE_Z):
                for c in range(CORES):
                    nx, ny, nz, nc = move(x, y, z, c)
                    pairs.append((device(x, y, z, c), device(nx % SIZE_X, ny % SIZE_Y, nz % SIZE_Z, nc)))
    with jax.named_scope(name):
        return lax.ppermute(values, AXES, pairs)


def first(k):
    return lambda x, y, z, c: (x + k, y, z, c) if c == 0 else (x, y + k, z, c)


def second(k):
    return lambda x, y, z, c: (x, y + k, z, c) if c == 0 else (x + k, y, z, c)


def line(k):
    return lambda x, y, z, c: (x, y, z + k, c) if c == 0 else (x, y, z - k, c)


def cross(k):
    return lambda x, y, z, c: (x, y, z + k, 0) if c == 1 else (x, y, z - k, 1)


def other(x, y, z, c):
    return (x, y, z, 1 - c)


def call(kernel, outs, arrays, ties=(), first=(), scratch=(), flops=0, limit=8):
    vmem = pl.BlockSpec(memory_space=pltpu.VMEM)
    anywhere = pl.BlockSpec(memory_space=pl.ANY)
    n_in = len(first) + len(arrays)
    return pl.pallas_call(
        lambda *refs: kernel(*refs[:n_in], *refs[n_in + len(ties):]),
        out_shape=tuple(jax.ShapeDtypeStruct(shape, dtype) for shape, dtype in outs),
        in_specs=[anywhere] * len(first) + [vmem] * len(arrays) + [anywhere] * len(ties),
        out_specs=tuple([vmem] * len(outs)),
        scratch_shapes=list(scratch),
        compiler_params=pltpu.CompilerParams(vmem_limit_bytes=limit * 1024 * 1024),
        cost_estimate=pl.CostEstimate(flops=flops, bytes_accessed=1024, transcendentals=0),
    )(*first, *arrays, *ties)


def token_kernel(token_ref):
    token_ref[...] = jnp.zeros_like(token_ref)


def token(*values):
    return call(token_kernel, [((8, 128), F32)], [], ties=values, flops=40_000_000_000, limit=1)[0]


def unit_rows(raw):
    values = raw.astype(F32)
    inverse = lax.rsqrt(jnp.sum(values * values, axis=1, keepdims=True) + 1e-06)
    return values * inverse, inverse


def back_norm(unit, inverse, grad_unit):
    along = jnp.sum(unit * grad_unit, axis=1, keepdims=True)
    return (grad_unit - unit * along) * inverse


def stack_kernel(own_hbm, *refs):
    *parts, out_ref, sem = refs
    rows = own_hbm.shape[0]
    copy = pltpu.make_async_copy(own_hbm, out_ref.at[pl.ds(0, rows)], sem)
    copy.start()
    at = rows
    for part in parts:
        rows = part.shape[0]
        out_ref[at:at + rows, :] = part[...]
        at += rows
    copy.wait()


def stack(own_raw, parts, ties=()):
    rows, dim = own_raw.shape
    rows += sum(p.shape[0] for p in parts)
    return call(
        stack_kernel, [((rows, dim), BF16)], parts, ties=ties, first=[own_raw], scratch=[pltpu.SemaphoreType.DMA(())]
    )[0]


def round_rows(raw_ref, start, out_ref, at, rows, own=None):
    step = 64
    for n in range(0, rows, step):
        unit, inverse = unit_rows(raw_ref[start + n:start + n + step, :])
        out_ref[at + n:at + n + step, :] = unit.astype(BF16)
        if own is not None and n == 0:
            own[0][...] = unit
            own[1][...] = jnp.broadcast_to(inverse, own[1].shape)


def group_round_kernel(raw_ref, out_ref, unit_ref, inv_ref):
    round_rows(raw_ref, 0, out_ref, 0, raw_ref.shape[0], (unit_ref, inv_ref))


def early_round_kernel(raw_ref, out_ref, unit_ref, inv_ref):
    own = unit_ref.shape[0]
    round_rows(raw_ref, 0, out_ref, 0, own, (unit_ref, inv_ref))
    round_rows(raw_ref, 2 * own, out_ref, own, 2 * own)


def mine_round_kernel(early_ref, near13_ref, near4_ref, out_ref):
    own = near4_ref.shape[0]
    out_ref[:own, :] = early_ref[:own, :]
    round_rows(near13_ref, 0, out_ref, own, 4 * own)
    out_ref[5 * own:7 * own, :] = early_ref[own:, :]
    round_rows(near4_ref, 0, out_ref, 7 * own, own)


def scalar_kernel(log_ref, bias_ref, scal_ref):
    temp = jnp.exp(jnp.broadcast_to(log_ref[...], (1, 128)))
    scal_ref[...] = jnp.zeros_like(scal_ref)
    scal_ref[0:1, :] = temp
    scal_ref[1:2, :] = -LOG2E * temp
    scal_ref[2:3, :] = jnp.broadcast_to(-LOG2E * bias_ref[...], (1, 128))


def sigmoid_weights(power, scale):
    return (scale / (1.0 + jnp.exp2(power))).astype(BF16)


def powers(img, txt, scal_ref):
    slope, offset = scal_ref[1:2, 0:1], scal_ref[2:3, 0:1]
    dots = lax.dot_general(img, txt, (((1,), (1,)), ((), ())), preferred_element_type=F32)
    return dots * slope + offset


def text_grads(w_ref, img_ref, out_ref):
    step = 256
    for t in range(0, out_ref.shape[0], step):
        grad = lax.dot_general(
            w_ref[:, t:t + step], img_ref[...], (((0,), (0,)), ((), ())), preferred_element_type=F32
        )
        out_ref[t:t + step, :] = grad.astype(out_ref.dtype)


def mine_kernel(own, txt_ref, scal_ref, *refs):
    *parts, w_ref, img_ref, keep_ref = refs
    temp = scal_ref[0:1, 0:1]
    at = 0
    for part in parts:
        rows = part.shape[0]
        img = part[...] if at == 0 else unit_rows(part[...])[0].astype(BF16)
        img_ref[at:at + rows, :] = img
        power = powers(img, txt_ref[...], scal_ref)
        w_ref[at:at + rows, :] = sigmoid_weights(power, temp)
        if at == 0:
            corner = power[:own, :2 * own]
            row = lax.broadcasted_iota(jnp.int32, corner.shape, 0)
            column = lax.broadcasted_iota(jnp.int32, corner.shape, 1)
            positive = row == column
            signed = jnp.where(positive, -corner, corner)
            w_ref[:own, :2 * own] = sigmoid_weights(signed, jnp.where(positive, -temp, temp))
        at += rows
    text_grads(w_ref, img_ref, keep_ref)


def theirs_kernel(txt_ref, scal_ref, img_ref, w_ref, send_ref):
    step = 256
    for at in range(0, img_ref.shape[0], step):
        power = powers(img_ref[at:at + step, :], txt_ref[...], scal_ref)
        w_ref[at:at + step, :] = sigmoid_weights(power, scal_ref[0:1, 0:1])
    text_grads(w_ref, img_ref, send_ref)


def image_kernel(at, w1_ref, w2_ref, txt1_ref, txt2_ref, out_ref):
    rows = out_ref.shape[0]
    grad = jnp.dot(w1_ref[at:at + rows, :], txt1_ref[...], preferred_element_type=F32)
    grad += jnp.dot(w2_ref[at:at + rows, :], txt2_ref[...], preferred_element_type=F32)
    out_ref[...] = grad.astype(out_ref.dtype)


def total_kernel(keep_ref, got_ref, own_ref, part13_ref, part2_ref, part4_ref):
    at = 0
    for out in (own_ref, part13_ref, part2_ref, part4_ref):
        rows = out.shape[0]
        total = keep_ref[at:at + rows, :].astype(F32) + got_ref[at:at + rows, :].astype(F32)
        out[...] = total.astype(out.dtype)
        at += rows


def middle_kernel(part2_ref, got13_ref, got4_ref, out_ref):
    rows = got4_ref.shape[0]
    total = part2_ref[...] + got13_ref[2 * rows:, :].astype(F32)
    out_ref[:rows, :] = (total[:rows] + got4_ref[...].astype(F32)).astype(BF16)
    out_ref[rows:, :] = total[rows:].astype(BF16)


def landed_kernel(own_ref, got13_ref, got2_ref, sum_ref, send_ref):
    rows = own_ref.shape[0]
    sum_ref[...] = own_ref[...] + got13_ref[:rows, :].astype(F32) + got2_ref[:rows, :].astype(F32)
    send_ref[...] = (got13_ref[rows:2 * rows, :].astype(F32) + got2_ref[rows:, :].astype(F32)).astype(BF16)


def partial_kernel(own_ref, first_ref, second_ref, out_ref):
    out_ref[...] = own_ref[...] + first_ref[...].astype(F32) + second_ref[...].astype(F32)


def sums_kernel(sum_ref, last_ref, *outs):
    rows = outs[0].shape[0]
    for n, out in enumerate(outs):
        at = slice(n * rows, (n + 1) * rows)
        out[...] = (sum_ref[at, :] + last_ref[at, :].astype(F32)).astype(out.dtype)


def final_kernel(*refs):
    *ins, img_ref, txt_ref = refs
    for (unit_ref, inv_ref, own_ref, *parts), out_ref in ((ins[:6], img_ref), (ins[6:], txt_ref)):
        grad = own_ref[...] + sum(p[...].astype(F32) for p in parts)
        out_ref[...] = back_norm(unit_ref[...], inv_ref[:, :1], grad)


def local(images, texts, log_temp, bias):
    own, dim = images.shape

    side = [shift(images, first(k), "gA%d" % k) for k in (1, 2, 3)]
    line2 = shift(texts, line(2), "gZ2")
    cross2 = shift(texts, cross(2), "gX2")
    swapped = shift(texts, other, "gC")
    group = stack(images, side, [token(swapped)])
    send13 = stack(texts, [swapped, line2, cross2])
    far = [shift(group, second(k), "gB%d" % k) for k in (1, 3, 2)]
    near13 = shift(send13, line(1), "gZ13")
    near4 = shift(line2, line(2), "gZ4")
    first_token = token(group)
    (scalars,) = call(
        scalar_kernel, [((8, 128), F32)], [log_temp.reshape(1, 1), bias.reshape(1, 1)], [near13]
    )
    per_row = [((own, dim), F32), ((own, 128), F32)]
    group, img_unit, inv_img = call(group_round_kernel, [(group.shape, BF16)] + per_row, [group], [scalars])
    early, txt_unit, inv_txt = call(early_round_kernel, [((3 * own, dim), BF16)] + per_row, [send13], [scalars])
    (mine,) = call(
        mine_round_kernel, [((8 * own, dim), BF16)], [early, near13, near4], [group, first_token, *far]
    )
    theirs = shift(mine, other, "gS")

    half = mine.shape[0]
    rows = group.shape[0] * (1 + len(far))
    flops = 2 * rows * half * dim
    w_mine, img_all, keep = call(
        lambda *refs: mine_kernel(own, *refs), [((rows, half), BF16), ((rows, dim), BF16), ((half, dim), BF16)],
        [mine, scalars, group, *far], flops=2 * flops, limit=24,
    )
    w_theirs, send = call(
        theirs_kernel, [((rows, half), BF16), ((half, dim), BF16)],
        [theirs, scalars, img_all], ties=[keep], flops=2 * flops, limit=24,
    )
    each = group.shape[0]

    def image_grads(index, dtype, ties):
        return call(
            lambda *refs: image_kernel(index * each, *refs), [((each, dim), dtype)],
            [w_mine, w_theirs, mine, theirs], ties=ties, flops=flops // 2, limit=24,
        )[0]

    grad2 = image_grads(3, BF16, [send])
    back2 = shift(grad2, second(-2), "rB2")
    grad3 = image_grads(2, BF16, [grad2])
    back3 = shift(grad3, second(-3), "rB3")

    total_own, part13, part2, part4 = call(
        total_kernel,
        [((own, dim), F32), ((4 * own, dim), BF16), ((2 * own, dim), F32), ((own, dim), BF16)],
        [keep, shift(send, other, "rC")], ties=[grad3],
    )
    grad1 = image_grads(1, BF16, [part13])
    back1 = shift(grad1, second(-1), "rB1")
    grad0 = image_grads(0, F32, [grad1])
    (partial,) = call(partial_kernel, [((each, dim), F32)], [grad0, back2, back3])
    got13 = shift(part13, line(-1), "rZ13")
    got4 = shift(part4, line(-2), "rZ4")
    (middle,) = call(middle_kernel, [((2 * own, dim), BF16)], [part2, got13, got4], [partial])
    got2 = shift(middle, line(-2), "rZ2")
    txt_sum, txt_send = call(landed_kernel, [((own, dim), F32), ((own, dim), BF16)], [total_own, got13, got2])
    txt_last = shift(txt_send, other, "rS")

    img_sum, *parts = call(
        sums_kernel, [((own, dim), F32)] + [((own, dim), BF16)] * 3, [partial, back1], ties=[token(middle)]
    )
    last = [shift(p, first(-k), "rA%d" % k) for k, p in zip((1, 2, 3), parts)]

    return call(
        final_kernel, [((own, dim), F32)] * 2,
        [img_unit, inv_img, img_sum, *last, txt_unit, inv_txt, txt_sum, txt_last],
    )


def solution(mesh):
    in_specs = (P(("row", "col"), None), P(("row", "col"), None), P(), P())
    out_specs = (P(("row", "col"), None), P(("row", "col"), None))
    return jax.shard_map(local, mesh=mesh, in_specs=in_specs, out_specs=out_specs, check_vma=False)
```

```python
import jax
import jax.numpy as jnp
from jax import lax
from jax.experimental import pallas as pl
from jax.experimental.pallas import tpu as pltpu
from jax.sharding import PartitionSpec as P

AXES = ("row", "col")
F32 = jnp.float32
BF16 = jnp.bfloat16
LOG2E = 1.4426950408889634
SIZE_X, SIZE_Y, SIZE_Z, CORES = 4, 4, 8, 2


def device(x, y, z, c):
    return ((z // 4) * 16 + x * 4 + y) * 8 + (z % 4) * 2 + c


def shift(values, move, name="move"):
    pairs = []
    for x in range(SIZE_X):
        for y in range(SIZE_Y):
            for z in range(SIZE_Z):
                for c in range(CORES):
                    nx, ny, nz, nc = move(x, y, z, c)
                    pairs.append((device(x, y, z, c), device(nx % SIZE_X, ny % SIZE_Y, nz % SIZE_Z, nc)))
    with jax.named_scope(name):
        return lax.ppermute(values, AXES, pairs)


def first(k):
    return lambda x, y, z, c: (x + k, y, z, c) if c == 0 else (x, y + k, z, c)


def second(k):
    return lambda x, y, z, c: (x, y + k, z, c) if c == 0 else (x + k, y, z, c)


def line(k):
    return lambda x, y, z, c: (x, y, z + k, c) if c == 0 else (x, y, z - k, c)


def cross(k):
    return lambda x, y, z, c: (x, y, z + k, 0) if c == 1 else (x, y, z - k, 1)


def other(x, y, z, c):
    return (x, y, z, 1 - c)


def call(kernel, outs, arrays, ties=(), first=(), scratch=(), flops=0, limit=8):
    vmem = pl.BlockSpec(memory_space=pltpu.VMEM)
    anywhere = pl.BlockSpec(memory_space=pl.ANY)
    n_in = len(first) + len(arrays)
    return pl.pallas_call(
        lambda *refs: kernel(*refs[:n_in], *refs[n_in + len(ties):]),
        out_shape=tuple(jax.ShapeDtypeStruct(shape, dtype) for shape, dtype in outs),
        in_specs=[anywhere] * len(first) + [vmem] * len(arrays) + [anywhere] * len(ties),
        out_specs=tuple([vmem] * len(outs)),
        scratch_shapes=list(scratch),
        compiler_params=pltpu.CompilerParams(vmem_limit_bytes=limit * 1024 * 1024),
        cost_estimate=pl.CostEstimate(flops=flops, bytes_accessed=1024, transcendentals=0),
    )(*first, *arrays, *ties)


def token_kernel(token_ref):
    token_ref[...] = jnp.zeros_like(token_ref)


def token(*values):
    return call(token_kernel, [((8, 128), F32)], [], ties=values, flops=40_000_000_000, limit=1)[0]


def unit_rows(raw):
    values = raw.astype(F32)
    inverse = lax.rsqrt(jnp.sum(values * values, axis=1, keepdims=True) + 1e-06)
    return values * inverse, inverse


def back_norm(unit, inverse, grad_unit):
    along = jnp.sum(unit * grad_unit, axis=1, keepdims=True)
    return (grad_unit - unit * along) * inverse


def stack_kernel(own_hbm, *refs):
    *parts, out_ref, sem = refs
    rows = own_hbm.shape[0]
    copy = pltpu.make_async_copy(own_hbm, out_ref.at[pl.ds(0, rows)], sem)
    copy.start()
    at = rows
    for part in parts:
        rows = part.shape[0]
        out_ref[at:at + rows, :] = part[...]
        at += rows
    copy.wait()


def stack(own_raw, parts, ties=()):
    rows, dim = own_raw.shape
    rows += sum(p.shape[0] for p in parts)
    return call(
        stack_kernel, [((rows, dim), BF16)], parts, ties=ties, first=[own_raw], scratch=[pltpu.SemaphoreType.DMA(())]
    )[0]


def round_rows(raw_ref, start, out_ref, at, rows, own=None):
    step = 64
    for n in range(0, rows, step):
        unit, inverse = unit_rows(raw_ref[start + n:start + n + step, :])
        out_ref[at + n:at + n + step, :] = unit.astype(BF16)
        if own is not None and n == 0:
            own[0][...] = unit
            own[1][...] = jnp.broadcast_to(inverse, own[1].shape)


def group_round_kernel(raw_ref, out_ref, unit_ref, inv_ref):
    round_rows(raw_ref, 0, out_ref, 0, raw_ref.shape[0], (unit_ref, inv_ref))


def early_round_kernel(raw_ref, out_ref, unit_ref, inv_ref):
    own = unit_ref.shape[0]
    round_rows(raw_ref, 0, out_ref, 0, own, (unit_ref, inv_ref))
    round_rows(raw_ref, 2 * own, out_ref, own, 2 * own)


def mine_round_kernel(early_ref, near13_ref, near4_ref, out_ref):
    own = near4_ref.shape[0]
    out_ref[:own, :] = early_ref[:own, :]
    round_rows(near13_ref, 0, out_ref, own, 4 * own)
    out_ref[5 * own:7 * own, :] = early_ref[own:, :]
    round_rows(near4_ref, 0, out_ref, 7 * own, own)


def scalar_kernel(log_ref, bias_ref, scal_ref):
    temp = jnp.exp(jnp.broadcast_to(log_ref[...], (1, 128)))
    scal_ref[...] = jnp.zeros_like(scal_ref)
    scal_ref[0:1, :] = temp
    scal_ref[1:2, :] = -LOG2E * temp
    scal_ref[2:3, :] = jnp.broadcast_to(-LOG2E * bias_ref[...], (1, 128))


def sigmoid_weights(power, scale):
    return (scale / (1.0 + jnp.exp2(power))).astype(BF16)


def powers(img, txt, scal_ref):
    slope, offset = scal_ref[1:2, 0:1], scal_ref[2:3, 0:1]
    dots = lax.dot_general(img, txt, (((1,), (1,)), ((), ())), preferred_element_type=F32)
    return dots * slope + offset


def text_grads(w_ref, img_ref, out_ref):
    step = 256
    for t in range(0, out_ref.shape[0], step):
        grad = lax.dot_general(
            w_ref[:, t:t + step], img_ref[...], (((0,), (0,)), ((), ())), preferred_element_type=F32
        )
        out_ref[t:t + step, :] = grad.astype(out_ref.dtype)


def mine_kernel(own, txt_ref, scal_ref, *refs):
    *parts, w_ref, img_ref, keep_ref = refs
    temp = scal_ref[0:1, 0:1]
    at = 0
    for part in parts:
        rows = part.shape[0]
        img = part[...] if at == 0 else unit_rows(part[...])[0].astype(BF16)
        img_ref[at:at + rows, :] = img
        power = powers(img, txt_ref[...], scal_ref)
        w_ref[at:at + rows, :] = sigmoid_weights(power, temp)
        if at == 0:
            corner = power[:own, :2 * own]
            row = lax.broadcasted_iota(jnp.int32, corner.shape, 0)
            column = lax.broadcasted_iota(jnp.int32, corner.shape, 1)
            positive = row == column
            signed = jnp.where(positive, -corner, corner)
            w_ref[:own, :2 * own] = sigmoid_weights(signed, jnp.where(positive, -temp, temp))
        at += rows
    text_grads(w_ref, img_ref, keep_ref)


def theirs_kernel(txt_ref, scal_ref, img_ref, w_ref, send_ref):
    step = 256
    for at in range(0, img_ref.shape[0], step):
        power = powers(img_ref[at:at + step, :], txt_ref[...], scal_ref)
        w_ref[at:at + step, :] = sigmoid_weights(power, scal_ref[0:1, 0:1])
    text_grads(w_ref, img_ref, send_ref)


def image_kernel(at, w1_ref, w2_ref, txt1_ref, txt2_ref, out_ref):
    rows = out_ref.shape[0]
    grad = jnp.dot(w1_ref[at:at + rows, :], txt1_ref[...], preferred_element_type=F32)
    grad += jnp.dot(w2_ref[at:at + rows, :], txt2_ref[...], preferred_element_type=F32)
    out_ref[...] = grad.astype(out_ref.dtype)


def total_kernel(keep_ref, got_ref, own_ref, part13_ref, part2_ref, part4_ref):
    at = 0
    for out in (own_ref, part13_ref, part2_ref, part4_ref):
        rows = out.shape[0]
        total = keep_ref[at:at + rows, :].astype(F32) + got_ref[at:at + rows, :].astype(F32)
        out[...] = total.astype(out.dtype)
        at += rows


def middle_kernel(part2_ref, got13_ref, got4_ref, out_ref):
    rows = got4_ref.shape[0]
    total = part2_ref[...] + got13_ref[2 * rows:, :].astype(F32)
    out_ref[:rows, :] = (total[:rows] + got4_ref[...].astype(F32)).astype(BF16)
    out_ref[rows:, :] = total[rows:].astype(BF16)


def landed_kernel(own_ref, got13_ref, got2_ref, sum_ref, send_ref):
    rows = own_ref.shape[0]
    sum_ref[...] = own_ref[...] + got13_ref[:rows, :].astype(F32) + got2_ref[:rows, :].astype(F32)
    send_ref[...] = (got13_ref[rows:2 * rows, :].astype(F32) + got2_ref[rows:, :].astype(F32)).astype(BF16)


def partial_kernel(own_ref, first_ref, second_ref, out_ref):
    out_ref[...] = own_ref[...] + first_ref[...].astype(F32) + second_ref[...].astype(F32)


def sums_kernel(sum_ref, last_ref, *outs):
    rows = outs[0].shape[0]
    for n, out in enumerate(outs):
        at = slice(n * rows, (n + 1) * rows)
        out[...] = (sum_ref[at, :] + last_ref[at, :].astype(F32)).astype(out.dtype)


def final_kernel(*refs):
    *ins, img_ref, txt_ref = refs
    for (unit_ref, inv_ref, own_ref, *parts), out_ref in ((ins[:6], img_ref), (ins[6:], txt_ref)):
        grad = own_ref[...] + sum(p[...].astype(F32) for p in parts)
        out_ref[...] = back_norm(unit_ref[...], inv_ref[:, :1], grad)


def local(images, texts, log_temp, bias):
    own, dim = images.shape

    side = [shift(images, first(k), "gA%d" % k) for k in (1, 2, 3)]
    line2 = shift(texts, line(2), "gZ2")
    cross2 = shift(texts, cross(2), "gX2")
    swapped = shift(texts, other, "gC")
    group = stack(images, side, [token(swapped)])
    send13 = stack(texts, [swapped, line2, cross2])
    far = [shift(group, second(k), "gB%d" % k) for k in (1, 3, 2)]
    near13 = shift(send13, line(1), "gZ13")
    near4 = shift(line2, line(2), "gZ4")
    first_token = token(group)
    (scalars,) = call(
        scalar_kernel, [((8, 128), F32)], [log_temp.reshape(1, 1), bias.reshape(1, 1)], [near13]
    )
    per_row = [((own, dim), F32), ((own, 128), F32)]
    group, img_unit, inv_img = call(group_round_kernel, [(group.shape, BF16)] + per_row, [group], [scalars])
    early, txt_unit, inv_txt = call(early_round_kernel, [((3 * own, dim), BF16)] + per_row, [send13], [scalars])
    (mine,) = call(
        mine_round_kernel, [((8 * own, dim), BF16)], [early, near13, near4], [group, first_token, *far]
    )
    theirs = shift(mine, other, "gS")

    half = mine.shape[0]
    rows = group.shape[0] * (1 + len(far))
    flops = 2 * rows * half * dim
    w_mine, img_all, keep = call(
        lambda *refs: mine_kernel(own, *refs), [((rows, half), BF16), ((rows, dim), BF16), ((half, dim), BF16)],
        [mine, scalars, group, *far], flops=2 * flops, limit=24,
    )
    w_theirs, send = call(
        theirs_kernel, [((rows, half), BF16), ((half, dim), BF16)],
        [theirs, scalars, img_all], ties=[keep], flops=2 * flops, limit=24,
    )
    each = group.shape[0]

    def image_grads(index, dtype, ties):
        return call(
            lambda *refs: image_kernel(index * each, *refs), [((each, dim), dtype)],
            [w_mine, w_theirs, mine, theirs], ties=ties, flops=flops // 2, limit=24,
        )[0]

    grad2 = image_grads(3, BF16, [send])
    back2 = shift(grad2, second(-2), "rB2")
    grad3 = image_grads(2, BF16, [grad2])
    back3 = shift(grad3, second(-3), "rB3")

    total_own, part13, part2, part4 = call(
        total_kernel,
        [((own, dim), F32), ((4 * own, dim), BF16), ((2 * own, dim), F32), ((own, dim), BF16)],
        [keep, shift(send, other, "rC")], ties=[grad3],
    )
    grad1 = image_grads(1, BF16, [part13])
    back1 = shift(grad1, second(-1), "rB1")
    grad0 = image_grads(0, F32, [grad1])
    (partial,) = call(partial_kernel, [((each, dim), F32)], [grad0, back2, back3])
    got13 = shift(part13, line(-1), "rZ13")
    got4 = shift(part4, line(-2), "rZ4")
    (middle,) = call(middle_kernel, [((2 * own, dim), BF16)], [part2, got13, got4], [token(got13, partial)])
    got2 = shift(middle, line(-2), "rZ2")
    txt_sum, txt_send = call(landed_kernel, [((own, dim), F32), ((own, dim), BF16)], [total_own, got13, got2])
    txt_last = shift(txt_send, other, "rS")

    img_sum, *parts = call(
        sums_kernel, [((own, dim), F32)] + [((own, dim), BF16)] * 3, [partial, back1], ties=[token(middle)]
    )
    last = [shift(p, first(-k), "rA%d" % k) for k, p in zip((1, 2, 3), parts)]

    return call(
        final_kernel, [((own, dim), F32)] * 2,
        [img_unit, inv_img, img_sum, *last, txt_unit, inv_txt, txt_sum, txt_last],
    )


def solution(mesh):
    in_specs = (P(("row", "col"), None), P(("row", "col"), None), P(), P())
    out_specs = (P(("row", "col"), None), P(("row", "col"), None))
    return jax.shard_map(local, mesh=mesh, in_specs=in_specs, out_specs=out_specs, check_vma=False)
```
